128 devices in a mesh: fx: 8 (over y, core), fy: 16 (over z, x).
Axes of the slice: x: 4, y: 4, z: 4, core: 2. Of those that a mesh axis runs over, the one named last changes fastest.
Arguments:
- tracers: float32 [64, 16, 32768], P(None, None, ('fx', 'fy')), may hold values from -6 to 6
- node_mass: float32 [16, 32768], P(None, ('fx', 'fy')), may hold values from 0.05 to 1
- point_order: int32 [2, 128, 4096], P(None, ('fx', 'fy')), may hold values from 0 to 4095, each once within a row
- offsets: int32 [2, 128, 10], P(None, ('fx', 'fy')), may hold values from 0 to 4096, as said below
- source: int32 [2, 524288], P(None, ('fx', 'fy')), may hold values from 0 to 255
- coords: int32 [2, 2, 524288], P(None, None, ('fx', 'fy')), may hold values from 0 to 1024
Outputs:
- transported: float32 [64, 16, 32768], P(None, None, ('fx', 'fy'))
The draws below stay inside these ranges and needn't reach their ends.
Inputs may be any that keep to these rules, and one draw needn't show every extreme that they name: offsets[s, t, 0] = 0 and offsets[s, t, 9] = 4096, never falling; every run k other than 4 holds at least 32 and at most 128 positions, and on every tile in every substep some run holds exactly 128.
All inputs are finite; a program needn't handle non-finite values.
Results may differ from the reference program's by a relative error of at most 0.0003.
Values sent between devices are 32-bit elements; how exact they have to be, the bound alone decides.
No kernel may reach another device: no remote copies, remote signals or barrier semaphores. Data moves between devices by JAX's collectives and lax.ppermute only.
A program may use at most 128 MiB of HBM per device.

```python
import math
import jax
import jax.numpy as jnp
from jax import lax

TRACERS = 4
LEV = 16
TX = 16
TY = 16
CAP = 128
QGRID = 1024
SUBSTEPS = 2
E_DEV = 256
POINTS = 4096
ELEMS = 32768
N_FX = 8
N_FY = 16


def draw_offsets(key, part):
    key = jax.random.fold_in(key, 11)
    key_runs, key_full = jax.random.split(key)
    devices = N_FX * N_FY
    run_lengths = jax.random.randint(key_runs, (SUBSTEPS, devices, 8), CAP // 4, CAP + 1)
    fullest = jax.random.randint(key_full, (SUBSTEPS, devices, 1), 0, 8)
    run_lengths = jnp.where(jnp.arange(8)[None, None, :] == fullest, CAP, run_lengths)
    own_points = POINTS - jnp.sum(run_lengths, axis=2, keepdims=True)
    counts = jnp.concatenate([run_lengths[:, :, :4], own_points, run_lengths[:, :, 4:]], axis=2)
    starts = jnp.concatenate([jnp.zeros((SUBSTEPS, devices, 1), jnp.int32), jnp.cumsum(counts, axis=2)], axis=2)
    return starts.astype(jnp.int32)


def set_ends(values, rng, low, largest):
    spot = [jax.random.randint(jax.random.fold_in(rng, axis), (), 0, length) for axis, length in enumerate(values.shape)]
    longest = values.shape.index(max(values.shape))
    next_to = spot[:longest] + [(spot[longest] + 1) % values.shape[longest]] + spot[longest + 1:]
    return values.at[tuple(spot)].set(low).at[tuple(next_to)].set(largest)


def steps_of(rng, extent, cuts, least, largest):
    level = 1.0
    for dim, shards_of in cuts:
        steps = jax.random.uniform(jax.random.fold_in(jax.random.fold_in(rng, 6), dim), (shards_of,), jnp.float32, least / len(cuts), largest / len(cuts))
        level = level * jnp.repeat(jnp.exp(steps), extent[dim] // shards_of).reshape((-1,) + (1,) * (len(extent) - 1 - dim))
    return level


def bell_draw(stream_key, dims, deviation, limit, cuts=(), held_as=jnp.bfloat16):
    factor_of = steps_of(stream_key, dims, cuts, -0.22, 0.18) if cuts else 1.0
    array = jax.random.normal(stream_key, dims, jnp.float32) * deviation * factor_of
    return jnp.minimum(jnp.maximum(array, -limit), limit).astype(held_as)


def setup_inputs(seed: int = 0) -> dict:
    key_of = jax.random.split(jax.random.key(seed), 7)
    tracers = bell_draw(key_of[0], (TRACERS * LEV, 16, ELEMS), 1.0, 6.0, ((2, 128),), jnp.float32)
    node_mass = jnp.clip(jnp.exp(math.log(1.0) - 2.9957323 * jax.random.uniform(key_of[1], (16, ELEMS), jnp.float32) ** steps_of(key_of[1], (16, ELEMS), ((1, 128),), -0.2, 0.2)), 0.05, 1.0)
    point_order = jax.vmap(lambda own: jax.random.permutation(own, POINTS))(jax.random.split(key_of[2], SUBSTEPS * (N_FX * N_FY))).reshape((SUBSTEPS, N_FX * N_FY, POINTS)).astype(jnp.int32)
    offsets = draw_offsets(jax.random.fold_in(key_of[6], 71), 0)
    source = set_ends(jax.random.randint(key_of[4], (SUBSTEPS, POINTS * N_FX * N_FY), 0, E_DEV), jax.random.fold_in(key_of[4], 1), 0, E_DEV - 1).astype(jnp.int32)
    coords = set_ends(jax.random.randint(key_of[5], (SUBSTEPS, 2, POINTS * N_FX * N_FY), 0, QGRID + 1), jax.random.fold_in(key_of[5], 1), 0, QGRID).astype(jnp.int32)
    return dict(tracers=tracers, node_mass=node_mass, point_order=point_order, offsets=offsets, source=source, coords=coords)


GLL_NODES = (-1.0, -0.4472135954999579, 0.4472135954999579, 1.0)


def lagrange(coordinate):
    basis_rows = []
    for a in range(4):
        factor = jnp.ones_like(coordinate)
        for b in range(4):
            if b != a:
                factor = factor * ((coordinate - GLL_NODES[b]) / (GLL_NODES[a] - GLL_NODES[b]))
        basis_rows.append(factor)
    return jnp.stack(basis_rows)


def interpolate(tracer_field, request):
    total_points = request.shape[1]
    width_block = math.gcd(total_points, 512)
    portions = request.reshape(3, total_points // width_block, width_block).transpose(1, 0, 2)

    def per_block(portion):
        along_first = lagrange(portion[1].astype(jnp.float32) * (2.0 / QGRID) - 1.0)
        along_second = lagrange(portion[2].astype(jnp.float32) * (2.0 / QGRID) - 1.0)
        weights = (along_first[:, None, :] * along_second[None, :, :]).reshape(16, width_block)
        picked = jnp.take(tracer_field, portion[0], axis=2)
        return jnp.sum(picked * weights[None], axis=1)

    result = lax.map(per_block, portions)
    return result.transpose(1, 0, 2).reshape(tracer_field.shape[0], total_points)


def edge_roll(lattice):
    lower_edge = lattice[:, 0] + jnp.roll(lattice[:, 3], 1, axis=2)
    upper_edge = lattice[:, 3] + jnp.roll(lattice[:, 0], -1, axis=2)
    lattice = jnp.concatenate([lower_edge[:, None], lattice[:, 1:3], upper_edge[:, None]], axis=1)
    lower_edge = lattice[:, :, 0] + jnp.roll(lattice[:, :, 3], 1, axis=3)
    upper_edge = lattice[:, :, 3] + jnp.roll(lattice[:, :, 0], -1, axis=3)
    return jnp.concatenate([lower_edge[:, :, None], lattice[:, :, 1:3], upper_edge[:, :, None]], axis=2)


def average_nodes(moved, node_mass):
    fields = moved.shape[0]
    weighted = jnp.concatenate([moved * node_mass[None], node_mass[None]], axis=0)
    lattice = weighted.reshape(fields + 1, 4, 4, N_FX, N_FY, TX, TY)
    lattice = lattice.transpose(0, 1, 2, 3, 5, 4, 6).reshape(fields + 1, 4, 4, N_FX * TX, N_FY * TY)
    lattice = edge_roll(lattice)
    flattened = lattice.reshape(fields + 1, 4, 4, N_FX, TX, N_FY, TY).transpose(0, 1, 2, 3, 5, 4, 6)
    flattened = flattened.reshape(fields + 1, 16, ELEMS)
    return flattened[:fields] / flattened[fields]


def reference(tracers, node_mass, point_order, offsets, source, coords):
    tile_count = N_FX * N_FY
    fields = TRACERS * LEV
    tracer_field = tracers
    for substep in range(SUBSTEPS):
        source_rows = source[substep].reshape(tile_count, POINTS)
        coord_rows = coords[substep].reshape(2, tile_count, POINTS).transpose(1, 0, 2)
        current_field = tracer_field

        def per_tile(bundle):
            tile_id, own_source, own_coords, own_order, starts = bundle
            position = jnp.arange(POINTS, dtype=jnp.int32)
            run_index = jnp.sum((position[:, None] >= starts[None, 1:9]).astype(jnp.int32), axis=1)
            tile_row = tile_id // N_FY
            tile_column = tile_id % N_FY
            owner = ((tile_row + run_index // 3 - 1) % N_FX) * N_FY + (tile_column + run_index % 3 - 1) % N_FY
            element = (owner * E_DEV + own_source).astype(jnp.int32)
            request = jnp.concatenate([element[None], own_coords], axis=0)
            values = interpolate(current_field, request)
            placed = jnp.zeros((fields, POINTS), jnp.float32).at[:, own_order].set(values)
            return placed.reshape(fields, 16, E_DEV)

        moved = lax.map(per_tile, (jnp.arange(tile_count, dtype=jnp.int32), source_rows, coord_rows, point_order[substep], offsets[substep]))
        moved = moved.transpose(1, 2, 0, 3).reshape(fields, 16, ELEMS)
        tracer_field = average_nodes(moved, node_mass)
    return tracer_field
```

```python
import jax
import jax.numpy as jnp
from jax import lax
from jax.experimental import pallas as pl
from jax.experimental.pallas import tpu as pltpu
from jax.sharding import PartitionSpec as P

TX = 16
CAP = 128
QGRID = 1024
SUBSTEPS = 2
F = 64
E = 256
NODES = 16
POINTS = 4096
TILES = POINTS // 128
PIECES = (((0, 10), (10, 14), (14, 16)), ((0, 8), (8, 14), (14, 16)))
GLL_NODES = (-1.0, -0.4472135954999579, 0.4472135954999579, 1.0)
REMOTE = (0, 1, 2, 3, 5, 6, 7, 8)
BF16 = jnp.bfloat16
F32 = jnp.float32
VMEM_LIMIT = 40 * 2**20


def call(body, out_shape, name, hbm=(), count=0, after=0, scratch=()):
    specs = [
        pl.BlockSpec(memory_space=pltpu.HBM if i in hbm else pltpu.VMEM) for i in range(count)
    ] + [pl.BlockSpec(memory_space=pl.ANY)] * after

    def kernel(*refs):
        body(*refs[:count], *refs[count + after :])

    return pl.pallas_call(
        kernel,
        out_shape=out_shape,
        in_specs=specs,
        scratch_shapes=scratch,
        name=name,
        compiler_params=pltpu.CompilerParams(vmem_limit_bytes=VMEM_LIMIT),
    )


def in_hbm(array):
    return pltpu.with_memory_space_constraint(array, pltpu.HBM)


def shape(dims, dtype=F32):
    return jax.ShapeDtypeStruct(dims, dtype)


def swap_far(axis, block):
    size = lax.axis_size(axis)
    pairs = [(i, (((i + size - 1) % size ^ 1) + 1) % size) for i in range(size)]
    return lax.ppermute(block, axis, pairs)


def swap_near(axis, block):
    return lax.ppermute(block, axis, [(i, i ^ 1) for i in range(lax.axis_size(axis))])


def swap(axis, far, near):
    return swap_far(axis, far), swap_near(axis, near)


def to_swaps(axis, low, high):
    even = lax.axis_index(axis) % 2 == 0
    return jnp.where(even, low, high), jnp.where(even, high, low)


def from_swaps(axis, first, second):
    even = lax.axis_index(axis) % 2 == 0
    return jnp.where(even, first, second), jnp.where(even, second, first)


def lagrange(step):
    x = step * (2.0 / QGRID) - 1.0
    rows = []
    for a in range(4):
        factor = None
        for b in range(4):
            if b != a:
                term = (x - GLL_NODES[b]) * (1.0 / (GLL_NODES[a] - GLL_NODES[b]))
                factor = term if factor is None else factor * term
        rows.append(factor)
    return rows


def halves(block):
    high = block.astype(BF16)
    return high, (block - high.astype(F32)).astype(BF16)


def one_hot(index_rows, depth):
    rows = lax.broadcasted_iota(jnp.int32, (depth, 128), 0).astype(F32).astype(BF16)
    parts = [jnp.where(rows == r.astype(BF16), BF16(1), BF16(0)) for r in index_rows]
    return jnp.concatenate(parts, axis=1)


def lane_index(rows):
    return lax.broadcasted_iota(jnp.int32, (rows, 128), 1)


def eight(row):
    return jnp.broadcast_to(row, (8, row.shape[1]))


def pick_lanes(block, index):
    return jnp.take_along_axis(block, index, axis=1, mode="promise_in_bounds")


def faces(tile):
    rows = tile(0, 0).shape[0]
    lane = lane_index(rows)
    along_x = jnp.zeros((rows, 128), F32)
    for b in range(4):
        along_x = jnp.where(lane // 16 == b, pltpu.roll(tile(b, 0), b * 16, 1), along_x)
        shifted = pltpu.roll(tile(12 + b, 1), (b * 16 + 80) % 128, 1)
        along_x = jnp.where(lane // 16 == b + 4, shifted, along_x)
    along_y = jnp.zeros((rows, 128), F32)
    index = (lane % 8) * 16
    for a in range(4):
        for t in range(2):
            here = ((lane % 64) // 16 == a) & ((lane % 16) // 8 == t)
            first = pick_lanes(tile(4 * a, t), index)
            last = pick_lanes(tile(4 * a + 3, t), index + 15)
            along_y = jnp.where(here, jnp.where(lane < 64, first, last), along_y)
    return along_x, along_y


def summed_faces(own, low, high):
    lane = lane_index(own.shape[0])
    place = lane % 64
    behind = pltpu.roll(own, 128 - 48 + 1, 1)
    ahead = pltpu.roll(own, 48 - 1, 1)
    behind = jnp.where(lane == 0, low[:, 64:65], jnp.where(lane == 64, low[:, 127:128], behind))
    ahead = jnp.where(lane == 63, high[:, 0:1], jnp.where(lane == 127, high[:, 63:64], ahead))
    return own + jnp.where(place < 16, behind, jnp.where(place >= 48, ahead, 0.0))


def summed_nodes(nodes, low, high):
    rows = nodes[0].shape[0]
    lane = lane_index(rows)
    wide = lax.broadcasted_iota(jnp.int32, (rows, E), 1)
    nodes = list(nodes)
    for b in range(4):
        first, last = nodes[b], nodes[12 + b]
        behind = pltpu.roll(last, 16, 1)
        ahead = pltpu.roll(first, E - 16, 1)
        from_low = pltpu.roll(low, (128 - 64 - 16 * b) % 128, 1)
        from_high = pltpu.roll(high, 112 - 16 * b, 1)
        behind = jnp.concatenate(
            [jnp.where(lane < 16, from_low, behind[:, :128]), behind[:, 128:]], axis=1
        )
        ahead = jnp.concatenate(
            [ahead[:, :128], jnp.where(lane >= 112, from_high, ahead[:, 128:])], axis=1
        )
        nodes[b] = first + behind
        nodes[12 + b] = last + ahead
    for a in range(4):
        first, last = nodes[4 * a], nodes[4 * a + 3]
        behind = jnp.where(wide % 16 == 0, 0.0, pltpu.roll(last, 1, 1))
        ahead = jnp.where(wide % 16 == 15, 0.0, pltpu.roll(first, E - 1, 1))
        nodes[4 * a] = first + behind
        nodes[4 * a + 3] = last + ahead
    return nodes


def halo_of(low, high):
    lane = lane_index(low.shape[0])
    return pltpu.roll(jnp.where(lane >= 64, low, high), 64, 1)


def with_halo(n, node, halo):
    if n % 4 not in (0, 3):
        return node
    rows = node.shape[0]
    lane = lane_index(rows)
    wide = lax.broadcasted_iota(jnp.int32, (rows, E), 1)
    start = 16 * (n // 4) + (64 if n % 4 == 3 else 0)
    spread = [pick_lanes(halo, start + 8 * t + lane // 16) for t in range(2)]
    at = 15 if n % 4 == 3 else 0
    return node + jnp.where(wide % 16 == at, jnp.concatenate(spread, axis=1), 0.0)


def fetch(pairs, sems):
    copies = [pltpu.make_async_copy(*pair, sems.at[i]) for i, pair in enumerate(pairs)]
    for copy in copies:
        copy.start()
    for copy in copies:
        copy.wait()


def asks_body(
    offsets_in, source_in, coords_in, mass_in, first, second, mid, mass_faces,
    offsets, source, coords, mass, rows, message, sems,
):
    fetch(
        [(offsets_in, offsets), (source_in, source), (coords_in, coords), (mass_in, mass)], sems
    )
    for s in range(SUBSTEPS):
        rows[3 * s : 3 * s + 1, :] = source[s : s + 1, :].astype(F32)
        rows[3 * s + 1 : 3 * s + 3, :] = coords[s].astype(F32)
    rows[6:8, :] = jnp.zeros((2, POINTS), F32)
    early = lax.broadcasted_iota(jnp.int32, (8, 128), 0) < 3
    for k in REMOTE:
        parts = []
        for s in range(SUBSTEPS):
            start = offsets[s, 0, k]
            tile = jnp.minimum(start // 128, TILES - 1)
            after = jnp.minimum(tile + 1, TILES - 1)
            wide = jnp.concatenate(
                [rows[:, pl.ds(pl.multiple_of(t * 128, 128), 128)] for t in (tile, after)], axis=1
            )
            parts.append(pltpu.roll(wide, 256 - (start - tile * 128), 1)[:, 0:128])
        message[k * 8 : (k + 1) * 8, :] = jnp.where(early, parts[0], parts[1])
    along_x, along_y = faces(lambda n, t: eight(mass[n : n + 1, t * 128 : (t + 1) * 128]))
    for k in (1, 7):
        message[k * 8 + 6 : k * 8 + 7, :] = along_x[0:1]
    mass_faces[:, 0:128] = along_x
    mass_faces[:, 128:256] = along_y
    message[32:40, :] = jnp.zeros((8, 128), F32)
    first[...], second[...] = to_swaps("fx", message[0:24, :], message[48:72, :])
    mid[...] = message[24:48, :]


def order_body(
    s, offsets_in, order_in, source_in, coords_in, picks, factors, face_picks,
    offsets, order, source, coords, sems,
):
    fetch(
        [(offsets_in, offsets), (order_in, order), (source_in, source), (coords_in, coords)], sems
    )
    chunk = 1024
    total = None
    for c in range(POINTS // chunk):
        lanes = slice(c * chunk, (c + 1) * chunk)
        node = order[s, :, lanes]
        tile_of = (node // 128).astype(F32).astype(BF16)
        lane_of = (node % 128).astype(F32).astype(BF16)
        position = lax.broadcasted_iota(jnp.int32, (1, chunk), 1) + c * chunk
        run = jnp.zeros((1, chunk), jnp.int32)
        begin = jnp.zeros((1, chunk), jnp.int32) + offsets[s, 0, 0]
        for k in range(1, 9):
            passed = position >= offsets[s, 0, k]
            run = run + passed.astype(jnp.int32)
            begin = jnp.where(passed, offsets[s, 0, k], begin)
        own = run == 4
        kind = jnp.where(own, 8, jnp.where(run > 4, run - 1, run))
        pick = jnp.where(own, source[s : s + 1, lanes], position - begin)
        cx = coords[s, 0:1, lanes]
        cy = coords[s, 1:2, lanes]
        values = [pick, cx // 8, cx % 8, cy // 8, cy % 8, kind]
        tiles = lax.broadcasted_iota(jnp.int32, (TILES, chunk), 0).astype(F32).astype(BF16)
        here = tiles == tile_of
        left = jnp.concatenate(
            [jnp.where(here, v.astype(F32).astype(BF16), BF16(0)) for v in values], axis=0
        )
        spots = lax.broadcasted_iota(jnp.int32, (128, chunk), 0).astype(F32).astype(BF16)
        right = jnp.where(spots == lane_of, BF16(1), BF16(0))
        part = lax.dot_general(left, right, (((1,), (1,)), ((), ())), preferred_element_type=F32)
        total = part if total is None else total + part
    pick, xh, xl, yh, yl, kind = [total[q * TILES : (q + 1) * TILES] for q in range(6)]
    own = kind > 7.5
    picks[0] = jnp.where(own, pick, -1.0)
    picks[1] = jnp.where(own, -1.0, pick)
    mask = jnp.where(own, 1.0, 0.0)
    along_x = [row * mask for row in lagrange(xh * 8.0 + xl)]
    along_y = lagrange(yh * 8.0 + yl)
    for n in range(NODES):
        factors[n] = along_x[n // 4] * along_y[n % 4]
    for d in range(8):
        factors[NODES + d] = jnp.where(jnp.abs(kind - d) < 0.5, 1.0, 0.0)
    for q, rows in enumerate((picks[1], kind, picks[0], xh * 8.0 + xl, yh * 8.0 + yl)):
        along = faces(lambda n, t: eight(rows[2 * n + t : 2 * n + t + 1]))
        face_picks[q : q + 1, :] = jnp.concatenate(along, axis=1)[0:1]


def table_body(tracers_in, table, tracers, sems):
    fetch([(tracers_in, tracers)], sems)
    for q in range(0, F, 16):
        block = jnp.swapaxes(tracers[q : q + 16], 0, 1)
        for n in range(NODES):
            high, low = halves(block[n])
            table[n * F + q : n * F + q + 16, 0:E] = high
            table[n * F + q : n * F + q + 16, E : 2 * E] = low


def column_body(x_first, x_second, mid, mass_faces, first, second):
    low, high = from_swaps("fx", x_first[...], x_second[...])
    masses = summed_faces(mass_faces[:, 128:256], low[8:16], high[8:16])[6:7]
    rows = lax.broadcasted_iota(jnp.int32, (8, 128), 0)
    columns = []
    for k in (0, 2):
        block = slice(k * 8, (k + 1) * 8)
        center = jnp.where(rows == 6, masses, mid[block, :])
        columns.append(jnp.concatenate([high[block], center, low[block]], axis=0))
    first[...], second[...] = to_swaps("fy", *columns)


def row_body(y_first, y_second, own, far, near):
    low, high = from_swaps("fy", y_first[...], y_second[...])
    mine = own[...]
    ahead = jnp.concatenate([low[0:F], mine[0:F], high[0:F]], axis=0)
    behind = jnp.concatenate([low[2 * F :], mine[F:], high[2 * F :]], axis=0)
    far[...], near[...] = to_swaps("fx", behind, ahead)


def combine(products, weights):
    total = None
    for n, weight in enumerate(weights):
        term = products[n * F : (n + 1) * F] * weight
        total = term if total is None else total + term
    return total


def asked_blocks(x_first, x_second, y_first, y_second):
    x_low, x_high = from_swaps("fx", x_first[...], x_second[...])
    y_low, y_high = from_swaps("fy", y_first[...], y_second[...])
    by_direction = {(1, 0): x_low[8:16], (-1, 0): x_high[8:16]}
    for k in range(3):
        by_direction[(k - 1, 1)] = y_low[k * 8 : (k + 1) * 8]
        by_direction[(k - 1, -1)] = y_high[k * 8 : (k + 1) * 8]
    return [by_direction[(k // 3 - 1, k % 3 - 1)] for k in REMOTE]


def asked_rows(s, asked):
    return [
        jnp.concatenate([r[s * 3 + q : s * 3 + q + 1, :] for r in asked], axis=0) for q in range(3)
    ]


def weights_of(cx, cy):
    along_x = lagrange(cx)
    along_y = lagrange(cy)
    return [along_x[n // 4] * along_y[n % 4] for n in range(NODES)]


def answer(table, pick, weights, directions):
    values = {}
    for both in directions:
        hot = one_hot([pick[d : d + 1] for d in both], E)
        products = jnp.dot(
            table[...], jnp.concatenate([hot, hot], axis=0), preferred_element_type=F32
        )
        for h, d in enumerate(both):
            lanes = slice(h * 128, (h + 1) * 128)
            values[d] = combine(products[:, lanes], [w[d : d + 1] for w in weights])
    return values


BEHIND = (2, 4, 7)
AHEAD = (0, 3, 5)
SIDES = (1, 6)


def sides_first(rows):
    even = lax.axis_index("fy") % 2 == 0
    pairs = [(rows[b : b + 1], rows[a : a + 1]) for b, a in zip(BEHIND, AHEAD)]
    far = [jnp.where(even, behind, ahead) for behind, ahead in pairs]
    near = [jnp.where(even, ahead, behind) for behind, ahead in pairs]
    return jnp.concatenate(far + near + [rows[0:2]], axis=0)


def reply_y_body(table, x_first, x_second, y_first, y_second, far, near):
    rows = asked_rows(0, asked_blocks(x_first, x_second, y_first, y_second))
    pick, cx, cy = [sides_first(block) for block in rows]
    values = answer(table, pick, weights_of(cx, cy), ((0, 1), (2, 3), (4, 5)))
    for k in range(3):
        far[k * F : (k + 1) * F, :] = values[k]
        near[k * F : (k + 1) * F, :] = values[3 + k]


def reply_x_body(s, table, x_first, x_second, y_first, y_second, own):
    pick, cx, cy = asked_rows(s, asked_blocks(x_first, x_second, y_first, y_second))
    values = answer(table, pick, weights_of(cx, cy), (SIDES,))
    for k, d in enumerate(SIDES):
        own[k * F : (k + 1) * F, :] = values[d]


def early_body(s, table, x_first, x_second, y_first, y_second, values, lanes, shares):
    rows = asked_rows(s, asked_blocks(x_first, x_second, y_first, y_second))
    pick, cx, cy = [sides_first(block) for block in rows]
    weights = weights_of(cx, cy)
    found = answer(table, pick, weights, ((0, 1), (2, 3), (4, 5)))
    for d, value in found.items():
        values[d] = value
    element = pick.astype(jnp.int32)
    lanes[...] = element // 16 + jnp.where(element % 16 == 15, 64, 0)
    for a in range(4):
        share = jnp.where(element % 16 == 15, weights[4 * a + 3], 0.0)
        shares[a] = jnp.where(element % 16 == 0, weights[4 * a], share)


def late_body(values, lanes, shares, y_first, y_second, scale, far, near):
    halo = halo_of(*from_swaps("fy", y_first[...], y_second[...])) * scale[0:1, :]
    for d in range(6):
        index = jnp.broadcast_to(lanes[d : d + 1, :], (F, 128))
        value = values[d]
        for a in range(4):
            value = value + pick_lanes(halo, index + 16 * a) * shares[a, d : d + 1, :]
        (far if d < 3 else near)[d % 3 * F : (d % 3 + 1) * F, :] = value


def own_body(begin, table, picks, factors, result):
    def block(i, carry):
        at = 2 * (begin + i)
        hot = one_hot([picks[0, pl.ds(at + h, 1), :] for h in range(2)], E)
        products = jnp.dot(
            table[...], jnp.concatenate([hot, hot], axis=0), preferred_element_type=F32
        )
        weights = [
            jnp.concatenate([factors[n, pl.ds(at + h, 1), :] for h in range(2)], axis=1)
            for n in range(NODES)
        ]
        result[:, pl.ds(pl.multiple_of(i * E, E), E)] = combine(products, weights)
        return carry

    count = result.shape[1] // E
    lax.fori_loop(0, count, block, 0, unroll=5 if count == 10 else 4 if count == 8 else 3 if count == 6 else count)


def stacked(blocks):
    return jnp.concatenate([jnp.concatenate(halves(block), axis=1) for block in blocks], axis=0)


def three(ref):
    return [ref[k * F : (k + 1) * F, :] for k in range(3)]


def middles(y_first, y_second):
    return list(from_swaps("fy", y_first[F : 2 * F, :], y_second[F : 2 * F, :]))


def arrived(x_first, x_second, y_first, y_second):
    even = lax.axis_index("fx") % 2 == 0
    pairs = list(zip(three(x_first), three(x_second)))
    low = [jnp.where(even, far, near) for far, near in pairs]
    high = [jnp.where(even, near, far) for far, near in pairs]
    return stacked(low + middles(y_first, y_second) + high)


def placed(answers, slots, masks):
    hot = one_hot(slots, CAP)
    products = jnp.dot(answers, jnp.concatenate([hot, hot], axis=0), preferred_element_type=F32)
    return combine(products, masks)


def masks_of(kind, bases):
    return [jnp.where(jnp.abs(kind - base) < 0.5, 1.0, 0.0) for base in bases]


def kinds(even, near):
    start = jnp.where(even == near, 5.0, 0.0)
    return [start + k for k in range(3)]


def face_slots(face_picks):
    return [face_picks[0:1, h * 128 : (h + 1) * 128] for h in range(2)]


def own_faces_body(table, face_picks, result):
    hot = one_hot([face_picks[2:3, h * 128 : (h + 1) * 128] for h in range(2)], E)
    products = jnp.dot(table[...], jnp.concatenate([hot, hot], axis=0), preferred_element_type=F32)
    result[...] = combine(products, weights_of(face_picks[3:4, :], face_picks[4:5, :]))


def face_near_body(
    own, near, far, y_first, y_second, face_picks, mass_faces, partial, message
):
    even = lax.axis_index("fx") % 2 == 0
    masks = masks_of(face_picks[1:2, :], kinds(even, True) + [3.0, 4.0])
    answers = stacked(three(near) + middles(y_first, y_second))
    moved = own[...] + placed(answers, face_slots(face_picks), masks)
    moved = moved * mass_faces[0:1, :]
    partial[...] = moved
    message[0 : 3 * F, :] = far[...]
    message[3 * F : 4 * F, :] = moved[:, 0:128]
    message[4 * F : 4 * F + 8, :] = face_picks[:, 0:128]
    message[4 * F + 2 : 4 * F + 3, :] = mass_faces[0:1, 0:128]


def face_far_body(partial, far, sent, face_picks, mass_faces, along_x, along_y, other):
    even = lax.axis_index("fx") % 2 == 0
    masks = masks_of(face_picks[1:2, :], kinds(even, False))
    moved = placed(stacked(three(far)), face_slots(face_picks), masks) * mass_faces[0:1, :]
    result = partial[...] + moved
    along_x[...] = result[:, 0:128]
    along_y[...] = result[:, 128:256]
    slot, kind, weight = [far[4 * F + q : 4 * F + q + 1, :] for q in range(3)]
    moved = placed(stacked(three(sent)), [slot], masks_of(kind, kinds(even, True)))
    other[...] = far[3 * F : 4 * F, :] + moved * weight


def place_body(
    s, own_a, own_b, own_c, x_first, x_second, y_first, y_second, picks, factors, mass, result
):
    answers = arrived(x_first, x_second, y_first, y_second)
    for n in range(NODES):
        tiles = [slice(2 * n + h, 2 * n + h + 1) for h in range(2)]
        masks = [
            jnp.concatenate([factors[NODES + d, t, :] for t in tiles], axis=1) for d in range(8)
        ]
        moved = placed(answers, [picks[1, t, :] for t in tiles], masks)
        for ref, (begin, end) in zip((own_a, own_b, own_c), PIECES[s]):
            if begin <= n < end:
                own = ref[:, (n - begin) * E : (n - begin + 1) * E]
        result[:, n * E : (n + 1) * E] = (own + moved) * mass[n : n + 1, :]


def rim_body(along_y, x_first, x_second, first, second):
    low, high = from_swaps("fx", x_first[...], x_second[...])
    result = summed_faces(along_y[...], low, high)
    first[...] = result
    second[...] = result


def scale_body(mass, x_first, x_second, y_first, y_second, inverse, on_faces):
    x_low, x_high = from_swaps("fx", x_first[8:16, :], x_second[8:16, :])
    y_low, y_high = from_swaps("fy", y_first[8:16, :], y_second[8:16, :])
    low, high, halo = [
        eight(row[6:7]) for row in (x_low, x_high, halo_of(y_low, y_high))
    ]
    nodes = [eight(mass[n : n + 1, :]) for n in range(NODES)]
    nodes = summed_nodes(nodes, low, high)
    nodes = [1.0 / with_halo(n, node, halo) for n, node in enumerate(nodes)]
    for n in range(NODES):
        inverse[n : n + 1, :] = nodes[n][0:1]
    on_faces[...] = faces(lambda n, t: nodes[n][:, t * 128 : (t + 1) * 128])[1]


def sum_body(weighted, x_first, x_second, inverse, result, table=None):
    low, high = from_swaps("fx", x_first[...], x_second[...])
    nodes = summed_nodes([weighted[:, n * E : (n + 1) * E] for n in range(NODES)], low, high)
    for n in range(NODES):
        node = nodes[n] * inverse[n : n + 1, :]
        result[:, n * E : (n + 1) * E] = node
        if table is not None:
            high_part, low_part = halves(node)
            table[n * F : (n + 1) * F, 0:E] = high_part
            table[n * F : (n + 1) * F, E : 2 * E] = low_part


def finish_body(summed, y_first, y_second, scale, table):
    halo = halo_of(*from_swaps("fy", y_first[...], y_second[...])) * scale[0:1, :]
    for n in range(NODES):
        node = with_halo(n, summed[:, n * E : (n + 1) * E], halo)
        high, low = halves(node)
        table[n * F : (n + 1) * F, 0:E] = high
        table[n * F : (n + 1) * F, E : 2 * E] = low


def last_body(summed, y_first, y_second, scale, result, block, sems):
    halo = halo_of(*from_swaps("fy", y_first[...], y_second[...])) * scale[0:1, :]
    copies = []
    for i in range(F // 8):
        rows = slice(i * 8, (i + 1) * 8)
        nodes = [
            with_halo(n, summed[rows, n * E : (n + 1) * E], halo[rows]) for n in range(NODES)
        ]
        block[rows] = jnp.swapaxes(jnp.stack(nodes), 0, 1)
        copy = pltpu.make_async_copy(block.at[rows], result.at[rows], sems.at[i])
        copy.start()
        copies.append(copy)
    for copy in copies:
        copy.wait()


def per_device(tracers, node_mass, point_order, offsets, source, coords):
    ask = shape((24, 128))
    answers = shape((3 * F, 128))
    face = shape((F, 128))
    table_shape = shape((NODES * F, 2 * E), BF16)
    lists = [
        pltpu.SMEM(offsets.shape, jnp.int32),
        pltpu.VMEM(source.shape, jnp.int32),
        pltpu.VMEM(coords.shape, jnp.int32),
    ]
    first, second, mid, mass_faces = call(
        asks_body,
        [ask, ask, ask, shape((8, 256))],
        "asks",
        hbm=(0, 1, 2, 3),
        count=4,
        scratch=lists
        + [
            pltpu.VMEM(node_mass.shape, F32),
            pltpu.VMEM((8, POINTS), F32),
            pltpu.VMEM((72, 128), F32),
            pltpu.SemaphoreType.DMA((4,)),
        ],
    )(*[in_hbm(a) for a in (offsets, source, coords, node_mass)])
    asked = swap("fx", first, second)
    lists_in = [in_hbm(a) for a in (offsets, point_order, source, coords)]

    def requests(s, after=0):
        return call(
            lambda *refs: order_body(s, *refs),
            [shape((2, TILES, 128)), shape((NODES + 8, TILES, 128)), shape((8, 256))],
            "order",
            hbm=(0, 1, 2, 3),
            count=4,
            after=after,
            scratch=lists[:1]
            + [pltpu.VMEM(point_order.shape, jnp.int32)]
            + lists[1:]
            + [pltpu.SemaphoreType.DMA((4,))],
        )

    def interpolate(s, piece, after=0):
        begin, end = PIECES[s][piece]
        return call(
            lambda *refs: own_body(begin, *refs),
            shape((F, (end - begin) * E)),
            "own",
            count=3,
            after=after,
        )

    ordered = [requests(0)(*lists_in)]
    asked += swap(
        "fy",
        *call(column_body, [ask] * 2, "column", count=4)(*asked, mid, mass_faces),
    )
    table = call(
        table_body,
        table_shape,
        "table",
        hbm=(0,),
        count=1,
        scratch=[pltpu.VMEM(tracers.shape, F32), pltpu.SemaphoreType.DMA((1,))],
    )(in_hbm(tracers))
    far, near = call(reply_y_body, [answers] * 2, "reply_y", count=5, after=1)(
        table, *asked, ordered[0][2]
    )
    answers_y = swap("fy", far, near)
    inverse, scale = call(scale_body, [shape((NODES, E)), shape((8, 128))], "scale", count=5)(
        node_mass, *asked
    )
    for s in range(SUBSTEPS):
        picks, factors, face_picks = ordered[s]
        if s == 1:
            table = call(finish_body, table_shape, "finish", count=4)(summed, *edges_y, scale)
        own = call(
            lambda *refs, s=s: reply_x_body(s, *refs), shape((2 * F, 128)), "reply_x", count=5
        )(table, *asked)
        own_faces = call(own_faces_body, shape((F, 256)), "own_faces", count=2)(table, face_picks)
        own_a = interpolate(s, 0)(table, picks, factors)
        far, near = call(row_body, [answers] * 2, "row", count=3, after=3)(
            *answers_y, own, own_a, scale, own_faces
        )
        near = swap_near("fx", near)
        partial, message = call(
            face_near_body, [shape((F, 256)), shape((4 * F + 8, 128))], "faces_near", count=7
        )(own_faces, near, far, *answers_y, face_picks, mass_faces)
        far = swap_far("fx", message)
        own_b = interpolate(s, 1, after=1)(table, picks, factors, partial)
        if s == 0:
            ordered.append(requests(1, after=1)(*lists_in, partial))
        along_x, along_y, other = call(
            face_far_body, [face] * 3, "faces_far", count=5, after=2
        )(partial, far, message, face_picks, mass_faces, own_b, ordered[1][2])
        edges_x = (other, swap_near("fx", along_x))
        first, second = call(rim_body, [face] * 2, "rim", count=3)(along_y, *edges_x)
        edges_y = swap("fy", first, second)
        own_c = interpolate(s, 2, after=1)(table, picks, factors, second)
        weighted = call(
            lambda *refs, s=s: place_body(s, *refs), shape((F, POINTS)), "place", count=10
        )(
            own_a, own_b, own_c, far, near, *answers_y, picks, factors, node_mass
        )
        if s == 0:
            summed, early_table = call(
                sum_body, [shape((F, POINTS)), table_shape], "sum", count=4
            )(weighted, *edges_x, inverse)
            early = call(
                lambda *refs: early_body(1, *refs),
                [shape((8, F, 128)), shape((8, 128), jnp.int32), shape((4, 8, 128))],
                "early",
                count=5,
            )(early_table, *asked)
            far, near = call(late_body, [answers] * 2, "late", count=6)(
                *early, *edges_y, scale
            )
            answers_y = swap("fy", far, near)
        else:
            summed = call(sum_body, shape((F, POINTS)), "sum", count=4)(
                weighted, *edges_x, inverse
            )
            result = pl.pallas_call(
                last_body,
                out_shape=shape((F, NODES, E)),
                in_specs=[pl.BlockSpec(memory_space=pltpu.VMEM)] * 4,
                out_specs=pl.BlockSpec(memory_space=pltpu.HBM),
                scratch_shapes=[
                    pltpu.VMEM((F, NODES, E), F32),
                    pltpu.SemaphoreType.DMA((F // 8,)),
                ],
                name="last",
                compiler_params=pltpu.CompilerParams(vmem_limit_bytes=VMEM_LIMIT),
            )(summed, *edges_y, scale)
    return result


def solution(mesh):
    return jax.shard_map(
        per_device,
        mesh=mesh,
        in_specs=(
            P(None, None, ("fx", "fy")),
            P(None, ("fx", "fy")),
            P(None, ("fx", "fy"), None),
            P(None, ("fx", "fy"), None),
            P(None, ("fx", "fy")),
            P(None, None, ("fx", "fy")),
        ),
        out_specs=P(None, None, ("fx", "fy")),
        check_vma=False,
    )
```

```python
import jax
import jax.numpy as jnp
from jax import lax
from jax.experimental import pallas as pl
from jax.experimental.pallas import tpu as pltpu
from jax.sharding import PartitionSpec as P

TX = 16
CAP = 128
QGRID = 1024
SUBSTEPS = 2
F = 64
E = 256
NODES = 16
POINTS = 4096
TILES = POINTS // 128
PIECES = (((0, 10), (10, 14), (14, 16)), ((0, 9), (9, 13), (13, 16)))
GLL_NODES = (-1.0, -0.4472135954999579, 0.4472135954999579, 1.0)
REMOTE = (0, 1, 2, 3, 5, 6, 7, 8)
BF16 = jnp.bfloat16
F32 = jnp.float32
VMEM_LIMIT = 40 * 2**20


def call(body, out_shape, name, hbm=(), count=0, after=0, scratch=()):
    specs = [
        pl.BlockSpec(memory_space=pltpu.HBM if i in hbm else pltpu.VMEM) for i in range(count)
    ] + [pl.BlockSpec(memory_space=pl.ANY)] * after

    def kernel(*refs):
        body(*refs[:count], *refs[count + after :])

    return pl.pallas_call(
        kernel,
        out_shape=out_shape,
        in_specs=specs,
        scratch_shapes=scratch,
        name=name,
        compiler_params=pltpu.CompilerParams(vmem_limit_bytes=VMEM_LIMIT),
    )


def in_hbm(array):
    return pltpu.with_memory_space_constraint(array, pltpu.HBM)


def shape(dims, dtype=F32):
    return jax.ShapeDtypeStruct(dims, dtype)


def swap_far(axis, block):
    size = lax.axis_size(axis)
    pairs = [(i, (((i + size - 1) % size ^ 1) + 1) % size) for i in range(size)]
    return lax.ppermute(block, axis, pairs)


def swap_near(axis, block):
    return lax.ppermute(block, axis, [(i, i ^ 1) for i in range(lax.axis_size(axis))])


def swap(axis, far, near):
    return swap_far(axis, far), swap_near(axis, near)


def to_swaps(axis, low, high):
    even = lax.axis_index(axis) % 2 == 0
    return jnp.where(even, low, high), jnp.where(even, high, low)


def from_swaps(axis, first, second):
    even = lax.axis_index(axis) % 2 == 0
    return jnp.where(even, first, second), jnp.where(even, second, first)


def lagrange(step):
    x = step * (2.0 / QGRID) - 1.0
    rows = []
    for a in range(4):
        factor = None
        for b in range(4):
            if b != a:
                term = (x - GLL_NODES[b]) * (1.0 / (GLL_NODES[a] - GLL_NODES[b]))
                factor = term if factor is None else factor * term
        rows.append(factor)
    return rows


def halves(block):
    high = block.astype(BF16)
    return high, (block - high.astype(F32)).astype(BF16)


def one_hot(index_rows, depth):
    rows = lax.broadcasted_iota(jnp.int32, (depth, 128), 0).astype(F32).astype(BF16)
    parts = [jnp.where(rows == r.astype(BF16), BF16(1), BF16(0)) for r in index_rows]
    return jnp.concatenate(parts, axis=1)


def lane_index(rows):
    return lax.broadcasted_iota(jnp.int32, (rows, 128), 1)


def eight(row):
    return jnp.broadcast_to(row, (8, row.shape[1]))


def pick_lanes(block, index):
    return jnp.take_along_axis(block, index, axis=1, mode="promise_in_bounds")


def faces(tile):
    rows = tile(0, 0).shape[0]
    lane = lane_index(rows)
    along_x = jnp.zeros((rows, 128), F32)
    for b in range(4):
        along_x = jnp.where(lane // 16 == b, pltpu.roll(tile(b, 0), b * 16, 1), along_x)
        shifted = pltpu.roll(tile(12 + b, 1), (b * 16 + 80) % 128, 1)
        along_x = jnp.where(lane // 16 == b + 4, shifted, along_x)
    along_y = jnp.zeros((rows, 128), F32)
    index = (lane % 8) * 16
    for a in range(4):
        for t in range(2):
            here = ((lane % 64) // 16 == a) & ((lane % 16) // 8 == t)
            first = pick_lanes(tile(4 * a, t), index)
            last = pick_lanes(tile(4 * a + 3, t), index + 15)
            along_y = jnp.where(here, jnp.where(lane < 64, first, last), along_y)
    return along_x, along_y


def summed_faces(own, low, high):
    lane = lane_index(own.shape[0])
    place = lane % 64
    behind = pltpu.roll(own, 128 - 48 + 1, 1)
    ahead = pltpu.roll(own, 48 - 1, 1)
    behind = jnp.where(lane == 0, low[:, 64:65], jnp.where(lane == 64, low[:, 127:128], behind))
    ahead = jnp.where(lane == 63, high[:, 0:1], jnp.where(lane == 127, high[:, 63:64], ahead))
    return own + jnp.where(place < 16, behind, jnp.where(place >= 48, ahead, 0.0))


def summed_nodes(nodes, low, high):
    rows = nodes[0].shape[0]
    lane = lane_index(rows)
    wide = lax.broadcasted_iota(jnp.int32, (rows, E), 1)
    nodes = list(nodes)
    for b in range(4):
        first, last = nodes[b], nodes[12 + b]
        behind = pltpu.roll(last, 16, 1)
        ahead = pltpu.roll(first, E - 16, 1)
        from_low = pltpu.roll(low, (128 - 64 - 16 * b) % 128, 1)
        from_high = pltpu.roll(high, 112 - 16 * b, 1)
        behind = jnp.concatenate(
            [jnp.where(lane < 16, from_low, behind[:, :128]), behind[:, 128:]], axis=1
        )
        ahead = jnp.concatenate(
            [ahead[:, :128], jnp.where(lane >= 112, from_high, ahead[:, 128:])], axis=1
        )
        nodes[b] = first + behind
        nodes[12 + b] = last + ahead
    for a in range(4):
        first, last = nodes[4 * a], nodes[4 * a + 3]
        behind = jnp.where(wide % 16 == 0, 0.0, pltpu.roll(last, 1, 1))
        ahead = jnp.where(wide % 16 == 15, 0.0, pltpu.roll(first, E - 1, 1))
        nodes[4 * a] = first + behind
        nodes[4 * a + 3] = last + ahead
    return nodes


def halo_of(low, high):
    lane = lane_index(low.shape[0])
    return pltpu.roll(jnp.where(lane >= 64, low, high), 64, 1)


def with_halo(n, node, halo):
    if n % 4 not in (0, 3):
        return node
    rows = node.shape[0]
    lane = lane_index(rows)
    wide = lax.broadcasted_iota(jnp.int32, (rows, E), 1)
    start = 16 * (n // 4) + (64 if n % 4 == 3 else 0)
    spread = [pick_lanes(halo, start + 8 * t + lane // 16) for t in range(2)]
    at = 15 if n % 4 == 3 else 0
    return node + jnp.where(wide % 16 == at, jnp.concatenate(spread, axis=1), 0.0)


def fetch(pairs, sems):
    copies = [pltpu.make_async_copy(*pair, sems.at[i]) for i, pair in enumerate(pairs)]
    for copy in copies:
        copy.start()
    for copy in copies:
        copy.wait()


def asks_body(
    offsets_in, source_in, coords_in, mass_in, first, second, mid, mass_faces,
    offsets, source, coords, mass, rows, message, sems,
):
    fetch(
        [(offsets_in, offsets), (source_in, source), (coords_in, coords), (mass_in, mass)], sems
    )
    for s in range(SUBSTEPS):
        rows[3 * s : 3 * s + 1, :] = source[s : s + 1, :].astype(F32)
        rows[3 * s + 1 : 3 * s + 3, :] = coords[s].astype(F32)
    rows[6:8, :] = jnp.zeros((2, POINTS), F32)
    early = lax.broadcasted_iota(jnp.int32, (8, 128), 0) < 3
    for k in REMOTE:
        parts = []
        for s in range(SUBSTEPS):
            start = offsets[s, 0, k]
            tile = jnp.minimum(start // 128, TILES - 1)
            after = jnp.minimum(tile + 1, TILES - 1)
            wide = jnp.concatenate(
                [rows[:, pl.ds(pl.multiple_of(t * 128, 128), 128)] for t in (tile, after)], axis=1
            )
            parts.append(pltpu.roll(wide, 256 - (start - tile * 128), 1)[:, 0:128])
        message[k * 8 : (k + 1) * 8, :] = jnp.where(early, parts[0], parts[1])
    along_x, along_y = faces(lambda n, t: eight(mass[n : n + 1, t * 128 : (t + 1) * 128]))
    for k in (1, 7):
        message[k * 8 + 6 : k * 8 + 7, :] = along_x[0:1]
    mass_faces[:, 0:128] = along_x
    mass_faces[:, 128:256] = along_y
    message[32:40, :] = jnp.zeros((8, 128), F32)
    first[...], second[...] = to_swaps("fx", message[0:24, :], message[48:72, :])
    mid[...] = message[24:48, :]


def order_body(
    offsets_in, order_in, source_in, coords_in, picks, factors, face_picks, later, later_starts,
    offsets, order, source, coords, sems,
):
    fetch(
        [(offsets_in, offsets), (order_in, order), (source_in, source), (coords_in, coords)], sems
    )
    ordered(
        order[0], source[0:1], coords[0, 0:1], coords[0, 1:2], offsets[0], picks, factors, face_picks
    )
    later[0:1, :] = order[1]
    later[1:2, :] = source[1:2, :]
    later[2:4, :] = coords[1]
    later_starts[0:1, 0:10] = offsets[1]


def later_body(lists, starts, picks, factors, face_picks):
    ordered(
        lists[0:1], lists[1:2], lists[2:3], lists[3:4], starts[0:1], picks, factors, face_picks
    )


def ordered(nodes, sources, xs, ys, starts, picks, factors, face_picks):
    chunk = 1024
    total = None
    for c in range(POINTS // chunk):
        lanes = slice(c * chunk, (c + 1) * chunk)
        node = nodes[:, lanes]
        tile_of = (node // 128).astype(F32).astype(BF16)
        lane_of = (node % 128).astype(F32).astype(BF16)
        position = lax.broadcasted_iota(jnp.int32, (1, chunk), 1) + c * chunk
        run = jnp.zeros((1, chunk), jnp.int32)
        begin = jnp.broadcast_to(starts[:, 0:1], (1, chunk))
        for k in range(1, 9):
            start = jnp.broadcast_to(starts[:, k : k + 1], (1, chunk))
            passed = position >= start
            run = run + passed.astype(jnp.int32)
            begin = jnp.where(passed, start, begin)
        own = run == 4
        kind = jnp.where(own, 8, jnp.where(run > 4, run - 1, run))
        pick = jnp.where(own, sources[:, lanes], position - begin)
        cx = xs[:, lanes]
        cy = ys[:, lanes]
        values = [pick, cx // 8, cx % 8, cy // 8, cy % 8, kind]
        tiles = lax.broadcasted_iota(jnp.int32, (TILES, chunk), 0).astype(F32).astype(BF16)
        here = tiles == tile_of
        left = jnp.concatenate(
            [jnp.where(here, v.astype(F32).astype(BF16), BF16(0)) for v in values], axis=0
        )
        spots = lax.broadcasted_iota(jnp.int32, (128, chunk), 0).astype(F32).astype(BF16)
        right = jnp.where(spots == lane_of, BF16(1), BF16(0))
        part = lax.dot_general(left, right, (((1,), (1,)), ((), ())), preferred_element_type=F32)
        total = part if total is None else total + part
    pick, xh, xl, yh, yl, kind = [total[q * TILES : (q + 1) * TILES] for q in range(6)]
    own = kind > 7.5
    picks[0] = jnp.where(own, pick, -1.0)
    picks[1] = jnp.where(own, -1.0, pick)
    mask = jnp.where(own, 1.0, 0.0)
    along_x = [row * mask for row in lagrange(xh * 8.0 + xl)]
    along_y = lagrange(yh * 8.0 + yl)
    for n in range(NODES):
        factors[n] = along_x[n // 4] * along_y[n % 4]
    for d in range(8):
        factors[NODES + d] = jnp.where(jnp.abs(kind - d) < 0.5, 1.0, 0.0)
    for q, rows in enumerate((picks[1], kind, picks[0], xh * 8.0 + xl, yh * 8.0 + yl)):
        along = faces(lambda n, t: eight(rows[2 * n + t : 2 * n + t + 1]))
        face_picks[q : q + 1, :] = jnp.concatenate(along, axis=1)[0:1]


def table_body(tracers_in, table, tracers, sems):
    fetch([(tracers_in, tracers)], sems)
    for q in range(0, F, 16):
        block = jnp.swapaxes(tracers[q : q + 16], 0, 1)
        for n in range(NODES):
            high, low = halves(block[n])
            table[n * F + q : n * F + q + 16, 0:E] = high
            table[n * F + q : n * F + q + 16, E : 2 * E] = low


def column_body(x_first, x_second, mid, mass_faces, first, second):
    low, high = from_swaps("fx", x_first[...], x_second[...])
    masses = summed_faces(mass_faces[:, 128:256], low[8:16], high[8:16])[6:7]
    rows = lax.broadcasted_iota(jnp.int32, (8, 128), 0)
    columns = []
    for k in (0, 2):
        block = slice(k * 8, (k + 1) * 8)
        center = jnp.where(rows == 6, masses, mid[block, :])
        columns.append(jnp.concatenate([high[block], center, low[block]], axis=0))
    first[...], second[...] = to_swaps("fy", *columns)


def row_body(y_first, y_second, own, near, far):
    low, high = from_swaps("fy", y_first[...], y_second[...])
    mine = own[...]
    ahead = jnp.concatenate([low[0:F], mine[0:F], high[0:F]], axis=0)
    behind = jnp.concatenate([low[2 * F :], mine[F:], high[2 * F :]], axis=0)
    far[...], near[...] = to_swaps("fx", behind, ahead)


def combine(products, weights):
    total = None
    for n, weight in enumerate(weights):
        term = products[n * F : (n + 1) * F] * weight
        total = term if total is None else total + term
    return total


def asked_blocks(x_first, x_second, y_first, y_second):
    x_low, x_high = from_swaps("fx", x_first[...], x_second[...])
    y_low, y_high = from_swaps("fy", y_first[...], y_second[...])
    by_direction = {(1, 0): x_low[8:16], (-1, 0): x_high[8:16]}
    for k in range(3):
        by_direction[(k - 1, 1)] = y_low[k * 8 : (k + 1) * 8]
        by_direction[(k - 1, -1)] = y_high[k * 8 : (k + 1) * 8]
    return [by_direction[(k // 3 - 1, k % 3 - 1)] for k in REMOTE]


def asked_rows(s, asked):
    return [
        jnp.concatenate([r[s * 3 + q : s * 3 + q + 1, :] for r in asked], axis=0) for q in range(3)
    ]


def weights_of(cx, cy):
    along_x = lagrange(cx)
    along_y = lagrange(cy)
    return [along_x[n // 4] * along_y[n % 4] for n in range(NODES)]


def answer(table, pick, weights, directions):
    values = {}
    for both in directions:
        hot = one_hot([pick[d : d + 1] for d in both], E)
        products = jnp.dot(
            table[...], jnp.concatenate([hot, hot], axis=0), preferred_element_type=F32
        )
        for h, d in enumerate(both):
            lanes = slice(h * 128, (h + 1) * 128)
            values[d] = combine(products[:, lanes], [w[d : d + 1] for w in weights])
    return values


BEHIND = (2, 4, 7)
AHEAD = (0, 3, 5)
SIDES = (1, 6)


def sides_first(rows):
    even = lax.axis_index("fy") % 2 == 0
    pairs = [(rows[b : b + 1], rows[a : a + 1]) for b, a in zip(BEHIND, AHEAD)]
    far = [jnp.where(even, behind, ahead) for behind, ahead in pairs]
    near = [jnp.where(even, ahead, behind) for behind, ahead in pairs]
    return jnp.concatenate(far + near + [rows[0:2]], axis=0)


def reply_y_body(table, x_first, x_second, y_first, y_second, far, near):
    rows = asked_rows(0, asked_blocks(x_first, x_second, y_first, y_second))
    pick, cx, cy = [sides_first(block) for block in rows]
    values = answer(table, pick, weights_of(cx, cy), ((0, 1), (2, 3), (4, 5)))
    for k in range(3):
        far[k * F : (k + 1) * F, :] = values[k]
        near[k * F : (k + 1) * F, :] = values[3 + k]


def reply_x_body(s, table, x_first, x_second, y_first, y_second, own):
    pick, cx, cy = asked_rows(s, asked_blocks(x_first, x_second, y_first, y_second))
    values = answer(table, pick, weights_of(cx, cy), (SIDES,))
    for k, d in enumerate(SIDES):
        own[k * F : (k + 1) * F, :] = values[d]


def early_body(s, table, x_first, x_second, y_first, y_second, values, lanes, shares):
    rows = asked_rows(s, asked_blocks(x_first, x_second, y_first, y_second))
    pick, cx, cy = [sides_first(block) for block in rows]
    weights = weights_of(cx, cy)
    found = answer(table, pick, weights, ((0, 1), (2, 3), (4, 5)))
    for d, value in found.items():
        values[d] = value
    element = pick.astype(jnp.int32)
    lanes[...] = element // 16 + jnp.where(element % 16 == 15, 64, 0)
    for a in range(4):
        share = jnp.where(element % 16 == 15, weights[4 * a + 3], 0.0)
        shares[a] = jnp.where(element % 16 == 0, weights[4 * a], share)


def late_body(values, lanes, shares, y_first, y_second, scale, far, near):
    halo = halo_of(*from_swaps("fy", y_first[...], y_second[...])) * scale[0:1, :]
    for d in range(6):
        index = jnp.broadcast_to(lanes[d : d + 1, :], (F, 128))
        value = values[d]
        for a in range(4):
            value = value + pick_lanes(halo, index + 16 * a) * shares[a, d : d + 1, :]
        (far if d < 3 else near)[d % 3 * F : (d % 3 + 1) * F, :] = value


def own_body(begin, table, picks, factors, result):
    def block(i, carry):
        at = 2 * (begin + i)
        hot = one_hot([picks[0, pl.ds(at + h, 1), :] for h in range(2)], E)
        products = jnp.dot(
            table[...], jnp.concatenate([hot, hot], axis=0), preferred_element_type=F32
        )
        weights = [
            jnp.concatenate([factors[n, pl.ds(at + h, 1), :] for h in range(2)], axis=1)
            for n in range(NODES)
        ]
        result[:, pl.ds(pl.multiple_of(i * E, E), E)] = combine(products, weights)
        return carry

    count = result.shape[1] // E
    lax.fori_loop(0, count, block, 0, unroll=5 if count == 10 else 3 if count == 9 else count)


def stacked(blocks):
    return jnp.concatenate([jnp.concatenate(halves(block), axis=1) for block in blocks], axis=0)


def three(ref):
    return [ref[k * F : (k + 1) * F, :] for k in range(3)]


def middles(y_first, y_second):
    return list(from_swaps("fy", y_first[F : 2 * F, :], y_second[F : 2 * F, :]))


def arrived(x_first, x_second, y_first, y_second):
    even = lax.axis_index("fx") % 2 == 0
    pairs = list(zip(three(x_first), three(x_second)))
    low = [jnp.where(even, far, near) for far, near in pairs]
    high = [jnp.where(even, near, far) for far, near in pairs]
    return stacked(low + middles(y_first, y_second) + high)


def placed(answers, slots, masks):
    hot = one_hot(slots, CAP)
    products = jnp.dot(answers, jnp.concatenate([hot, hot], axis=0), preferred_element_type=F32)
    return combine(products, masks)


def masks_of(kind, bases):
    return [jnp.where(jnp.abs(kind - base) < 0.5, 1.0, 0.0) for base in bases]


def kinds(even, near):
    start = jnp.where(even == near, 5.0, 0.0)
    return [start + k for k in range(3)]


def face_slots(face_picks):
    return [face_picks[0:1, h * 128 : (h + 1) * 128] for h in range(2)]


def own_faces_body(table, face_picks, result):
    hot = one_hot([face_picks[2:3, h * 128 : (h + 1) * 128] for h in range(2)], E)
    products = jnp.dot(table[...], jnp.concatenate([hot, hot], axis=0), preferred_element_type=F32)
    result[...] = combine(products, weights_of(face_picks[3:4, :], face_picks[4:5, :]))


def face_near_body(
    own, near, y_first, y_second, face_picks, mass_faces, partial, message
):
    even = lax.axis_index("fx") % 2 == 0
    masks = masks_of(face_picks[1:2, :], kinds(even, True) + [3.0, 4.0])
    answers = stacked(three(near) + middles(y_first, y_second))
    moved = own[...] + placed(answers, face_slots(face_picks), masks)
    moved = moved * mass_faces[0:1, :]
    partial[...] = moved
    message[0:F, :] = moved[:, 0:128]
    message[F : F + 8, :] = face_picks[:, 0:128]
    message[F + 2 : F + 3, :] = mass_faces[0:1, 0:128]


def face_far_body(partial, far, faces_in, sent, face_picks, mass_faces, along_x, along_y, other):
    even = lax.axis_index("fx") % 2 == 0
    masks = masks_of(face_picks[1:2, :], kinds(even, False))
    moved = placed(stacked(three(far)), face_slots(face_picks), masks) * mass_faces[0:1, :]
    result = partial[...] + moved
    along_x[...] = result[:, 0:128]
    along_y[...] = result[:, 128:256]
    slot, kind, weight = [faces_in[F + q : F + q + 1, :] for q in range(3)]
    moved = placed(stacked(three(sent)), [slot], masks_of(kind, kinds(even, True)))
    other[...] = faces_in[0:F, :] + moved * weight


def place_body(
    s, own_a, own_b, own_c, x_first, x_second, y_first, y_second, picks, factors, mass, result
):
    answers = arrived(x_first, x_second, y_first, y_second)
    for n in range(NODES):
        tiles = [slice(2 * n + h, 2 * n + h + 1) for h in range(2)]
        masks = [
            jnp.concatenate([factors[NODES + d, t, :] for t in tiles], axis=1) for d in range(8)
        ]
        moved = placed(answers, [picks[1, t, :] for t in tiles], masks)
        for ref, (begin, end) in zip((own_a, own_b, own_c), PIECES[s]):
            if begin <= n < end:
                own = ref[:, (n - begin) * E : (n - begin + 1) * E]
        result[:, n * E : (n + 1) * E] = (own + moved) * mass[n : n + 1, :]


def rim_body(along_y, x_first, x_second, first, second):
    low, high = from_swaps("fx", x_first[...], x_second[...])
    result = summed_faces(along_y[...], low, high)
    first[...] = result
    second[...] = result


def scale_body(mass, x_first, x_second, y_first, y_second, inverse, on_faces):
    x_low, x_high = from_swaps("fx", x_first[8:16, :], x_second[8:16, :])
    y_low, y_high = from_swaps("fy", y_first[8:16, :], y_second[8:16, :])
    low, high, halo = [
        eight(row[6:7]) for row in (x_low, x_high, halo_of(y_low, y_high))
    ]
    nodes = [eight(mass[n : n + 1, :]) for n in range(NODES)]
    nodes = summed_nodes(nodes, low, high)
    nodes = [1.0 / with_halo(n, node, halo) for n, node in enumerate(nodes)]
    for n in range(NODES):
        inverse[n : n + 1, :] = nodes[n][0:1]
    on_faces[...] = faces(lambda n, t: nodes[n][:, t * 128 : (t + 1) * 128])[1]


def sum_body(weighted, x_first, x_second, inverse, result, table=None):
    low, high = from_swaps("fx", x_first[...], x_second[...])
    nodes = summed_nodes([weighted[:, n * E : (n + 1) * E] for n in range(NODES)], low, high)
    for n in range(NODES):
        node = nodes[n] * inverse[n : n + 1, :]
        result[:, n * E : (n + 1) * E] = node
        if table is not None:
            high_part, low_part = halves(node)
            table[n * F : (n + 1) * F, 0:E] = high_part
            table[n * F : (n + 1) * F, E : 2 * E] = low_part


def finish_body(summed, y_first, y_second, scale, table):
    halo = halo_of(*from_swaps("fy", y_first[...], y_second[...])) * scale[0:1, :]
    for n in range(NODES):
        node = with_halo(n, summed[:, n * E : (n + 1) * E], halo)
        high, low = halves(node)
        table[n * F : (n + 1) * F, 0:E] = high
        table[n * F : (n + 1) * F, E : 2 * E] = low


def last_body(summed, y_first, y_second, scale, result, block, sems):
    halo = halo_of(*from_swaps("fy", y_first[...], y_second[...])) * scale[0:1, :]
    copies = []
    for i in range(F // 8):
        rows = slice(i * 8, (i + 1) * 8)
        nodes = [
            with_halo(n, summed[rows, n * E : (n + 1) * E], halo[rows]) for n in range(NODES)
        ]
        block[rows] = jnp.swapaxes(jnp.stack(nodes), 0, 1)
        copy = pltpu.make_async_copy(block.at[rows], result.at[rows], sems.at[i])
        copy.start()
        copies.append(copy)
    for copy in copies:
        copy.wait()


def per_device(tracers, node_mass, point_order, offsets, source, coords):
    ask = shape((24, 128))
    answers = shape((3 * F, 128))
    face = shape((F, 128))
    table_shape = shape((NODES * F, 2 * E), BF16)
    lists = [
        pltpu.SMEM(offsets.shape, jnp.int32),
        pltpu.VMEM(source.shape, jnp.int32),
        pltpu.VMEM(coords.shape, jnp.int32),
    ]
    first, second, mid, mass_faces = call(
        asks_body,
        [ask, ask, ask, shape((8, 256))],
        "asks",
        hbm=(0, 1, 2, 3),
        count=4,
        scratch=lists
        + [
            pltpu.VMEM(node_mass.shape, F32),
            pltpu.VMEM((8, POINTS), F32),
            pltpu.VMEM((72, 128), F32),
            pltpu.SemaphoreType.DMA((4,)),
        ],
    )(*[in_hbm(a) for a in (offsets, source, coords, node_mass)])
    asked = swap("fx", first, second)
    requests = [shape((2, TILES, 128)), shape((NODES + 8, TILES, 128)), shape((8, 256))]
    *now, later, later_starts = call(
        order_body,
        requests + [shape((8, POINTS), jnp.int32), shape((8, 128), jnp.int32)],
        "order",
        hbm=(0, 1, 2, 3),
        count=4,
        scratch=[pltpu.VMEM(a.shape, jnp.int32) for a in (offsets, point_order, source, coords)]
        + [pltpu.SemaphoreType.DMA((4,))],
    )(*[in_hbm(a) for a in (offsets, point_order, source, coords)])
    ordered_lists = [now]

    def interpolate(s, piece, after=0):
        begin, end = PIECES[s][piece]
        return call(
            lambda *refs: own_body(begin, *refs),
            shape((F, (end - begin) * E)),
            "own",
            count=3,
            after=after,
        )

    asked += swap(
        "fy",
        *call(column_body, [ask] * 2, "column", count=4)(*asked, mid, mass_faces),
    )
    table = call(
        table_body,
        table_shape,
        "table",
        hbm=(0,),
        count=1,
        scratch=[pltpu.VMEM(tracers.shape, F32), pltpu.SemaphoreType.DMA((1,))],
    )(in_hbm(tracers))
    far, near = call(reply_y_body, [answers] * 2, "reply_y", count=5, after=1)(
        table, *asked, now[2]
    )
    answers_y = swap("fy", far, near)
    inverse, scale = call(scale_body, [shape((NODES, E)), shape((8, 128))], "scale", count=5)(
        node_mass, *asked
    )
    for s in range(SUBSTEPS):
        picks, factors, face_picks = ordered_lists[s]
        if s == 1:
            table = call(finish_body, table_shape, "finish", count=4)(summed, *edges_y, scale)
        own = call(
            lambda *refs, s=s: reply_x_body(s, *refs), shape((2 * F, 128)), "reply_x", count=5
        )(table, *asked)
        own_faces = call(own_faces_body, shape((F, 256)), "own_faces", count=2)(table, face_picks)
        own_a = interpolate(s, 0)(table, picks, factors)
        near_sent, far_sent = call(row_body, [answers] * 2, "row", count=3, after=3)(
            *answers_y, own, own_a, scale, own_faces
        )
        near = swap_near("fx", near_sent)
        far = swap_far("fx", far_sent)
        partial, message = call(
            face_near_body, [shape((F, 256)), shape((F + 8, 128))], "faces_near", count=6
        )(own_faces, near, *answers_y, face_picks, mass_faces)
        faces_in = swap_far("fx", message)
        own_b = interpolate(s, 1, after=1)(table, picks, factors, partial)
        if s == 0:
            ordered_lists.append(
                call(later_body, requests, "order", count=2, after=1)(
                    later, later_starts, partial
                )
            )
        along_x, along_y, other = call(
            face_far_body, [face] * 3, "faces_far", count=6, after=2
        )(partial, far, faces_in, far_sent, face_picks, mass_faces, own_b, ordered_lists[1][2])
        edges_x = (other, swap_near("fx", along_x))
        first, second = call(rim_body, [face] * 2, "rim", count=3)(along_y, *edges_x)
        edges_y = swap("fy", first, second)
        own_c = interpolate(s, 2, after=1)(table, picks, factors, second)
        weighted = call(
            lambda *refs, s=s: place_body(s, *refs), shape((F, POINTS)), "place", count=10
        )(
            own_a, own_b, own_c, far, near, *answers_y, picks, factors, node_mass
        )
        if s == 0:
            summed, early_table = call(
                sum_body, [shape((F, POINTS)), table_shape], "sum", count=4
            )(weighted, *edges_x, inverse)
            early = call(
                lambda *refs: early_body(1, *refs),
                [shape((8, F, 128)), shape((8, 128), jnp.int32), shape((4, 8, 128))],
                "early",
                count=5,
            )(early_table, *asked)
            far, near = call(late_body, [answers] * 2, "late", count=6)(
                *early, *edges_y, scale
            )
            answers_y = swap("fy", far, near)
        else:
            summed = call(sum_body, shape((F, POINTS)), "sum", count=4)(
                weighted, *edges_x, inverse
            )
            result = pl.pallas_call(
                last_body,
                out_shape=shape((F, NODES, E)),
                in_specs=[pl.BlockSpec(memory_space=pltpu.VMEM)] * 4,
                out_specs=pl.BlockSpec(memory_space=pltpu.HBM),
                scratch_shapes=[
                    pltpu.VMEM((F, NODES, E), F32),
                    pltpu.SemaphoreType.DMA((F // 8,)),
                ],
                name="last",
                compiler_params=pltpu.CompilerParams(vmem_limit_bytes=VMEM_LIMIT),
            )(summed, *edges_y, scale)
    return result


def solution(mesh):
    return jax.shard_map(
        per_device,
        mesh=mesh,
        in_specs=(
            P(None, None, ("fx", "fy")),
            P(None, ("fx", "fy")),
            P(None, ("fx", "fy"), None),
            P(None, ("fx", "fy"), None),
            P(None, ("fx", "fy")),
            P(None, None, ("fx", "fy")),
        ),
        out_specs=P(None, None, ("fx", "fy")),
        check_vma=False,
    )
```

```python
import jax
import jax.numpy as jnp
from jax import lax
from jax.experimental import pallas as pl
from jax.experimental.pallas import tpu as pltpu
from jax.sharding import PartitionSpec as P

TX = 16
CAP = 128
QGRID = 1024
SUBSTEPS = 2
F = 64
E = 256
NODES = 16
POINTS = 4096
TILES = POINTS // 128
PIECES = (((0, 10), (10, 16)), ((0, 9), (9, 16)))
GLL_NODES = (-1.0, -0.4472135954999579, 0.4472135954999579, 1.0)
REMOTE = (0, 1, 2, 3, 5, 6, 7, 8)
BF16 = jnp.bfloat16
F32 = jnp.float32
VMEM_LIMIT = 40 * 2**20


def call(body, out_shape, name, hbm=(), count=0, after=0, scratch=()):
    specs = [
        pl.BlockSpec(memory_space=pltpu.HBM if i in hbm else pltpu.VMEM) for i in range(count)
    ] + [pl.BlockSpec(memory_space=pl.ANY)] * after

    def kernel(*refs):
        body(*refs[:count], *refs[count + after :])

    return pl.pallas_call(
        kernel,
        out_shape=out_shape,
        in_specs=specs,
        scratch_shapes=scratch,
        name=name,
        compiler_params=pltpu.CompilerParams(vmem_limit_bytes=VMEM_LIMIT),
    )


def in_hbm(array):
    return pltpu.with_memory_space_constraint(array, pltpu.HBM)


def shape(dims, dtype=F32):
    return jax.ShapeDtypeStruct(dims, dtype)


def swap_far(axis, block):
    size = lax.axis_size(axis)
    pairs = [(i, (((i + size - 1) % size ^ 1) + 1) % size) for i in range(size)]
    return lax.ppermute(block, axis, pairs)


def swap_near(axis, block):
    return lax.ppermute(block, axis, [(i, i ^ 1) for i in range(lax.axis_size(axis))])


def swap(axis, far, near):
    return swap_far(axis, far), swap_near(axis, near)


def to_swaps(axis, low, high):
    even = lax.axis_index(axis) % 2 == 0
    return jnp.where(even, low, high), jnp.where(even, high, low)


def from_swaps(axis, first, second):
    even = lax.axis_index(axis) % 2 == 0
    return jnp.where(even, first, second), jnp.where(even, second, first)


def lagrange(step):
    x = step * (2.0 / QGRID) - 1.0
    rows = []
    for a in range(4):
        factor = None
        for b in range(4):
            if b != a:
                term = (x - GLL_NODES[b]) * (1.0 / (GLL_NODES[a] - GLL_NODES[b]))
                factor = term if factor is None else factor * term
        rows.append(factor)
    return rows


def halves(block):
    high = block.astype(BF16)
    return high, (block - high.astype(F32)).astype(BF16)


def one_hot(index_rows, depth):
    rows = lax.broadcasted_iota(jnp.int32, (depth, 128), 0).astype(F32).astype(BF16)
    parts = [jnp.where(rows == r.astype(BF16), BF16(1), BF16(0)) for r in index_rows]
    return jnp.concatenate(parts, axis=1)


def lane_index(rows):
    return lax.broadcasted_iota(jnp.int32, (rows, 128), 1)


def eight(row):
    return jnp.broadcast_to(row, (8, row.shape[1]))


def pick_lanes(block, index):
    return jnp.take_along_axis(block, index, axis=1, mode="promise_in_bounds")


def faces(tile):
    rows = tile(0, 0).shape[0]
    lane = lane_index(rows)
    along_x = jnp.zeros((rows, 128), F32)
    for b in range(4):
        along_x = jnp.where(lane // 16 == b, pltpu.roll(tile(b, 0), b * 16, 1), along_x)
        shifted = pltpu.roll(tile(12 + b, 1), (b * 16 + 80) % 128, 1)
        along_x = jnp.where(lane // 16 == b + 4, shifted, along_x)
    along_y = jnp.zeros((rows, 128), F32)
    index = (lane % 8) * 16
    for a in range(4):
        for t in range(2):
            here = ((lane % 64) // 16 == a) & ((lane % 16) // 8 == t)
            first = pick_lanes(tile(4 * a, t), index)
            last = pick_lanes(tile(4 * a + 3, t), index + 15)
            along_y = jnp.where(here, jnp.where(lane < 64, first, last), along_y)
    return along_x, along_y


def summed_faces(own, low, high):
    lane = lane_index(own.shape[0])
    place = lane % 64
    behind = pltpu.roll(own, 128 - 48 + 1, 1)
    ahead = pltpu.roll(own, 48 - 1, 1)
    behind = jnp.where(lane == 0, low[:, 64:65], jnp.where(lane == 64, low[:, 127:128], behind))
    ahead = jnp.where(lane == 63, high[:, 0:1], jnp.where(lane == 127, high[:, 63:64], ahead))
    return own + jnp.where(place < 16, behind, jnp.where(place >= 48, ahead, 0.0))


def summed_nodes(nodes, low, high):
    rows = nodes[0].shape[0]
    lane = lane_index(rows)
    wide = lax.broadcasted_iota(jnp.int32, (rows, E), 1)
    nodes = list(nodes)
    for b in range(4):
        first, last = nodes[b], nodes[12 + b]
        behind = pltpu.roll(last, 16, 1)
        ahead = pltpu.roll(first, E - 16, 1)
        from_low = pltpu.roll(low, (128 - 64 - 16 * b) % 128, 1)
        from_high = pltpu.roll(high, 112 - 16 * b, 1)
        behind = jnp.concatenate(
            [jnp.where(lane < 16, from_low, behind[:, :128]), behind[:, 128:]], axis=1
        )
        ahead = jnp.concatenate(
            [ahead[:, :128], jnp.where(lane >= 112, from_high, ahead[:, 128:])], axis=1
        )
        nodes[b] = first + behind
        nodes[12 + b] = last + ahead
    for a in range(4):
        first, last = nodes[4 * a], nodes[4 * a + 3]
        behind = jnp.where(wide % 16 == 0, 0.0, pltpu.roll(last, 1, 1))
        ahead = jnp.where(wide % 16 == 15, 0.0, pltpu.roll(first, E - 1, 1))
        nodes[4 * a] = first + behind
        nodes[4 * a + 3] = last + ahead
    return nodes


def halo_of(low, high):
    lane = lane_index(low.shape[0])
    return pltpu.roll(jnp.where(lane >= 64, low, high), 64, 1)


def with_halo(n, node, halo):
    if n % 4 not in (0, 3):
        return node
    rows = node.shape[0]
    lane = lane_index(rows)
    wide = lax.broadcasted_iota(jnp.int32, (rows, E), 1)
    start = 16 * (n // 4) + (64 if n % 4 == 3 else 0)
    spread = [pick_lanes(halo, start + 8 * t + lane // 16) for t in range(2)]
    at = 15 if n % 4 == 3 else 0
    return node + jnp.where(wide % 16 == at, jnp.concatenate(spread, axis=1), 0.0)


def fetch(pairs, sems):
    copies = [pltpu.make_async_copy(*pair, sems.at[i]) for i, pair in enumerate(pairs)]
    for copy in copies:
        copy.start()
    for copy in copies:
        copy.wait()


def asks_body(
    offsets_in, source_in, coords_in, mass_in, first, second, mid, mass_faces,
    offsets, source, coords, mass, rows, message, sems,
):
    fetch(
        [(offsets_in, offsets), (source_in, source), (coords_in, coords), (mass_in, mass)], sems
    )
    for s in range(SUBSTEPS):
        rows[3 * s : 3 * s + 1, :] = source[s : s + 1, :].astype(F32)
        rows[3 * s + 1 : 3 * s + 3, :] = coords[s].astype(F32)
    rows[6:8, :] = jnp.zeros((2, POINTS), F32)
    early = lax.broadcasted_iota(jnp.int32, (8, 128), 0) < 3
    for k in REMOTE:
        parts = []
        for s in range(SUBSTEPS):
            start = offsets[s, 0, k]
            tile = jnp.minimum(start // 128, TILES - 1)
            after = jnp.minimum(tile + 1, TILES - 1)
            wide = jnp.concatenate(
                [rows[:, pl.ds(pl.multiple_of(t * 128, 128), 128)] for t in (tile, after)], axis=1
            )
            parts.append(pltpu.roll(wide, 256 - (start - tile * 128), 1)[:, 0:128])
        message[k * 8 : (k + 1) * 8, :] = jnp.where(early, parts[0], parts[1])
    along_x, along_y = faces(lambda n, t: eight(mass[n : n + 1, t * 128 : (t + 1) * 128]))
    for k in (1, 7):
        message[k * 8 + 6 : k * 8 + 7, :] = along_x[0:1]
    mass_faces[:, 0:128] = along_x
    mass_faces[:, 128:256] = along_y
    message[32:40, :] = jnp.zeros((8, 128), F32)
    first[...], second[...] = to_swaps("fx", message[0:24, :], message[48:72, :])
    mid[...] = message[24:48, :]


def order_body(
    offsets_in, order_in, source_in, coords_in, picks, factors, face_picks, later, later_starts,
    offsets, order, source, coords, sems,
):
    fetch(
        [(offsets_in, offsets), (order_in, order), (source_in, source), (coords_in, coords)], sems
    )
    ordered(
        order[0], source[0:1], coords[0, 0:1], coords[0, 1:2], offsets[0], picks, factors, face_picks
    )
    later[0:1, :] = order[1]
    later[1:2, :] = source[1:2, :]
    later[2:4, :] = coords[1]
    later_starts[0:1, 0:10] = offsets[1]


def later_body(lists, starts, picks, factors, face_picks):
    ordered(
        lists[0:1], lists[1:2], lists[2:3], lists[3:4], starts[0:1], picks, factors, face_picks
    )


def ordered(nodes, sources, xs, ys, starts, picks, factors, face_picks):
    chunk = 1024
    total = None
    for c in range(POINTS // chunk):
        lanes = slice(c * chunk, (c + 1) * chunk)
        node = nodes[:, lanes]
        tile_of = (node // 128).astype(F32).astype(BF16)
        lane_of = (node % 128).astype(F32).astype(BF16)
        position = lax.broadcasted_iota(jnp.int32, (1, chunk), 1) + c * chunk
        run = jnp.zeros((1, chunk), jnp.int32)
        begin = jnp.broadcast_to(starts[:, 0:1], (1, chunk))
        for k in range(1, 9):
            start = jnp.broadcast_to(starts[:, k : k + 1], (1, chunk))
            passed = position >= start
            run = run + passed.astype(jnp.int32)
            begin = jnp.where(passed, start, begin)
        own = run == 4
        kind = jnp.where(own, 8, jnp.where(run > 4, run - 1, run))
        pick = jnp.where(own, sources[:, lanes], position - begin)
        cx = xs[:, lanes]
        cy = ys[:, lanes]
        values = [pick, cx // 8, cx % 8, cy // 8, cy % 8, kind]
        tiles = lax.broadcasted_iota(jnp.int32, (TILES, chunk), 0).astype(F32).astype(BF16)
        here = tiles == tile_of
        left = jnp.concatenate(
            [jnp.where(here, v.astype(F32).astype(BF16), BF16(0)) for v in values], axis=0
        )
        spots = lax.broadcasted_iota(jnp.int32, (128, chunk), 0).astype(F32).astype(BF16)
        right = jnp.where(spots == lane_of, BF16(1), BF16(0))
        part = lax.dot_general(left, right, (((1,), (1,)), ((), ())), preferred_element_type=F32)
        total = part if total is None else total + part
    pick, xh, xl, yh, yl, kind = [total[q * TILES : (q + 1) * TILES] for q in range(6)]
    own = kind > 7.5
    picks[0] = jnp.where(own, pick, -1.0)
    picks[1] = jnp.where(own, -1.0, pick)
    mask = jnp.where(own, 1.0, 0.0)
    along_x = [row * mask for row in lagrange(xh * 8.0 + xl)]
    along_y = lagrange(yh * 8.0 + yl)
    for n in range(NODES):
        factors[n] = along_x[n // 4] * along_y[n % 4]
    for d in range(8):
        factors[NODES + d] = jnp.where(jnp.abs(kind - d) < 0.5, 1.0, 0.0)
    for q, rows in enumerate((picks[1], kind, picks[0], xh * 8.0 + xl, yh * 8.0 + yl)):
        along = faces(lambda n, t: eight(rows[2 * n + t : 2 * n + t + 1]))
        face_picks[q : q + 1, :] = jnp.concatenate(along, axis=1)[0:1]


def table_body(tracers_in, table, tracers, sems):
    fetch([(tracers_in, tracers)], sems)
    for q in range(0, F, 16):
        block = jnp.swapaxes(tracers[q : q + 16], 0, 1)
        for n in range(NODES):
            high, low = halves(block[n])
            table[n * F + q : n * F + q + 16, 0:E] = high
            table[n * F + q : n * F + q + 16, E : 2 * E] = low


def column_body(x_first, x_second, mid, mass_faces, first, second, kept):
    low, high = from_swaps("fx", x_first[...], x_second[...])
    masses = summed_faces(mass_faces[:, 128:256], low[8:16], high[8:16])[6:7]
    rows = lax.broadcasted_iota(jnp.int32, (8, 128), 0)
    columns = []
    for k in (0, 2):
        block = slice(k * 8, (k + 1) * 8)
        center = jnp.where(rows == 6, masses, mid[block, :])
        columns.append(jnp.concatenate([high[block], center, low[block]], axis=0))
    first[...], second[...] = to_swaps("fy", *columns)
    kept[...] = first[...]


def row_body(y_first, y_second, own, near, far):
    low, high = from_swaps("fy", y_first[...], y_second[...])
    mine = own[...]
    ahead = jnp.concatenate([low[0:F], mine[0:F], high[0:F]], axis=0)
    behind = jnp.concatenate([low[2 * F :], mine[F:], high[2 * F :]], axis=0)
    far[...], near[...] = to_swaps("fx", behind, ahead)


def combine(products, weights):
    total = None
    for n, weight in enumerate(weights):
        term = products[n * F : (n + 1) * F] * weight
        total = term if total is None else total + term
    return total


def asked_blocks(x_first, x_second, y_first, y_second):
    x_low, x_high = from_swaps("fx", x_first[...], x_second[...])
    y_low, y_high = from_swaps("fy", y_first[...], y_second[...])
    by_direction = {(1, 0): x_low[8:16], (-1, 0): x_high[8:16]}
    for k in range(3):
        by_direction[(k - 1, 1)] = y_low[k * 8 : (k + 1) * 8]
        by_direction[(k - 1, -1)] = y_high[k * 8 : (k + 1) * 8]
    return [by_direction[(k // 3 - 1, k % 3 - 1)] for k in REMOTE]


def asked_rows(s, asked):
    return [
        jnp.concatenate([r[s * 3 + q : s * 3 + q + 1, :] for r in asked], axis=0) for q in range(3)
    ]


def weights_of(cx, cy):
    along_x = lagrange(cx)
    along_y = lagrange(cy)
    return [along_x[n // 4] * along_y[n % 4] for n in range(NODES)]


def answer(table, pick, weights, directions):
    values = {}
    for both in directions:
        hot = one_hot([pick[d : d + 1] for d in both], E)
        products = jnp.dot(
            table[...], jnp.concatenate([hot, hot], axis=0), preferred_element_type=F32
        )
        for h, d in enumerate(both):
            lanes = slice(h * 128, (h + 1) * 128)
            values[d] = combine(products[:, lanes], [w[d : d + 1] for w in weights])
    return values


BEHIND = (2, 4, 7)
AHEAD = (0, 3, 5)
SIDES = (1, 6)


def sides_first(rows):
    even = lax.axis_index("fy") % 2 == 0
    pairs = [(rows[b : b + 1], rows[a : a + 1]) for b, a in zip(BEHIND, AHEAD)]
    far = [jnp.where(even, behind, ahead) for behind, ahead in pairs]
    near = [jnp.where(even, ahead, behind) for behind, ahead in pairs]
    return jnp.concatenate(far + near + [rows[0:2]], axis=0)


def reply_y_body(table, x_first, x_second, y_first, y_second, far, near):
    rows = asked_rows(0, asked_blocks(x_first, x_second, y_first, y_second))
    pick, cx, cy = [sides_first(block) for block in rows]
    values = answer(table, pick, weights_of(cx, cy), ((0, 1), (2, 3), (4, 5)))
    for k in range(3):
        far[k * F : (k + 1) * F, :] = values[k]
        near[k * F : (k + 1) * F, :] = values[3 + k]


def reply_x_body(s, table, x_first, x_second, y_first, y_second, own):
    pick, cx, cy = asked_rows(s, asked_blocks(x_first, x_second, y_first, y_second))
    values = answer(table, pick, weights_of(cx, cy), (SIDES,))
    for k, d in enumerate(SIDES):
        own[k * F : (k + 1) * F, :] = values[d]


def early_body(s, table, x_first, x_second, y_first, y_second, values, lanes, shares):
    rows = asked_rows(s, asked_blocks(x_first, x_second, y_first, y_second))
    pick, cx, cy = [sides_first(block) for block in rows]
    weights = weights_of(cx, cy)
    found = answer(table, pick, weights, ((0, 1), (2, 3), (4, 5)))
    for d, value in found.items():
        values[d] = value
    element = pick.astype(jnp.int32)
    lanes[...] = element // 16 + jnp.where(element % 16 == 15, 64, 0)
    for a in range(4):
        share = jnp.where(element % 16 == 15, weights[4 * a + 3], 0.0)
        shares[a] = jnp.where(element % 16 == 0, weights[4 * a], share)


def shared(values, lanes, shares, halo, rows):
    for d in rows:
        index = jnp.broadcast_to(lanes[d : d + 1, :], (F, 128))
        value = values[d]
        for a in range(4):
            value = value + pick_lanes(halo, index + 16 * a) * shares[a, d : d + 1, :]
        yield value


def late_far_body(values, lanes, shares, near, scale, message):
    even = lax.axis_index("fy") % 2 == 0
    block = pltpu.roll(near[...], 64, 1) * scale[0:1, :]
    lane = lane_index(F)
    halo = jnp.where(jnp.where(even, lane - 64, 63 - lane) >= 0, block, 0.0)
    for k, value in enumerate(shared(values, lanes, shares, halo, range(3))):
        message[k * F : (k + 1) * F, :] = value


def late_near_body(values, lanes, shares, far, near, scale, message):
    halo = halo_of(*from_swaps("fy", far[...], near[...])) * scale[0:1, :]
    for k, value in enumerate(shared(values, lanes, shares, halo, range(3, 6))):
        message[k * F : (k + 1) * F, :] = value


def fix_body(far, asked, rims, scale, result):
    even = lax.axis_index("fy") % 2 == 0
    pick, cx, cy = [
        jnp.concatenate([asked[k * 8 + 3 + q : k * 8 + 4 + q, :] for k in range(3)], axis=0)
        for q in range(3)
    ]
    weights = weights_of(cx, cy)
    element = pick.astype(jnp.int32)
    on_face = element % 16 == jnp.where(even, 15, 0)
    lanes = element // 16 + jnp.where(even, 0, 64)
    own = rims[...] * scale[0:1, :]
    for k in range(3):
        index = jnp.broadcast_to(lanes[k : k + 1], (F, 128))
        value = far[k * F : (k + 1) * F, :]
        for a in range(4):
            weight = jnp.where(even, weights[4 * a + 3], weights[4 * a])
            weight = jnp.where(on_face, weight, 0.0)
            value = value + pick_lanes(own, index + 16 * a) * weight[k : k + 1]
        result[k * F : (k + 1) * F, :] = value


def own_body(begin, table, picks, factors, result):
    def block(i, carry):
        at = 2 * (begin + i)
        hot = one_hot([picks[0, pl.ds(at + h, 1), :] for h in range(2)], E)
        products = jnp.dot(
            table[...], jnp.concatenate([hot, hot], axis=0), preferred_element_type=F32
        )
        weights = [
            jnp.concatenate([factors[n, pl.ds(at + h, 1), :] for h in range(2)], axis=1)
            for n in range(NODES)
        ]
        result[:, pl.ds(pl.multiple_of(i * E, E), E)] = combine(products, weights)
        return carry

    count = result.shape[1] // E
    lax.fori_loop(0, count, block, 0, unroll=5 if count == 10 else 3 if count in (6, 9) else count)


def stacked(blocks):
    return jnp.concatenate([jnp.concatenate(halves(block), axis=1) for block in blocks], axis=0)


def three(ref):
    return [ref[k * F : (k + 1) * F, :] for k in range(3)]


def middles(y_first, y_second):
    return list(from_swaps("fy", y_first[F : 2 * F, :], y_second[F : 2 * F, :]))


def arrived(x_first, x_second, y_first, y_second):
    even = lax.axis_index("fx") % 2 == 0
    pairs = list(zip(three(x_first), three(x_second)))
    low = [jnp.where(even, far, near) for far, near in pairs]
    high = [jnp.where(even, near, far) for far, near in pairs]
    return stacked(low + middles(y_first, y_second) + high)


def placed(answers, slots, masks):
    hot = one_hot(slots, CAP)
    products = jnp.dot(answers, jnp.concatenate([hot, hot], axis=0), preferred_element_type=F32)
    return combine(products, masks)


def masks_of(kind, bases):
    return [jnp.where(jnp.abs(kind - base) < 0.5, 1.0, 0.0) for base in bases]


def kinds(even, near):
    start = jnp.where(even == near, 5.0, 0.0)
    return [start + k for k in range(3)]


def face_slots(face_picks):
    return [face_picks[0:1, h * 128 : (h + 1) * 128] for h in range(2)]


def own_faces_body(table, face_picks, result):
    hot = one_hot([face_picks[2:3, h * 128 : (h + 1) * 128] for h in range(2)], E)
    products = jnp.dot(table[...], jnp.concatenate([hot, hot], axis=0), preferred_element_type=F32)
    result[...] = combine(products, weights_of(face_picks[3:4, :], face_picks[4:5, :]))


def face_near_body(
    own, near, y_first, y_second, face_picks, mass_faces, partial, message
):
    even = lax.axis_index("fx") % 2 == 0
    masks = masks_of(face_picks[1:2, :], kinds(even, True) + [3.0, 4.0])
    answers = stacked(three(near) + middles(y_first, y_second))
    moved = own[...] + placed(answers, face_slots(face_picks), masks)
    moved = moved * mass_faces[0:1, :]
    partial[...] = moved
    message[0:F, :] = moved[:, 0:128]
    message[F : F + 8, :] = face_picks[:, 0:128]
    message[F + 2 : F + 3, :] = mass_faces[0:1, 0:128]


def face_far_body(partial, far, faces_in, sent, face_picks, mass_faces, along_x, along_y, other):
    even = lax.axis_index("fx") % 2 == 0
    masks = masks_of(face_picks[1:2, :], kinds(even, False))
    moved = placed(stacked(three(far)), face_slots(face_picks), masks) * mass_faces[0:1, :]
    result = partial[...] + moved
    along_x[...] = result[:, 0:128]
    along_y[...] = result[:, 128:256]
    slot, kind, weight = [faces_in[F + q : F + q + 1, :] for q in range(3)]
    moved = placed(stacked(three(sent)), [slot], masks_of(kind, kinds(even, True)))
    other[...] = faces_in[0:F, :] + moved * weight


def place_body(
    s, own_a, own_b, x_first, x_second, y_first, y_second, picks, factors, mass, result
):
    answers = arrived(x_first, x_second, y_first, y_second)
    for n in range(NODES):
        tiles = [slice(2 * n + h, 2 * n + h + 1) for h in range(2)]
        masks = [
            jnp.concatenate([factors[NODES + d, t, :] for t in tiles], axis=1) for d in range(8)
        ]
        moved = placed(answers, [picks[1, t, :] for t in tiles], masks)
        for ref, (begin, end) in zip((own_a, own_b), PIECES[s]):
            if begin <= n < end:
                own = ref[:, (n - begin) * E : (n - begin + 1) * E]
        result[:, n * E : (n + 1) * E] = (own + moved) * mass[n : n + 1, :]


def rim_body(along_y, x_first, x_second, first, second, kept):
    low, high = from_swaps("fx", x_first[...], x_second[...])
    result = summed_faces(along_y[...], low, high)
    first[...] = result
    second[...] = result
    kept[...] = result


def scale_body(mass, x_first, x_second, y_first, y_second, inverse, on_faces):
    x_low, x_high = from_swaps("fx", x_first[8:16, :], x_second[8:16, :])
    y_low, y_high = from_swaps("fy", y_first[8:16, :], y_second[8:16, :])
    low, high, halo = [
        eight(row[6:7]) for row in (x_low, x_high, halo_of(y_low, y_high))
    ]
    nodes = [eight(mass[n : n + 1, :]) for n in range(NODES)]
    nodes = summed_nodes(nodes, low, high)
    nodes = [1.0 / with_halo(n, node, halo) for n, node in enumerate(nodes)]
    for n in range(NODES):
        inverse[n : n + 1, :] = nodes[n][0:1]
    on_faces[...] = faces(lambda n, t: nodes[n][:, t * 128 : (t + 1) * 128])[1]


def sum_body(weighted, x_first, x_second, inverse, result, table=None):
    low, high = from_swaps("fx", x_first[...], x_second[...])
    nodes = summed_nodes([weighted[:, n * E : (n + 1) * E] for n in range(NODES)], low, high)
    for n in range(NODES):
        node = nodes[n] * inverse[n : n + 1, :]
        result[:, n * E : (n + 1) * E] = node
        if table is not None:
            high_part, low_part = halves(node)
            table[n * F : (n + 1) * F, 0:E] = high_part
            table[n * F : (n + 1) * F, E : 2 * E] = low_part


def finish_body(summed, y_first, y_second, scale, table):
    halo = halo_of(*from_swaps("fy", y_first[...], y_second[...])) * scale[0:1, :]
    for n in range(NODES):
        node = with_halo(n, summed[:, n * E : (n + 1) * E], halo)
        high, low = halves(node)
        table[n * F : (n + 1) * F, 0:E] = high
        table[n * F : (n + 1) * F, E : 2 * E] = low


def last_body(summed, y_first, y_second, scale, result, block, sems):
    halo = halo_of(*from_swaps("fy", y_first[...], y_second[...])) * scale[0:1, :]
    copies = []
    for i in range(F // 8):
        rows = slice(i * 8, (i + 1) * 8)
        nodes = [
            with_halo(n, summed[rows, n * E : (n + 1) * E], halo[rows]) for n in range(NODES)
        ]
        block[rows] = jnp.swapaxes(jnp.stack(nodes), 0, 1)
        copy = pltpu.make_async_copy(block.at[rows], result.at[rows], sems.at[i])
        copy.start()
        copies.append(copy)
    for copy in copies:
        copy.wait()


def per_device(tracers, node_mass, point_order, offsets, source, coords):
    ask = shape((24, 128))
    answers = shape((3 * F, 128))
    face = shape((F, 128))
    table_shape = shape((NODES * F, 2 * E), BF16)
    lists = [
        pltpu.SMEM(offsets.shape, jnp.int32),
        pltpu.VMEM(source.shape, jnp.int32),
        pltpu.VMEM(coords.shape, jnp.int32),
    ]
    first, second, mid, mass_faces = call(
        asks_body,
        [ask, ask, ask, shape((8, 256))],
        "asks",
        hbm=(0, 1, 2, 3),
        count=4,
        scratch=lists
        + [
            pltpu.VMEM(node_mass.shape, F32),
            pltpu.VMEM((8, POINTS), F32),
            pltpu.VMEM((72, 128), F32),
            pltpu.SemaphoreType.DMA((4,)),
        ],
    )(*[in_hbm(a) for a in (offsets, source, coords, node_mass)])
    asked = swap("fx", first, second)
    requests = [shape((2, TILES, 128)), shape((NODES + 8, TILES, 128)), shape((8, 256))]
    *now, later, later_starts = call(
        order_body,
        requests + [shape((8, POINTS), jnp.int32), shape((8, 128), jnp.int32)],
        "order",
        hbm=(0, 1, 2, 3),
        count=4,
        scratch=[pltpu.VMEM(a.shape, jnp.int32) for a in (offsets, point_order, source, coords)]
        + [pltpu.SemaphoreType.DMA((4,))],
    )(*[in_hbm(a) for a in (offsets, point_order, source, coords)])
    ordered_lists = [now]

    def interpolate(s, piece, after=0):
        begin, end = PIECES[s][piece]
        return call(
            lambda *refs: own_body(begin, *refs),
            shape((F, (end - begin) * E)),
            "own",
            count=3,
            after=after,
        )

    column_far, column_near, column_kept = call(column_body, [ask] * 3, "column", count=4)(
        *asked, mid, mass_faces
    )
    asked += swap("fy", column_far, column_near)
    table = call(
        table_body,
        table_shape,
        "table",
        hbm=(0,),
        count=1,
        scratch=[pltpu.VMEM(tracers.shape, F32), pltpu.SemaphoreType.DMA((1,))],
    )(in_hbm(tracers))
    far, near = call(reply_y_body, [answers] * 2, "reply_y", count=5, after=1)(
        table, *asked, now[2]
    )
    answers_y = swap("fy", far, near)
    inverse, scale = call(scale_body, [shape((NODES, E)), shape((8, 128))], "scale", count=5)(
        node_mass, *asked
    )
    for s in range(SUBSTEPS):
        picks, factors, face_picks = ordered_lists[s]
        if s == 1:
            table = call(finish_body, table_shape, "finish", count=4)(summed, *edges_y, scale)
        own = call(
            lambda *refs, s=s: reply_x_body(s, *refs), shape((2 * F, 128)), "reply_x", count=5
        )(table, *asked)
        own_faces = call(own_faces_body, shape((F, 256)), "own_faces", count=2)(table, face_picks)
        own_a = interpolate(s, 0)(table, picks, factors)
        near_sent, far_sent = call(row_body, [answers] * 2, "row", count=3, after=3)(
            *answers_y, own, own_a, scale, own_faces
        )
        near = swap_near("fx", near_sent)
        far = swap_far("fx", far_sent)
        partial, message = call(
            face_near_body, [shape((F, 256)), shape((F + 8, 128))], "faces_near", count=6
        )(own_faces, near, *answers_y, face_picks, mass_faces)
        faces_in = swap_far("fx", message)
        own_b = interpolate(s, 1, after=1)(table, picks, factors, partial)
        if s == 0:
            ordered_lists.append(
                call(later_body, requests, "order", count=2, after=1)(
                    later, later_starts, partial
                )
            )
        along_x, along_y, other = call(
            face_far_body, [face] * 3, "faces_far", count=6, after=2
        )(partial, far, faces_in, far_sent, face_picks, mass_faces, own_b, ordered_lists[1][2])
        edges_x = (other, swap_near("fx", along_x))
        weighted = call(
            lambda *refs, s=s: place_body(s, *refs),
            shape((F, POINTS)),
            "place",
            count=9,
            after=1,
        )(own_a, own_b, far, near, *answers_y, picks, factors, node_mass, other)
        rims_far, rims_near, rims_kept = call(rim_body, [face] * 3, "rim", count=3, after=1)(
            along_y, *edges_x, weighted
        )
        edges_y = swap("fy", rims_far, rims_near)
        if s == 0:
            summed, early_table = call(
                sum_body, [shape((F, POINTS)), table_shape], "sum", count=4
            )(weighted, *edges_x, inverse)
            early = call(
                lambda *refs: early_body(1, *refs),
                [shape((8, F, 128)), shape((8, 128), jnp.int32), shape((4, 8, 128))],
                "early",
                count=5,
            )(early_table, *asked)
            far = call(late_far_body, answers, "late_far", count=5)(*early, edges_y[1], scale)
            far = swap_far("fy", far)
            near = call(late_near_body, answers, "late_near", count=6)(*early, *edges_y, scale)
            near = swap_near("fy", near)
            far = call(fix_body, answers, "fix", count=4)(far, column_kept, rims_kept, scale)
            answers_y = (far, near)
        else:
            summed = call(sum_body, shape((F, POINTS)), "sum", count=4)(
                weighted, *edges_x, inverse
            )
            result = pl.pallas_call(
                last_body,
                out_shape=shape((F, NODES, E)),
                in_specs=[pl.BlockSpec(memory_space=pltpu.VMEM)] * 4,
                out_specs=pl.BlockSpec(memory_space=pltpu.HBM),
                scratch_shapes=[
                    pltpu.VMEM((F, NODES, E), F32),
                    pltpu.SemaphoreType.DMA((F // 8,)),
                ],
                name="last",
                compiler_params=pltpu.CompilerParams(vmem_limit_bytes=VMEM_LIMIT),
            )(summed, *edges_y, scale)
    return result


def solution(mesh):
    return jax.shard_map(
        per_device,
        mesh=mesh,
        in_specs=(
            P(None, None, ("fx", "fy")),
            P(None, ("fx", "fy")),
            P(None, ("fx", "fy"), None),
            P(None, ("fx", "fy"), None),
            P(None, ("fx", "fy")),
            P(None, None, ("fx", "fy")),
        ),
        out_specs=P(None, None, ("fx", "fy")),
        check_vma=False,
    )
```

```python
import jax
import jax.numpy as jnp
from jax import lax
from jax.experimental import pallas as pl
from jax.experimental.pallas import tpu as pltpu
from jax.sharding import PartitionSpec as P

TX = 16
CAP = 128
QGRID = 1024
SUBSTEPS = 2
F = 64
E = 256
NODES = 16
POINTS = 4096
TILES = POINTS // 128
PIECES = (((0, 10), (10, 16)), ((0, 7), (7, 16)))
GLL_NODES = (-1.0, -0.4472135954999579, 0.4472135954999579, 1.0)
REMOTE = (0, 1, 2, 3, 5, 6, 7, 8)
BF16 = jnp.bfloat16
F32 = jnp.float32
VMEM_LIMIT = 40 * 2**20


def call(body, out_shape, name, hbm=(), count=0, after=0, scratch=()):
    specs = [
        pl.BlockSpec(memory_space=pltpu.HBM if i in hbm else pltpu.VMEM) for i in range(count)
    ] + [pl.BlockSpec(memory_space=pl.ANY)] * after

    def kernel(*refs):
        body(*refs[:count], *refs[count + after :])

    return pl.pallas_call(
        kernel,
        out_shape=out_shape,
        in_specs=specs,
        scratch_shapes=scratch,
        name=name,
        compiler_params=pltpu.CompilerParams(vmem_limit_bytes=VMEM_LIMIT),
    )


def in_hbm(array):
    return pltpu.with_memory_space_constraint(array, pltpu.HBM)


def shape(dims, dtype=F32):
    return jax.ShapeDtypeStruct(dims, dtype)


def swap_far(axis, block):
    size = lax.axis_size(axis)
    pairs = [(i, (((i + size - 1) % size ^ 1) + 1) % size) for i in range(size)]
    return lax.ppermute(block, axis, pairs)


def swap_near(axis, block):
    return lax.ppermute(block, axis, [(i, i ^ 1) for i in range(lax.axis_size(axis))])


def swap(axis, far, near):
    return swap_far(axis, far), swap_near(axis, near)


def to_swaps(axis, low, high):
    even = lax.axis_index(axis) % 2 == 0
    return jnp.where(even, low, high), jnp.where(even, high, low)


def from_swaps(axis, first, second):
    even = lax.axis_index(axis) % 2 == 0
    return jnp.where(even, first, second), jnp.where(even, second, first)


def lagrange(step):
    x = step * (2.0 / QGRID) - 1.0
    rows = []
    for a in range(4):
        factor = None
        for b in range(4):
            if b != a:
                term = (x - GLL_NODES[b]) * (1.0 / (GLL_NODES[a] - GLL_NODES[b]))
                factor = term if factor is None else factor * term
        rows.append(factor)
    return rows


def halves(block):
    high = block.astype(BF16)
    return high, (block - high.astype(F32)).astype(BF16)


def one_hot(index_rows, depth):
    rows = lax.broadcasted_iota(jnp.int32, (depth, 128), 0).astype(F32).astype(BF16)
    parts = [jnp.where(rows == r.astype(BF16), BF16(1), BF16(0)) for r in index_rows]
    return jnp.concatenate(parts, axis=1)


def lane_index(rows):
    return lax.broadcasted_iota(jnp.int32, (rows, 128), 1)


def eight(row):
    return jnp.broadcast_to(row, (8, row.shape[1]))


def pick_lanes(block, index):
    return jnp.take_along_axis(block, index, axis=1, mode="promise_in_bounds")


def faces(tile):
    rows = tile(0, 0).shape[0]
    lane = lane_index(rows)
    along_x = jnp.zeros((rows, 128), F32)
    for b in range(4):
        along_x = jnp.where(lane // 16 == b, pltpu.roll(tile(b, 0), b * 16, 1), along_x)
        shifted = pltpu.roll(tile(12 + b, 1), (b * 16 + 80) % 128, 1)
        along_x = jnp.where(lane // 16 == b + 4, shifted, along_x)
    along_y = jnp.zeros((rows, 128), F32)
    index = (lane % 8) * 16
    for a in range(4):
        for t in range(2):
            here = ((lane % 64) // 16 == a) & ((lane % 16) // 8 == t)
            first = pick_lanes(tile(4 * a, t), index)
            last = pick_lanes(tile(4 * a + 3, t), index + 15)
            along_y = jnp.where(here, jnp.where(lane < 64, first, last), along_y)
    return along_x, along_y


def summed_faces(own, low, high):
    lane = lane_index(own.shape[0])
    place = lane % 64
    behind = pltpu.roll(own, 128 - 48 + 1, 1)
    ahead = pltpu.roll(own, 48 - 1, 1)
    behind = jnp.where(lane == 0, low[:, 64:65], jnp.where(lane == 64, low[:, 127:128], behind))
    ahead = jnp.where(lane == 63, high[:, 0:1], jnp.where(lane == 127, high[:, 63:64], ahead))
    return own + jnp.where(place < 16, behind, jnp.where(place >= 48, ahead, 0.0))


def summed_nodes(nodes, low, high):
    rows = nodes[0].shape[0]
    lane = lane_index(rows)
    wide = lax.broadcasted_iota(jnp.int32, (rows, E), 1)
    nodes = list(nodes)
    for b in range(4):
        first, last = nodes[b], nodes[12 + b]
        behind = pltpu.roll(last, 16, 1)
        ahead = pltpu.roll(first, E - 16, 1)
        from_low = pltpu.roll(low, (128 - 64 - 16 * b) % 128, 1)
        from_high = pltpu.roll(high, 112 - 16 * b, 1)
        behind = jnp.concatenate(
            [jnp.where(lane < 16, from_low, behind[:, :128]), behind[:, 128:]], axis=1
        )
        ahead = jnp.concatenate(
            [ahead[:, :128], jnp.where(lane >= 112, from_high, ahead[:, 128:])], axis=1
        )
        nodes[b] = first + behind
        nodes[12 + b] = last + ahead
    for a in range(4):
        first, last = nodes[4 * a], nodes[4 * a + 3]
        behind = jnp.where(wide % 16 == 0, 0.0, pltpu.roll(last, 1, 1))
        ahead = jnp.where(wide % 16 == 15, 0.0, pltpu.roll(first, E - 1, 1))
        nodes[4 * a] = first + behind
        nodes[4 * a + 3] = last + ahead
    return nodes


def halo_of(low, high):
    lane = lane_index(low.shape[0])
    return pltpu.roll(jnp.where(lane >= 64, low, high), 64, 1)


def with_halo(n, node, halo):
    if n % 4 not in (0, 3):
        return node
    rows = node.shape[0]
    lane = lane_index(rows)
    wide = lax.broadcasted_iota(jnp.int32, (rows, E), 1)
    start = 16 * (n // 4) + (64 if n % 4 == 3 else 0)
    spread = [pick_lanes(halo, start + 8 * t + lane // 16) for t in range(2)]
    at = 15 if n % 4 == 3 else 0
    return node + jnp.where(wide % 16 == at, jnp.concatenate(spread, axis=1), 0.0)


def fetch(pairs, sems):
    copies = [pltpu.make_async_copy(*pair, sems.at[i]) for i, pair in enumerate(pairs)]
    for copy in copies:
        copy.start()
    for copy in copies:
        copy.wait()


def asks_body(
    offsets_in, source_in, coords_in, mass_in, first, second, mid, mass_faces,
    offsets, source, coords, mass, rows, message, sems,
):
    fetch(
        [(offsets_in, offsets), (source_in, source), (coords_in, coords), (mass_in, mass)], sems
    )
    for s in range(SUBSTEPS):
        rows[3 * s : 3 * s + 1, :] = source[s : s + 1, :].astype(F32)
        rows[3 * s + 1 : 3 * s + 3, :] = coords[s].astype(F32)
    rows[6:8, :] = jnp.zeros((2, POINTS), F32)
    early = lax.broadcasted_iota(jnp.int32, (8, 128), 0) < 3
    for k in REMOTE:
        parts = []
        for s in range(SUBSTEPS):
            start = offsets[s, 0, k]
            tile = jnp.minimum(start // 128, TILES - 1)
            after = jnp.minimum(tile + 1, TILES - 1)
            wide = jnp.concatenate(
                [rows[:, pl.ds(pl.multiple_of(t * 128, 128), 128)] for t in (tile, after)], axis=1
            )
            parts.append(pltpu.roll(wide, 256 - (start - tile * 128), 1)[:, 0:128])
        message[k * 8 : (k + 1) * 8, :] = jnp.where(early, parts[0], parts[1])
    along_x, along_y = faces(lambda n, t: eight(mass[n : n + 1, t * 128 : (t + 1) * 128]))
    for k in (1, 7):
        message[k * 8 + 6 : k * 8 + 7, :] = along_x[0:1]
    mass_faces[:, 0:128] = along_x
    mass_faces[:, 128:256] = along_y
    message[32:40, :] = jnp.zeros((8, 128), F32)
    first[...], second[...] = to_swaps("fx", message[0:24, :], message[48:72, :])
    mid[...] = message[24:48, :]


def order_body(
    offsets_in, order_in, source_in, coords_in, picks, factors, face_picks, later, later_starts,
    offsets, order, source, coords, sems,
):
    fetch(
        [(offsets_in, offsets), (order_in, order), (source_in, source), (coords_in, coords)], sems
    )
    ordered(
        order[0], source[0:1], coords[0, 0:1], coords[0, 1:2], offsets[0], picks, factors, face_picks
    )
    later[0:1, :] = order[1]
    later[1:2, :] = source[1:2, :]
    later[2:4, :] = coords[1]
    later_starts[0:1, 0:10] = offsets[1]


def later_body(lists, starts, picks, factors, face_picks):
    ordered(
        lists[0:1], lists[1:2], lists[2:3], lists[3:4], starts[0:1], picks, factors, face_picks
    )


def ordered(nodes, sources, xs, ys, starts, picks, factors, face_picks):
    chunk = 1024
    total = None
    for c in range(POINTS // chunk):
        lanes = slice(c * chunk, (c + 1) * chunk)
        node = nodes[:, lanes]
        tile_of = (node // 128).astype(F32).astype(BF16)
        lane_of = (node % 128).astype(F32).astype(BF16)
        position = lax.broadcasted_iota(jnp.int32, (1, chunk), 1) + c * chunk
        run = jnp.zeros((1, chunk), jnp.int32)
        begin = jnp.broadcast_to(starts[:, 0:1], (1, chunk))
        for k in range(1, 9):
            start = jnp.broadcast_to(starts[:, k : k + 1], (1, chunk))
            passed = position >= start
            run = run + passed.astype(jnp.int32)
            begin = jnp.where(passed, start, begin)
        own = run == 4
        kind = jnp.where(own, 8, jnp.where(run > 4, run - 1, run))
        pick = jnp.where(own, sources[:, lanes], position - begin)
        cx = xs[:, lanes]
        cy = ys[:, lanes]
        values = [pick, cx // 8, cx % 8, cy // 8, cy % 8, kind]
        tiles = lax.broadcasted_iota(jnp.int32, (TILES, chunk), 0).astype(F32).astype(BF16)
        here = tiles == tile_of
        left = jnp.concatenate(
            [jnp.where(here, v.astype(F32).astype(BF16), BF16(0)) for v in values], axis=0
        )
        spots = lax.broadcasted_iota(jnp.int32, (128, chunk), 0).astype(F32).astype(BF16)
        right = jnp.where(spots == lane_of, BF16(1), BF16(0))
        part = lax.dot_general(left, right, (((1,), (1,)), ((), ())), preferred_element_type=F32)
        total = part if total is None else total + part
    pick, xh, xl, yh, yl, kind = [total[q * TILES : (q + 1) * TILES] for q in range(6)]
    own = kind > 7.5
    picks[0] = jnp.where(own, pick, -1.0)
    picks[1] = jnp.where(own, -1.0, pick)
    mask = jnp.where(own, 1.0, 0.0)
    along_x = [row * mask for row in lagrange(xh * 8.0 + xl)]
    along_y = lagrange(yh * 8.0 + yl)
    for n in range(NODES):
        factors[n] = along_x[n // 4] * along_y[n % 4]
    for d in range(8):
        factors[NODES + d] = jnp.where(jnp.abs(kind - d) < 0.5, 1.0, 0.0)
    for q, rows in enumerate((picks[1], kind, picks[0], xh * 8.0 + xl, yh * 8.0 + yl)):
        along = faces(lambda n, t: eight(rows[2 * n + t : 2 * n + t + 1]))
        face_picks[q : q + 1, :] = jnp.concatenate(along, axis=1)[0:1]


def table_body(tracers_in, table, tracers, sems):
    fetch([(tracers_in, tracers)], sems)
    for q in range(0, F, 16):
        block = jnp.swapaxes(tracers[q : q + 16], 0, 1)
        for n in range(NODES):
            high, low = halves(block[n])
            table[n * F + q : n * F + q + 16, 0:E] = high
            table[n * F + q : n * F + q + 16, E : 2 * E] = low


def column_body(x_first, x_second, mid, mass_faces, first, second, kept):
    low, high = from_swaps("fx", x_first[...], x_second[...])
    masses = summed_faces(mass_faces[:, 128:256], low[8:16], high[8:16])[6:7]
    rows = lax.broadcasted_iota(jnp.int32, (8, 128), 0)
    columns = []
    for k in (0, 2):
        block = slice(k * 8, (k + 1) * 8)
        center = jnp.where(rows == 6, masses, mid[block, :])
        columns.append(jnp.concatenate([high[block], center, low[block]], axis=0))
    first[...], second[...] = to_swaps("fy", *columns)
    kept[...] = first[...]


def row_body(y_first, y_second, own, near, far):
    low, high = from_swaps("fy", y_first[...], y_second[...])
    mine = own[...]
    ahead = jnp.concatenate([low[0:F], mine[0:F], high[0:F]], axis=0)
    behind = jnp.concatenate([low[2 * F :], mine[F:], high[2 * F :]], axis=0)
    far[...], near[...] = to_swaps("fx", behind, ahead)


def combine(products, weights):
    total = None
    for n, weight in enumerate(weights):
        term = products[n * F : (n + 1) * F] * weight
        total = term if total is None else total + term
    return total


def asked_blocks(x_first, x_second, y_first, y_second):
    x_low, x_high = from_swaps("fx", x_first[...], x_second[...])
    y_low, y_high = from_swaps("fy", y_first[...], y_second[...])
    by_direction = {(1, 0): x_low[8:16], (-1, 0): x_high[8:16]}
    for k in range(3):
        by_direction[(k - 1, 1)] = y_low[k * 8 : (k + 1) * 8]
        by_direction[(k - 1, -1)] = y_high[k * 8 : (k + 1) * 8]
    return [by_direction[(k // 3 - 1, k % 3 - 1)] for k in REMOTE]


def asked_rows(s, asked):
    return [
        jnp.concatenate([r[s * 3 + q : s * 3 + q + 1, :] for r in asked], axis=0) for q in range(3)
    ]


def weights_of(cx, cy):
    along_x = lagrange(cx)
    along_y = lagrange(cy)
    return [along_x[n // 4] * along_y[n % 4] for n in range(NODES)]


def answer(table, pick, weights, directions):
    values = {}
    for both in directions:
        hot = one_hot([pick[d : d + 1] for d in both], E)
        products = jnp.dot(
            table[...], jnp.concatenate([hot, hot], axis=0), preferred_element_type=F32
        )
        for h, d in enumerate(both):
            lanes = slice(h * 128, (h + 1) * 128)
            values[d] = combine(products[:, lanes], [w[d : d + 1] for w in weights])
    return values


BEHIND = (2, 4, 7)
AHEAD = (0, 3, 5)
SIDES = (1, 6)


def side(rows, far):
    even = lax.axis_index("fy") % 2 == 0
    pairs = [(rows[b : b + 1], rows[a : a + 1]) for b, a in zip(BEHIND, AHEAD)]
    if far:
        return [jnp.where(even, behind, ahead) for behind, ahead in pairs]
    return [jnp.where(even, ahead, behind) for behind, ahead in pairs]


def sides_first(rows):
    return jnp.concatenate(side(rows, True) + side(rows, False) + [rows[0:2]], axis=0)


def reply_y_body(table, x_first, x_second, y_first, y_second, far, near):
    rows = asked_rows(0, asked_blocks(x_first, x_second, y_first, y_second))
    pick, cx, cy = [sides_first(block) for block in rows]
    values = answer(table, pick, weights_of(cx, cy), ((0, 1), (2, 3), (4, 5)))
    for k in range(3):
        far[k * F : (k + 1) * F, :] = values[k]
        near[k * F : (k + 1) * F, :] = values[3 + k]


def reply_x_body(s, table, x_first, x_second, y_first, y_second, own):
    pick, cx, cy = asked_rows(s, asked_blocks(x_first, x_second, y_first, y_second))
    values = answer(table, pick, weights_of(cx, cy), (SIDES,))
    for k, d in enumerate(SIDES):
        own[k * F : (k + 1) * F, :] = values[d]


def early_body(far, table, x_first, x_second, y_first, y_second, values, lanes, shares):
    rows = asked_rows(1, asked_blocks(x_first, x_second, y_first, y_second))
    pick, cx, cy = [jnp.concatenate(side(block, far) + [block[0:5]], axis=0) for block in rows]
    weights = weights_of(cx, cy)
    found = answer(table, pick, weights, ((0, 1), (2,)))
    for d, value in found.items():
        values[d] = value
    element = pick.astype(jnp.int32)
    lanes[...] = element // 16 + jnp.where(element % 16 == 15, 64, 0)
    for a in range(4):
        share = jnp.where(element % 16 == 15, weights[4 * a + 3], 0.0)
        shares[a] = jnp.where(element % 16 == 0, weights[4 * a], share)


def shared(values, lanes, shares, halo, message):
    for d in range(3):
        index = jnp.broadcast_to(lanes[d : d + 1, :], (F, 128))
        value = values[d]
        for a in range(4):
            value = value + pick_lanes(halo, index + 16 * a) * shares[a, d : d + 1, :]
        message[d * F : (d + 1) * F, :] = value


def late_far_body(values, lanes, shares, near, scale, message):
    even = lax.axis_index("fy") % 2 == 0
    block = pltpu.roll(near[...], 64, 1) * scale[0:1, :]
    lane = lane_index(F)
    halo = jnp.where(jnp.where(even, lane - 64, 63 - lane) >= 0, block, 0.0)
    shared(values, lanes, shares, halo, message)


def late_near_body(values, lanes, shares, far, near, scale, message):
    halo = halo_of(*from_swaps("fy", far[...], near[...])) * scale[0:1, :]
    shared(values, lanes, shares, halo, message)


def fix_body(far, asked, rims, scale, result):
    even = lax.axis_index("fy") % 2 == 0
    pick, cx, cy = [
        jnp.concatenate([asked[k * 8 + 3 + q : k * 8 + 4 + q, :] for k in range(3)], axis=0)
        for q in range(3)
    ]
    weights = weights_of(cx, cy)
    element = pick.astype(jnp.int32)
    on_face = element % 16 == jnp.where(even, 15, 0)
    lanes = element // 16 + jnp.where(even, 0, 64)
    own = rims[...] * scale[0:1, :]
    for k in range(3):
        index = jnp.broadcast_to(lanes[k : k + 1], (F, 128))
        value = far[k * F : (k + 1) * F, :]
        for a in range(4):
            weight = jnp.where(even, weights[4 * a + 3], weights[4 * a])
            weight = jnp.where(on_face, weight, 0.0)
            value = value + pick_lanes(own, index + 16 * a) * weight[k : k + 1]
        result[k * F : (k + 1) * F, :] = value


def own_body(begin, table, picks, factors, result):
    def block(i, carry):
        at = 2 * (begin + i)
        hot = one_hot([picks[0, pl.ds(at + h, 1), :] for h in range(2)], E)
        products = jnp.dot(
            table[...], jnp.concatenate([hot, hot], axis=0), preferred_element_type=F32
        )
        weights = [
            jnp.concatenate([factors[n, pl.ds(at + h, 1), :] for h in range(2)], axis=1)
            for n in range(NODES)
        ]
        result[:, pl.ds(pl.multiple_of(i * E, E), E)] = combine(products, weights)
        return carry

    count = result.shape[1] // E
    lax.fori_loop(0, count, block, 0, unroll=5 if count == 10 else 3 if count in (6, 9) else count)


def stacked(blocks):
    return jnp.concatenate([jnp.concatenate(halves(block), axis=1) for block in blocks], axis=0)


def three(ref):
    return [ref[k * F : (k + 1) * F, :] for k in range(3)]


def middles(y_first, y_second):
    return list(from_swaps("fy", y_first[F : 2 * F, :], y_second[F : 2 * F, :]))


def arrived(x_first, x_second, y_first, y_second):
    even = lax.axis_index("fx") % 2 == 0
    pairs = list(zip(three(x_first), three(x_second)))
    low = [jnp.where(even, far, near) for far, near in pairs]
    high = [jnp.where(even, near, far) for far, near in pairs]
    return stacked(low + middles(y_first, y_second) + high)


def placed(answers, slots, masks):
    hot = one_hot(slots, CAP)
    products = jnp.dot(answers, jnp.concatenate([hot, hot], axis=0), preferred_element_type=F32)
    return combine(products, masks)


def masks_of(kind, bases):
    return [jnp.where(jnp.abs(kind - base) < 0.5, 1.0, 0.0) for base in bases]


def kinds(even, near):
    start = jnp.where(even == near, 5.0, 0.0)
    return [start + k for k in range(3)]


def face_slots(face_picks):
    return [face_picks[0:1, h * 128 : (h + 1) * 128] for h in range(2)]


def own_faces_body(table, face_picks, result):
    hot = one_hot([face_picks[2:3, h * 128 : (h + 1) * 128] for h in range(2)], E)
    products = jnp.dot(table[...], jnp.concatenate([hot, hot], axis=0), preferred_element_type=F32)
    result[...] = combine(products, weights_of(face_picks[3:4, :], face_picks[4:5, :]))


def face_near_body(
    own, near, y_first, y_second, face_picks, mass_faces, partial, message
):
    even = lax.axis_index("fx") % 2 == 0
    masks = masks_of(face_picks[1:2, :], kinds(even, True) + [3.0, 4.0])
    answers = stacked(three(near) + middles(y_first, y_second))
    moved = own[...] + placed(answers, face_slots(face_picks), masks)
    moved = moved * mass_faces[0:1, :]
    partial[...] = moved
    message[0:F, :] = moved[:, 0:128]
    message[F : F + 8, :] = face_picks[:, 0:128]
    message[F + 2 : F + 3, :] = mass_faces[0:1, 0:128]


def face_far_body(partial, far, faces_in, sent, face_picks, mass_faces, along_x, along_y, other):
    even = lax.axis_index("fx") % 2 == 0
    masks = masks_of(face_picks[1:2, :], kinds(even, False))
    moved = placed(stacked(three(far)), face_slots(face_picks), masks) * mass_faces[0:1, :]
    result = partial[...] + moved
    along_x[...] = result[:, 0:128]
    along_y[...] = result[:, 128:256]
    slot, kind, weight = [faces_in[F + q : F + q + 1, :] for q in range(3)]
    moved = placed(stacked(three(sent)), [slot], masks_of(kind, kinds(even, True)))
    other[...] = faces_in[0:F, :] + moved * weight


def place_body(
    s, own_a, own_b, x_first, x_second, y_first, y_second, picks, factors, mass, result
):
    answers = arrived(x_first, x_second, y_first, y_second)
    for n in range(NODES):
        tiles = [slice(2 * n + h, 2 * n + h + 1) for h in range(2)]
        masks = [
            jnp.concatenate([factors[NODES + d, t, :] for t in tiles], axis=1) for d in range(8)
        ]
        moved = placed(answers, [picks[1, t, :] for t in tiles], masks)
        for ref, (begin, end) in zip((own_a, own_b), PIECES[s]):
            if begin <= n < end:
                own = ref[:, (n - begin) * E : (n - begin + 1) * E]
        result[:, n * E : (n + 1) * E] = (own + moved) * mass[n : n + 1, :]


def rim_body(along_y, x_first, x_second, *results):
    low, high = from_swaps("fx", x_first[...], x_second[...])
    result = summed_faces(along_y[...], low, high)
    for ref in results:
        ref[...] = result


def scale_body(mass, x_first, x_second, y_first, y_second, inverse, on_faces):
    x_low, x_high = from_swaps("fx", x_first[8:16, :], x_second[8:16, :])
    y_low, y_high = from_swaps("fy", y_first[8:16, :], y_second[8:16, :])
    low, high, halo = [
        eight(row[6:7]) for row in (x_low, x_high, halo_of(y_low, y_high))
    ]
    nodes = [eight(mass[n : n + 1, :]) for n in range(NODES)]
    nodes = summed_nodes(nodes, low, high)
    nodes = [1.0 / with_halo(n, node, halo) for n, node in enumerate(nodes)]
    for n in range(NODES):
        inverse[n : n + 1, :] = nodes[n][0:1]
    on_faces[...] = faces(lambda n, t: nodes[n][:, t * 128 : (t + 1) * 128])[1]


def sum_body(weighted, x_first, x_second, inverse, result, table=None):
    low, high = from_swaps("fx", x_first[...], x_second[...])
    nodes = summed_nodes([weighted[:, n * E : (n + 1) * E] for n in range(NODES)], low, high)
    for n in range(NODES):
        node = nodes[n] * inverse[n : n + 1, :]
        result[:, n * E : (n + 1) * E] = node
        if table is not None:
            high_part, low_part = halves(node)
            table[n * F : (n + 1) * F, 0:E] = high_part
            table[n * F : (n + 1) * F, E : 2 * E] = low_part


def finish_body(summed, y_first, y_second, scale, table):
    halo = halo_of(*from_swaps("fy", y_first[...], y_second[...])) * scale[0:1, :]
    for n in range(NODES):
        node = with_halo(n, summed[:, n * E : (n + 1) * E], halo)
        high, low = halves(node)
        table[n * F : (n + 1) * F, 0:E] = high
        table[n * F : (n + 1) * F, E : 2 * E] = low


FACE_NODES = tuple(n for n in range(NODES) if n % 4 in (0, 3))
INNER_NODES = tuple(n for n in range(NODES) if n % 4 in (1, 2))


def inner_body(weighted, x_first, x_second, inverse, part, result, block, sems):
    low, high = from_swaps("fx", x_first[...], x_second[...])
    nodes = summed_nodes([weighted[:, n * E : (n + 1) * E] for n in range(NODES)], low, high)
    copies = []
    for i, n in enumerate(INNER_NODES):
        block[i] = nodes[n] * inverse[n : n + 1, :]
        copy = pltpu.make_async_copy(block.at[i], result.at[:, n, :], sems.at[i])
        copy.start()
        copies.append(copy)
    for i, n in enumerate(FACE_NODES):
        part[:, i * E : (i + 1) * E] = nodes[n] * inverse[n : n + 1, :]
    for copy in copies:
        copy.wait()


def last_body(part, y_first, y_second, scale, begun, result, block, sems):
    halo = halo_of(*from_swaps("fy", y_first[...], y_second[...])) * scale[0:1, :]
    copies = []
    for i, n in enumerate(FACE_NODES):
        block[i] = with_halo(n, part[:, i * E : (i + 1) * E], halo)
        copy = pltpu.make_async_copy(block.at[i], result.at[:, n, :], sems.at[i])
        copy.start()
        copies.append(copy)
    for copy in copies:
        copy.wait()


def per_device(tracers, node_mass, point_order, offsets, source, coords):
    ask = shape((24, 128))
    answers = shape((3 * F, 128))
    face = shape((F, 128))
    table_shape = shape((NODES * F, 2 * E), BF16)
    lists = [
        pltpu.SMEM(offsets.shape, jnp.int32),
        pltpu.VMEM(source.shape, jnp.int32),
        pltpu.VMEM(coords.shape, jnp.int32),
    ]
    first, second, mid, mass_faces = call(
        asks_body,
        [ask, ask, ask, shape((8, 256))],
        "asks",
        hbm=(0, 1, 2, 3),
        count=4,
        scratch=lists
        + [
            pltpu.VMEM(node_mass.shape, F32),
            pltpu.VMEM((8, POINTS), F32),
            pltpu.VMEM((72, 128), F32),
            pltpu.SemaphoreType.DMA((4,)),
        ],
    )(*[in_hbm(a) for a in (offsets, source, coords, node_mass)])
    asked = swap("fx", first, second)
    requests = [shape((2, TILES, 128)), shape((NODES + 8, TILES, 128)), shape((8, 256))]
    *now, later, later_starts = call(
        order_body,
        requests + [shape((8, POINTS), jnp.int32), shape((8, 128), jnp.int32)],
        "order",
        hbm=(0, 1, 2, 3),
        count=4,
        scratch=[pltpu.VMEM(a.shape, jnp.int32) for a in (offsets, point_order, source, coords)]
        + [pltpu.SemaphoreType.DMA((4,))],
    )(*[in_hbm(a) for a in (offsets, point_order, source, coords)])
    ordered_lists = [now]

    def interpolate(s, piece, after=0):
        begin, end = PIECES[s][piece]
        return call(
            lambda *refs: own_body(begin, *refs),
            shape((F, (end - begin) * E)),
            "own",
            count=3,
            after=after,
        )

    column_far, column_near, column_kept = call(column_body, [ask] * 3, "column", count=4)(
        *asked, mid, mass_faces
    )
    asked += swap("fy", column_far, column_near)
    table = call(
        table_body,
        table_shape,
        "table",
        hbm=(0,),
        count=1,
        scratch=[pltpu.VMEM(tracers.shape, F32), pltpu.SemaphoreType.DMA((1,))],
    )(in_hbm(tracers))
    far, near = call(reply_y_body, [answers] * 2, "reply_y", count=5, after=1)(
        table, *asked, now[2]
    )
    answers_y = swap("fy", far, near)
    inverse, scale = call(scale_body, [shape((NODES, E)), shape((8, 128))], "scale", count=5)(
        node_mass, *asked
    )
    for s in range(SUBSTEPS):
        picks, factors, face_picks = ordered_lists[s]
        if s == 1:
            table = call(finish_body, table_shape, "finish", count=4)(summed, *edges_y, scale)
        own = call(
            lambda *refs, s=s: reply_x_body(s, *refs), shape((2 * F, 128)), "reply_x", count=5
        )(table, *asked)
        own_faces = call(own_faces_body, shape((F, 256)), "own_faces", count=2)(table, face_picks)
        own_a = interpolate(s, 0)(table, picks, factors)
        near_sent, far_sent = call(row_body, [answers] * 2, "row", count=3, after=3)(
            *answers_y, own, own_a, scale, own_faces
        )
        near = swap_near("fx", near_sent)
        far = swap_far("fx", far_sent)
        partial, message = call(
            face_near_body, [shape((F, 256)), shape((F + 8, 128))], "faces_near", count=6
        )(own_faces, near, *answers_y, face_picks, mass_faces)
        faces_in = swap_far("fx", message)
        own_b = interpolate(s, 1, after=1)(table, picks, factors, partial)
        if s == 0:
            ordered_lists.append(
                call(later_body, requests, "order", count=2, after=1)(
                    later, later_starts, partial
                )
            )
        along_x, along_y, other = call(
            face_far_body, [face] * 3, "faces_far", count=6, after=2
        )(partial, far, faces_in, far_sent, face_picks, mass_faces, own_b, ordered_lists[1][2])
        edges_x = (other, swap_near("fx", along_x))
        place = call(
            lambda *refs, s=s: place_body(s, *refs),
            shape((F, POINTS)),
            "place",
            count=9,
            after=1,
        )
        moved = (own_a, own_b, far, near, *answers_y, picks, factors, node_mass)
        if s == 0:
            weighted = place(*moved, other)
            rims_far, rims_near, rims_kept = call(rim_body, [face] * 3, "rim", count=3, after=1)(
                along_y, *edges_x, weighted
            )
        else:
            rims_far, rims_near = call(rim_body, [face] * 2, "rim", count=3)(along_y, *edges_x)
            weighted = place(*moved, rims_near)
        edges_y = swap("fy", rims_far, rims_near)
        if s == 0:
            summed, early_table = call(
                sum_body, [shape((F, POINTS)), table_shape], "sum", count=4
            )(weighted, *edges_x, inverse)
            early_shapes = [shape((3, F, 128)), shape((8, 128), jnp.int32), shape((4, 8, 128))]
            early = call(
                lambda *refs: early_body(True, *refs), early_shapes, "early_far", count=5
            )(early_table, *asked)
            sent = call(late_far_body, answers, "late_far", count=5)(*early, edges_y[1], scale)
            far = swap_far("fy", sent)
            early = call(
                lambda *refs: early_body(False, *refs), early_shapes, "early_near", count=5, after=1
            )(early_table, *asked, sent)
            near = call(late_near_body, answers, "late_near", count=6)(*early, *edges_y, scale)
            near = swap_near("fy", near)
            far = call(fix_body, answers, "fix", count=4)(far, column_kept, rims_kept, scale)
            answers_y = (far, near)
        else:
            scratch = [pltpu.VMEM((8, F, E), F32), pltpu.SemaphoreType.DMA((8,))]
            vmem = pl.BlockSpec(memory_space=pltpu.VMEM)
            hbm = pl.BlockSpec(memory_space=pltpu.HBM)
            params = pltpu.CompilerParams(vmem_limit_bytes=VMEM_LIMIT)
            part, begun = pl.pallas_call(
                inner_body,
                out_shape=[shape((F, 8 * E)), shape((F, NODES, E))],
                in_specs=[vmem] * 4,
                out_specs=[vmem, hbm],
                scratch_shapes=scratch,
                name="inner",
                compiler_params=params,
            )(weighted, *edges_x, inverse)
            result = pl.pallas_call(
                last_body,
                out_shape=shape((F, NODES, E)),
                in_specs=[vmem] * 4 + [hbm],
                out_specs=hbm,
                scratch_shapes=scratch,
                input_output_aliases={4: 0},
                name="last",
                compiler_params=params,
            )(part, *edges_y, scale, begun)
    return result


def solution(mesh):
    return jax.shard_map(
        per_device,
        mesh=mesh,
        in_specs=(
            P(None, None, ("fx", "fy")),
            P(None, ("fx", "fy")),
            P(None, ("fx", "fy"), None),
            P(None, ("fx", "fy"), None),
            P(None, ("fx", "fy")),
            P(None, None, ("fx", "fy")),
        ),
        out_specs=P(None, None, ("fx", "fy")),
        check_vma=False,
    )
```

```python
import jax
import jax.numpy as jnp
from jax import lax
from jax.experimental import pallas as pl
from jax.experimental.pallas import tpu as pltpu
from jax.sharding import PartitionSpec as P

TX = 16
CAP = 128
QGRID = 1024
SUBSTEPS = 2
F = 64
E = 256
NODES = 16
POINTS = 4096
TILES = POINTS // 128
PIECES = (((0, 10), (10, 16)), ((0, 7), (7, 16)))
GLL_NODES = (-1.0, -0.4472135954999579, 0.4472135954999579, 1.0)
REMOTE = (0, 1, 2, 3, 5, 6, 7, 8)
BF16 = jnp.bfloat16
F32 = jnp.float32
VMEM_LIMIT = 40 * 2**20


def call(body, out_shape, name, hbm=(), count=0, after=0, scratch=()):
    specs = [
        pl.BlockSpec(memory_space=pltpu.HBM if i in hbm else pltpu.VMEM) for i in range(count)
    ] + [pl.BlockSpec(memory_space=pl.ANY)] * after

    def kernel(*refs):
        body(*refs[:count], *refs[count + after :])

    return pl.pallas_call(
        kernel,
        out_shape=out_shape,
        in_specs=specs,
        scratch_shapes=scratch,
        name=name,
        compiler_params=pltpu.CompilerParams(vmem_limit_bytes=VMEM_LIMIT),
    )


def in_hbm(array):
    return pltpu.with_memory_space_constraint(array, pltpu.HBM)


def shape(dims, dtype=F32):
    return jax.ShapeDtypeStruct(dims, dtype)


def swap_far(axis, block):
    size = lax.axis_size(axis)
    pairs = [(i, (((i + size - 1) % size ^ 1) + 1) % size) for i in range(size)]
    return lax.ppermute(block, axis, pairs)


def swap_near(axis, block):
    return lax.ppermute(block, axis, [(i, i ^ 1) for i in range(lax.axis_size(axis))])


def swap(axis, far, near):
    return swap_far(axis, far), swap_near(axis, near)


def to_swaps(axis, low, high):
    even = lax.axis_index(axis) % 2 == 0
    return jnp.where(even, low, high), jnp.where(even, high, low)


def from_swaps(axis, first, second):
    even = lax.axis_index(axis) % 2 == 0
    return jnp.where(even, first, second), jnp.where(even, second, first)


def lagrange(step):
    x = step * (2.0 / QGRID) - 1.0
    rows = []
    for a in range(4):
        factor = None
        for b in range(4):
            if b != a:
                term = (x - GLL_NODES[b]) * (1.0 / (GLL_NODES[a] - GLL_NODES[b]))
                factor = term if factor is None else factor * term
        rows.append(factor)
    return rows


def halves(block):
    high = block.astype(BF16)
    return high, (block - high.astype(F32)).astype(BF16)


def one_hot(index_rows, depth):
    rows = lax.broadcasted_iota(jnp.int32, (depth, 128), 0).astype(F32).astype(BF16)
    parts = [jnp.where(rows == r.astype(BF16), BF16(1), BF16(0)) for r in index_rows]
    return jnp.concatenate(parts, axis=1)


def lane_index(rows):
    return lax.broadcasted_iota(jnp.int32, (rows, 128), 1)


def eight(row):
    return jnp.broadcast_to(row, (8, row.shape[1]))


def pick_lanes(block, index):
    return jnp.take_along_axis(block, index, axis=1, mode="promise_in_bounds")


def faces(tile):
    rows = tile(0, 0).shape[0]
    lane = lane_index(rows)
    along_x = jnp.zeros((rows, 128), F32)
    for b in range(4):
        along_x = jnp.where(lane // 16 == b, pltpu.roll(tile(b, 0), b * 16, 1), along_x)
        shifted = pltpu.roll(tile(12 + b, 1), (b * 16 + 80) % 128, 1)
        along_x = jnp.where(lane // 16 == b + 4, shifted, along_x)
    along_y = jnp.zeros((rows, 128), F32)
    index = (lane % 8) * 16
    for a in range(4):
        for t in range(2):
            here = ((lane % 64) // 16 == a) & ((lane % 16) // 8 == t)
            first = pick_lanes(tile(4 * a, t), index)
            last = pick_lanes(tile(4 * a + 3, t), index + 15)
            along_y = jnp.where(here, jnp.where(lane < 64, first, last), along_y)
    return along_x, along_y


def summed_faces(own, low, high):
    lane = lane_index(own.shape[0])
    place = lane % 64
    behind = pltpu.roll(own, 128 - 48 + 1, 1)
    ahead = pltpu.roll(own, 48 - 1, 1)
    behind = jnp.where(lane == 0, low[:, 64:65], jnp.where(lane == 64, low[:, 127:128], behind))
    ahead = jnp.where(lane == 63, high[:, 0:1], jnp.where(lane == 127, high[:, 63:64], ahead))
    return own + jnp.where(place < 16, behind, jnp.where(place >= 48, ahead, 0.0))


def summed_nodes(nodes, low, high):
    rows = nodes[0].shape[0]
    lane = lane_index(rows)
    wide = lax.broadcasted_iota(jnp.int32, (rows, E), 1)
    nodes = list(nodes)
    for b in range(4):
        first, last = nodes[b], nodes[12 + b]
        behind = pltpu.roll(last, 16, 1)
        ahead = pltpu.roll(first, E - 16, 1)
        from_low = pltpu.roll(low, (128 - 64 - 16 * b) % 128, 1)
        from_high = pltpu.roll(high, 112 - 16 * b, 1)
        behind = jnp.concatenate(
            [jnp.where(lane < 16, from_low, behind[:, :128]), behind[:, 128:]], axis=1
        )
        ahead = jnp.concatenate(
            [ahead[:, :128], jnp.where(lane >= 112, from_high, ahead[:, 128:])], axis=1
        )
        nodes[b] = first + behind
        nodes[12 + b] = last + ahead
    for a in range(4):
        first, last = nodes[4 * a], nodes[4 * a + 3]
        behind = jnp.where(wide % 16 == 0, 0.0, pltpu.roll(last, 1, 1))
        ahead = jnp.where(wide % 16 == 15, 0.0, pltpu.roll(first, E - 1, 1))
        nodes[4 * a] = first + behind
        nodes[4 * a + 3] = last + ahead
    return nodes


def halo_of(low, high):
    lane = lane_index(low.shape[0])
    return pltpu.roll(jnp.where(lane >= 64, low, high), 64, 1)


def with_halo(n, node, halo):
    if n % 4 not in (0, 3):
        return node
    rows = node.shape[0]
    lane = lane_index(rows)
    wide = lax.broadcasted_iota(jnp.int32, (rows, E), 1)
    start = 16 * (n // 4) + (64 if n % 4 == 3 else 0)
    spread = [pick_lanes(halo, start + 8 * t + lane // 16) for t in range(2)]
    at = 15 if n % 4 == 3 else 0
    return node + jnp.where(wide % 16 == at, jnp.concatenate(spread, axis=1), 0.0)


def fetch(pairs, sems):
    copies = [pltpu.make_async_copy(*pair, sems.at[i]) for i, pair in enumerate(pairs)]
    for copy in copies:
        copy.start()
    for copy in copies:
        copy.wait()


def asks_body(
    offsets_in, source_in, coords_in, mass_in, first, second, mid, mass_faces,
    offsets, source, coords, mass, rows, message, sems,
):
    fetch(
        [(offsets_in, offsets), (source_in, source), (coords_in, coords), (mass_in, mass)], sems
    )
    for s in range(SUBSTEPS):
        rows[3 * s : 3 * s + 1, :] = source[s : s + 1, :].astype(F32)
        rows[3 * s + 1 : 3 * s + 3, :] = coords[s].astype(F32)
    rows[6:8, :] = jnp.zeros((2, POINTS), F32)
    early = lax.broadcasted_iota(jnp.int32, (8, 128), 0) < 3
    for k in REMOTE:
        parts = []
        for s in range(SUBSTEPS):
            start = offsets[s, 0, k]
            tile = jnp.minimum(start // 128, TILES - 1)
            after = jnp.minimum(tile + 1, TILES - 1)
            wide = jnp.concatenate(
                [rows[:, pl.ds(pl.multiple_of(t * 128, 128), 128)] for t in (tile, after)], axis=1
            )
            parts.append(pltpu.roll(wide, 256 - (start - tile * 128), 1)[:, 0:128])
        message[k * 8 : (k + 1) * 8, :] = jnp.where(early, parts[0], parts[1])
    along_x, along_y = faces(lambda n, t: eight(mass[n : n + 1, t * 128 : (t + 1) * 128]))
    for k in (1, 7):
        message[k * 8 + 6 : k * 8 + 7, :] = along_x[0:1]
    mass_faces[:, 0:128] = along_x
    mass_faces[:, 128:256] = along_y
    message[32:40, :] = jnp.zeros((8, 128), F32)
    first[...], second[...] = to_swaps("fx", message[0:24, :], message[48:72, :])
    mid[...] = message[24:48, :]


def order_body(
    offsets_in, order_in, source_in, coords_in, picks, factors, face_picks, later, later_starts,
    offsets, order, source, coords, sems,
):
    fetch(
        [(offsets_in, offsets), (order_in, order), (source_in, source), (coords_in, coords)], sems
    )
    ordered(
        order[0], source[0:1], coords[0, 0:1], coords[0, 1:2], offsets[0], picks, factors, face_picks
    )
    later[0:1, :] = order[1]
    later[1:2, :] = source[1:2, :]
    later[2:4, :] = coords[1]
    later_starts[0:1, 0:10] = offsets[1]


def later_body(lists, starts, picks, factors, face_picks):
    ordered(
        lists[0:1], lists[1:2], lists[2:3], lists[3:4], starts[0:1], picks, factors, face_picks
    )


def ordered(nodes, sources, xs, ys, starts, picks, factors, face_picks):
    chunk = 1024
    total = None
    for c in range(POINTS // chunk):
        lanes = slice(c * chunk, (c + 1) * chunk)
        node = nodes[:, lanes]
        tile_of = (node // 128).astype(F32).astype(BF16)
        lane_of = (node % 128).astype(F32).astype(BF16)
        position = lax.broadcasted_iota(jnp.int32, (1, chunk), 1) + c * chunk
        run = jnp.zeros((1, chunk), jnp.int32)
        begin = jnp.broadcast_to(starts[:, 0:1], (1, chunk))
        for k in range(1, 9):
            start = jnp.broadcast_to(starts[:, k : k + 1], (1, chunk))
            passed = position >= start
            run = run + passed.astype(jnp.int32)
            begin = jnp.where(passed, start, begin)
        own = run == 4
        kind = jnp.where(own, 8, jnp.where(run > 4, run - 1, run))
        pick = jnp.where(own, sources[:, lanes], position - begin)
        cx = xs[:, lanes]
        cy = ys[:, lanes]
        values = [pick, cx // 8, cx % 8, cy // 8, cy % 8, kind]
        tiles = lax.broadcasted_iota(jnp.int32, (TILES, chunk), 0).astype(F32).astype(BF16)
        here = tiles == tile_of
        left = jnp.concatenate(
            [jnp.where(here, v.astype(F32).astype(BF16), BF16(0)) for v in values], axis=0
        )
        spots = lax.broadcasted_iota(jnp.int32, (128, chunk), 0).astype(F32).astype(BF16)
        right = jnp.where(spots == lane_of, BF16(1), BF16(0))
        part = lax.dot_general(left, right, (((1,), (1,)), ((), ())), preferred_element_type=F32)
        total = part if total is None else total + part
    pick, xh, xl, yh, yl, kind = [total[q * TILES : (q + 1) * TILES] for q in range(6)]
    own = kind > 7.5
    picks[0] = jnp.where(own, pick, -1.0)
    picks[1] = jnp.where(own, -1.0, pick)
    mask = jnp.where(own, 1.0, 0.0)
    along_x = [row * mask for row in lagrange(xh * 8.0 + xl)]
    along_y = lagrange(yh * 8.0 + yl)
    for n in range(NODES):
        factors[n] = along_x[n // 4] * along_y[n % 4]
    for d in range(8):
        factors[NODES + d] = jnp.where(jnp.abs(kind - d) < 0.5, 1.0, 0.0)
    for q, rows in enumerate((picks[1], kind, picks[0], xh * 8.0 + xl, yh * 8.0 + yl)):
        along = faces(lambda n, t: eight(rows[2 * n + t : 2 * n + t + 1]))
        face_picks[q : q + 1, :] = jnp.concatenate(along, axis=1)[0:1]


def table_body(tracers_in, table, tracers, sems):
    fetch([(tracers_in, tracers)], sems)
    for q in range(0, F, 16):
        block = jnp.swapaxes(tracers[q : q + 16], 0, 1)
        for n in range(NODES):
            high, low = halves(block[n])
            table[n * F + q : n * F + q + 16, 0:E] = high
            table[n * F + q : n * F + q + 16, E : 2 * E] = low


def column_body(x_first, x_second, mid, mass_faces, first, second, kept):
    low, high = from_swaps("fx", x_first[...], x_second[...])
    masses = summed_faces(mass_faces[:, 128:256], low[8:16], high[8:16])[6:7]
    rows = lax.broadcasted_iota(jnp.int32, (8, 128), 0)
    columns = []
    for k in (0, 2):
        block = slice(k * 8, (k + 1) * 8)
        center = jnp.where(rows == 6, masses, mid[block, :])
        columns.append(jnp.concatenate([high[block], center, low[block]], axis=0))
    first[...], second[...] = to_swaps("fy", *columns)
    kept[...] = first[...]


def row_body(y_first, y_second, own, near, far):
    low, high = from_swaps("fy", y_first[...], y_second[...])
    mine = own[...]
    ahead = jnp.concatenate([low[0:F], mine[0:F], high[0:F]], axis=0)
    behind = jnp.concatenate([low[2 * F :], mine[F:], high[2 * F :]], axis=0)
    far[...], near[...] = to_swaps("fx", behind, ahead)


def combine(products, weights):
    total = None
    for n, weight in enumerate(weights):
        term = products[n * F : (n + 1) * F] * weight
        total = term if total is None else total + term
    return total


def asked_blocks(x_first, x_second, y_first, y_second):
    x_low, x_high = from_swaps("fx", x_first[...], x_second[...])
    y_low, y_high = from_swaps("fy", y_first[...], y_second[...])
    by_direction = {(1, 0): x_low[8:16], (-1, 0): x_high[8:16]}
    for k in range(3):
        by_direction[(k - 1, 1)] = y_low[k * 8 : (k + 1) * 8]
        by_direction[(k - 1, -1)] = y_high[k * 8 : (k + 1) * 8]
    return [by_direction[(k // 3 - 1, k % 3 - 1)] for k in REMOTE]


def asked_rows(s, asked):
    return [
        jnp.concatenate([r[s * 3 + q : s * 3 + q + 1, :] for r in asked], axis=0) for q in range(3)
    ]


def weights_of(cx, cy):
    along_x = lagrange(cx)
    along_y = lagrange(cy)
    return [along_x[n // 4] * along_y[n % 4] for n in range(NODES)]


def answer(table, pick, weights, directions):
    values = {}
    for both in directions:
        hot = one_hot([pick[d : d + 1] for d in both], E)
        products = jnp.dot(
            table[...], jnp.concatenate([hot, hot], axis=0), preferred_element_type=F32
        )
        for h, d in enumerate(both):
            lanes = slice(h * 128, (h + 1) * 128)
            values[d] = combine(products[:, lanes], [w[d : d + 1] for w in weights])
    return values


BEHIND = (2, 4, 7)
AHEAD = (0, 3, 5)
SIDES = (1, 6)


def side(rows, far):
    even = lax.axis_index("fy") % 2 == 0
    pairs = [(rows[b : b + 1], rows[a : a + 1]) for b, a in zip(BEHIND, AHEAD)]
    if far:
        return [jnp.where(even, behind, ahead) for behind, ahead in pairs]
    return [jnp.where(even, ahead, behind) for behind, ahead in pairs]


def sides_first(rows):
    return jnp.concatenate(side(rows, True) + side(rows, False) + [rows[0:2]], axis=0)


def reply_y_body(table, x_first, x_second, y_first, y_second, far, near):
    rows = asked_rows(0, asked_blocks(x_first, x_second, y_first, y_second))
    pick, cx, cy = [sides_first(block) for block in rows]
    values = answer(table, pick, weights_of(cx, cy), ((0, 1), (2, 3), (4, 5)))
    for k in range(3):
        far[k * F : (k + 1) * F, :] = values[k]
        near[k * F : (k + 1) * F, :] = values[3 + k]


def reply_x_body(s, table, x_first, x_second, y_first, y_second, own):
    pick, cx, cy = asked_rows(s, asked_blocks(x_first, x_second, y_first, y_second))
    values = answer(table, pick, weights_of(cx, cy), (SIDES,))
    for k, d in enumerate(SIDES):
        own[k * F : (k + 1) * F, :] = values[d]


def partner_rows(s, asked):
    return [
        jnp.concatenate([asked[k * 8 + 3 * s + q : k * 8 + 3 * s + q + 1, :] for k in range(3)], axis=0)
        for q in range(3)
    ]


def between_body(
    weighted, x_first, x_second, inverse, asked_far, asked_near, rims_near, scale,
    summed, message, values, lanes, shares, table,
):
    sum_body(weighted, x_first, x_second, inverse, summed, table)
    pick, cx, cy = [
        jnp.concatenate(pair, axis=0)
        for pair in zip(partner_rows(1, asked_far), partner_rows(1, asked_near))
    ]
    weights = weights_of(cx, cy)
    found = answer(table, pick, weights, ((0, 1), (2, 3), (4, 5)))
    element = pick.astype(jnp.int32)
    lane_of = element // 16 + jnp.where(element % 16 == 15, 64, 0)
    share_of = []
    for a in range(4):
        share = jnp.where(element % 16 == 15, weights[4 * a + 3], 0.0)
        share_of.append(jnp.where(element % 16 == 0, weights[4 * a], share))
    even = lax.axis_index("fy") % 2 == 0
    block = pltpu.roll(rims_near[...], 64, 1) * scale[0:1, :]
    lane = lane_index(F)
    halo = jnp.where(jnp.where(even, lane - 64, 63 - lane) >= 0, block, 0.0)
    for d in range(3):
        index = jnp.broadcast_to(lane_of[d : d + 1], (F, 128))
        value = found[d]
        for a in range(4):
            value = value + pick_lanes(halo, index + 16 * a) * share_of[a][d : d + 1]
        message[d * F : (d + 1) * F, :] = value
        values[d] = found[3 + d]
    lanes[0:3, :] = lane_of[3:6]
    for a in range(4):
        shares[a, 0:3, :] = share_of[a][3:6]


def shared(values, lanes, shares, halo, message):
    for d in range(3):
        index = jnp.broadcast_to(lanes[d : d + 1, :], (F, 128))
        value = values[d]
        for a in range(4):
            value = value + pick_lanes(halo, index + 16 * a) * shares[a, d : d + 1, :]
        message[d * F : (d + 1) * F, :] = value


def late_near_body(values, lanes, shares, far, near, scale, message):
    halo = halo_of(*from_swaps("fy", far[...], near[...])) * scale[0:1, :]
    shared(values, lanes, shares, halo, message)


def fix_body(far, asked, rims, scale, result):
    even = lax.axis_index("fy") % 2 == 0
    pick, cx, cy = partner_rows(1, asked)
    weights = weights_of(cx, cy)
    element = pick.astype(jnp.int32)
    on_face = element % 16 == jnp.where(even, 15, 0)
    lanes = element // 16 + jnp.where(even, 0, 64)
    own = rims[...] * scale[0:1, :]
    for k in range(3):
        index = jnp.broadcast_to(lanes[k : k + 1], (F, 128))
        value = far[k * F : (k + 1) * F, :]
        for a in range(4):
            weight = jnp.where(even, weights[4 * a + 3], weights[4 * a])
            weight = jnp.where(on_face, weight, 0.0)
            value = value + pick_lanes(own, index + 16 * a) * weight[k : k + 1]
        result[k * F : (k + 1) * F, :] = value


def own_body(begin, table, picks, factors, result):
    def block(i, carry):
        at = 2 * (begin + i)
        hot = one_hot([picks[0, pl.ds(at + h, 1), :] for h in range(2)], E)
        products = jnp.dot(
            table[...], jnp.concatenate([hot, hot], axis=0), preferred_element_type=F32
        )
        weights = [
            jnp.concatenate([factors[n, pl.ds(at + h, 1), :] for h in range(2)], axis=1)
            for n in range(NODES)
        ]
        result[:, pl.ds(pl.multiple_of(i * E, E), E)] = combine(products, weights)
        return carry

    count = result.shape[1] // E
    lax.fori_loop(0, count, block, 0, unroll=5 if count == 10 else 3 if count in (6, 9) else count)


def stacked(blocks):
    return jnp.concatenate([jnp.concatenate(halves(block), axis=1) for block in blocks], axis=0)


def three(ref):
    return [ref[k * F : (k + 1) * F, :] for k in range(3)]


def middles(y_first, y_second):
    return list(from_swaps("fy", y_first[F : 2 * F, :], y_second[F : 2 * F, :]))


def arrived(x_first, x_second, y_first, y_second):
    even = lax.axis_index("fx") % 2 == 0
    pairs = list(zip(three(x_first), three(x_second)))
    low = [jnp.where(even, far, near) for far, near in pairs]
    high = [jnp.where(even, near, far) for far, near in pairs]
    return stacked(low + middles(y_first, y_second) + high)


def placed(answers, slots, masks):
    hot = one_hot(slots, CAP)
    products = jnp.dot(answers, jnp.concatenate([hot, hot], axis=0), preferred_element_type=F32)
    return combine(products, masks)


def masks_of(kind, bases):
    return [jnp.where(jnp.abs(kind - base) < 0.5, 1.0, 0.0) for base in bases]


def kinds(even, near):
    start = jnp.where(even == near, 5.0, 0.0)
    return [start + k for k in range(3)]


def face_slots(face_picks):
    return [face_picks[0:1, h * 128 : (h + 1) * 128] for h in range(2)]


def own_faces_body(table, face_picks, result):
    hot = one_hot([face_picks[2:3, h * 128 : (h + 1) * 128] for h in range(2)], E)
    products = jnp.dot(table[...], jnp.concatenate([hot, hot], axis=0), preferred_element_type=F32)
    result[...] = combine(products, weights_of(face_picks[3:4, :], face_picks[4:5, :]))


def face_near_body(
    own, near, y_first, y_second, face_picks, mass_faces, partial, message
):
    even = lax.axis_index("fx") % 2 == 0
    masks = masks_of(face_picks[1:2, :], kinds(even, True) + [3.0, 4.0])
    answers = stacked(three(near) + middles(y_first, y_second))
    moved = own[...] + placed(answers, face_slots(face_picks), masks)
    moved = moved * mass_faces[0:1, :]
    partial[...] = moved
    message[0:F, :] = moved[:, 0:128]
    message[F : F + 8, :] = face_picks[:, 0:128]
    message[F + 2 : F + 3, :] = mass_faces[0:1, 0:128]


def face_far_body(partial, far, faces_in, sent, face_picks, mass_faces, along_x, along_y, other):
    even = lax.axis_index("fx") % 2 == 0
    masks = masks_of(face_picks[1:2, :], kinds(even, False))
    moved = placed(stacked(three(far)), face_slots(face_picks), masks) * mass_faces[0:1, :]
    result = partial[...] + moved
    along_x[...] = result[:, 0:128]
    along_y[...] = result[:, 128:256]
    slot, kind, weight = [faces_in[F + q : F + q + 1, :] for q in range(3)]
    moved = placed(stacked(three(sent)), [slot], masks_of(kind, kinds(even, True)))
    other[...] = faces_in[0:F, :] + moved * weight


def place_body(
    s, own_a, own_b, x_first, x_second, y_first, y_second, picks, factors, mass, result
):
    answers = arrived(x_first, x_second, y_first, y_second)
    for n in range(NODES):
        tiles = [slice(2 * n + h, 2 * n + h + 1) for h in range(2)]
        masks = [
            jnp.concatenate([factors[NODES + d, t, :] for t in tiles], axis=1) for d in range(8)
        ]
        moved = placed(answers, [picks[1, t, :] for t in tiles], masks)
        for ref, (begin, end) in zip((own_a, own_b), PIECES[s]):
            if begin <= n < end:
                own = ref[:, (n - begin) * E : (n - begin + 1) * E]
        result[:, n * E : (n + 1) * E] = (own + moved) * mass[n : n + 1, :]


def rim_body(along_y, x_first, x_second, *results):
    low, high = from_swaps("fx", x_first[...], x_second[...])
    result = summed_faces(along_y[...], low, high)
    for ref in results:
        ref[...] = result


def scale_body(mass, x_first, x_second, y_first, y_second, inverse, on_faces):
    x_low, x_high = from_swaps("fx", x_first[8:16, :], x_second[8:16, :])
    y_low, y_high = from_swaps("fy", y_first[8:16, :], y_second[8:16, :])
    low, high, halo = [
        eight(row[6:7]) for row in (x_low, x_high, halo_of(y_low, y_high))
    ]
    nodes = [eight(mass[n : n + 1, :]) for n in range(NODES)]
    nodes = summed_nodes(nodes, low, high)
    nodes = [1.0 / with_halo(n, node, halo) for n, node in enumerate(nodes)]
    for n in range(NODES):
        inverse[n : n + 1, :] = nodes[n][0:1]
    on_faces[...] = faces(lambda n, t: nodes[n][:, t * 128 : (t + 1) * 128])[1]


def sum_body(weighted, x_first, x_second, inverse, result, table=None):
    low, high = from_swaps("fx", x_first[...], x_second[...])
    nodes = summed_nodes([weighted[:, n * E : (n + 1) * E] for n in range(NODES)], low, high)
    for n in range(NODES):
        node = nodes[n] * inverse[n : n + 1, :]
        result[:, n * E : (n + 1) * E] = node
        if table is not None:
            high_part, low_part = halves(node)
            table[n * F : (n + 1) * F, 0:E] = high_part
            table[n * F : (n + 1) * F, E : 2 * E] = low_part


def finish_body(summed, y_first, y_second, scale, table):
    halo = halo_of(*from_swaps("fy", y_first[...], y_second[...])) * scale[0:1, :]
    for n in range(NODES):
        node = with_halo(n, summed[:, n * E : (n + 1) * E], halo)
        high, low = halves(node)
        table[n * F : (n + 1) * F, 0:E] = high
        table[n * F : (n + 1) * F, E : 2 * E] = low


FACE_NODES = tuple(n for n in range(NODES) if n % 4 in (0, 3))
INNER_NODES = tuple(n for n in range(NODES) if n % 4 in (1, 2))


def inner_body(weighted, x_first, x_second, inverse, part, result, block, sems):
    low, high = from_swaps("fx", x_first[...], x_second[...])
    nodes = summed_nodes([weighted[:, n * E : (n + 1) * E] for n in range(NODES)], low, high)
    copies = []
    for i, n in enumerate(INNER_NODES):
        block[i] = nodes[n] * inverse[n : n + 1, :]
        copy = pltpu.make_async_copy(block.at[i], result.at[:, n, :], sems.at[i])
        copy.start()
        copies.append(copy)
    for i, n in enumerate(FACE_NODES):
        part[:, i * E : (i + 1) * E] = nodes[n] * inverse[n : n + 1, :]
    for copy in copies:
        copy.wait()


def last_body(part, y_first, y_second, scale, begun, result, block, sems):
    halo = halo_of(*from_swaps("fy", y_first[...], y_second[...])) * scale[0:1, :]
    copies = []
    for i, n in enumerate(FACE_NODES):
        block[i] = with_halo(n, part[:, i * E : (i + 1) * E], halo)
        copy = pltpu.make_async_copy(block.at[i], result.at[:, n, :], sems.at[i])
        copy.start()
        copies.append(copy)
    for copy in copies:
        copy.wait()


def per_device(tracers, node_mass, point_order, offsets, source, coords):
    ask = shape((24, 128))
    answers = shape((3 * F, 128))
    face = shape((F, 128))
    table_shape = shape((NODES * F, 2 * E), BF16)
    lists = [
        pltpu.SMEM(offsets.shape, jnp.int32),
        pltpu.VMEM(source.shape, jnp.int32),
        pltpu.VMEM(coords.shape, jnp.int32),
    ]
    first, second, mid, mass_faces = call(
        asks_body,
        [ask, ask, ask, shape((8, 256))],
        "asks",
        hbm=(0, 1, 2, 3),
        count=4,
        scratch=lists
        + [
            pltpu.VMEM(node_mass.shape, F32),
            pltpu.VMEM((8, POINTS), F32),
            pltpu.VMEM((72, 128), F32),
            pltpu.SemaphoreType.DMA((4,)),
        ],
    )(*[in_hbm(a) for a in (offsets, source, coords, node_mass)])
    asked = swap("fx", first, second)
    requests = [shape((2, TILES, 128)), shape((NODES + 8, TILES, 128)), shape((8, 256))]
    *now, later, later_starts = call(
        order_body,
        requests + [shape((8, POINTS), jnp.int32), shape((8, 128), jnp.int32)],
        "order",
        hbm=(0, 1, 2, 3),
        count=4,
        scratch=[pltpu.VMEM(a.shape, jnp.int32) for a in (offsets, point_order, source, coords)]
        + [pltpu.SemaphoreType.DMA((4,))],
    )(*[in_hbm(a) for a in (offsets, point_order, source, coords)])
    ordered_lists = [now]

    def interpolate(s, piece, after=0):
        begin, end = PIECES[s][piece]
        return call(
            lambda *refs: own_body(begin, *refs),
            shape((F, (end - begin) * E)),
            "own",
            count=3,
            after=after,
        )

    column_far, column_near, column_kept = call(column_body, [ask] * 3, "column", count=4)(
        *asked, mid, mass_faces
    )
    asked += swap("fy", column_far, column_near)
    table = call(
        table_body,
        table_shape,
        "table",
        hbm=(0,),
        count=1,
        scratch=[pltpu.VMEM(tracers.shape, F32), pltpu.SemaphoreType.DMA((1,))],
    )(in_hbm(tracers))
    far, near = call(reply_y_body, [answers] * 2, "reply_y", count=5, after=1)(
        table, *asked, now[2]
    )
    answers_y = swap("fy", far, near)
    inverse, scale = call(scale_body, [shape((NODES, E)), shape((8, 128))], "scale", count=5)(
        node_mass, *asked
    )
    for s in range(SUBSTEPS):
        picks, factors, face_picks = ordered_lists[s]
        if s == 1:
            table = call(finish_body, table_shape, "finish", count=4)(summed, *edges_y, scale)
        own = call(
            lambda *refs, s=s: reply_x_body(s, *refs), shape((2 * F, 128)), "reply_x", count=5
        )(table, *asked)
        own_faces = call(own_faces_body, shape((F, 256)), "own_faces", count=2)(table, face_picks)
        own_a = interpolate(s, 0)(table, picks, factors)
        near_sent, far_sent = call(row_body, [answers] * 2, "row", count=3, after=3)(
            *answers_y, own, own_a, scale, own_faces
        )
        near = swap_near("fx", near_sent)
        far = swap_far("fx", far_sent)
        partial, message = call(
            face_near_body, [shape((F, 256)), shape((F + 8, 128))], "faces_near", count=6
        )(own_faces, near, *answers_y, face_picks, mass_faces)
        faces_in = swap_far("fx", message)
        own_b = interpolate(s, 1, after=1)(table, picks, factors, partial)
        if s == 0:
            ordered_lists.append(
                call(later_body, requests, "order", count=2, after=1)(
                    later, later_starts, partial
                )
            )
        along_x, along_y, other = call(
            face_far_body, [face] * 3, "faces_far", count=6, after=2
        )(partial, far, faces_in, far_sent, face_picks, mass_faces, own_b, ordered_lists[1][2])
        edges_x = (other, swap_near("fx", along_x))
        place = call(
            lambda *refs, s=s: place_body(s, *refs),
            shape((F, POINTS)),
            "place",
            count=9,
            after=1,
        )
        moved = (own_a, own_b, far, near, *answers_y, picks, factors, node_mass)
        if s == 0:
            weighted = place(*moved, other)
            rims_far, rims_near, rims_kept = call(rim_body, [face] * 3, "rim", count=3, after=1)(
                along_y, *edges_x, weighted
            )
        else:
            rims_far, rims_near = call(rim_body, [face] * 2, "rim", count=3)(along_y, *edges_x)
            weighted = place(*moved, rims_near)
        edges_y = swap("fy", rims_far, rims_near)
        if s == 0:
            summed, sent, *early = call(
                between_body,
                [
                    shape((F, POINTS)),
                    answers,
                    shape((3, F, 128)),
                    shape((8, 128), jnp.int32),
                    shape((4, 8, 128)),
                ],
                "between",
                count=8,
                scratch=[pltpu.VMEM((NODES * F, 2 * E), BF16)],
            )(weighted, *edges_x, inverse, asked[2], asked[3], edges_y[1], scale)
            far = swap_far("fy", sent)
            near = call(late_near_body, answers, "late_near", count=6)(*early, *edges_y, scale)
            near = swap_near("fy", near)
            far = call(fix_body, answers, "fix", count=4)(far, column_kept, rims_kept, scale)
            answers_y = (far, near)
        else:
            scratch = [pltpu.VMEM((8, F, E), F32), pltpu.SemaphoreType.DMA((8,))]
            vmem = pl.BlockSpec(memory_space=pltpu.VMEM)
            hbm = pl.BlockSpec(memory_space=pltpu.HBM)
            params = pltpu.CompilerParams(vmem_limit_bytes=VMEM_LIMIT)
            part, begun = pl.pallas_call(
                inner_body,
                out_shape=[shape((F, 8 * E)), shape((F, NODES, E))],
                in_specs=[vmem] * 4,
                out_specs=[vmem, hbm],
                scratch_shapes=scratch,
                name="inner",
                compiler_params=params,
            )(weighted, *edges_x, inverse)
            result = pl.pallas_call(
                last_body,
                out_shape=shape((F, NODES, E)),
                in_specs=[vmem] * 4 + [hbm],
                out_specs=hbm,
                scratch_shapes=scratch,
                input_output_aliases={4: 0},
                name="last",
                compiler_params=params,
            )(part, *edges_y, scale, begun)
    return result


def solution(mesh):
    return jax.shard_map(
        per_device,
        mesh=mesh,
        in_specs=(
            P(None, None, ("fx", "fy")),
            P(None, ("fx", "fy")),
            P(None, ("fx", "fy"), None),
            P(None, ("fx", "fy"), None),
            P(None, ("fx", "fy")),
            P(None, None, ("fx", "fy")),
        ),
        out_specs=P(None, None, ("fx", "fy")),
        check_vma=False,
    )
```

```python
import jax
import jax.numpy as jnp
from jax import lax
from jax.experimental import pallas as pl
from jax.experimental.pallas import tpu as pltpu
from jax.sharding import PartitionSpec as P

TX = 16
CAP = 128
QGRID = 1024
SUBSTEPS = 2
F = 64
E = 256
NODES = 16
POINTS = 4096
TILES = POINTS // 128
PIECES = (((0, 10), (10, 16)), ((0, 7), (7, 16)))
GLL_NODES = (-1.0, -0.4472135954999579, 0.4472135954999579, 1.0)
REMOTE = (0, 1, 2, 3, 5, 6, 7, 8)
BF16 = jnp.bfloat16
F32 = jnp.float32
VMEM_LIMIT = 40 * 2**20


def call(body, out_shape, name, hbm=(), count=0, after=0, scratch=()):
    specs = [
        pl.BlockSpec(memory_space=pltpu.HBM if i in hbm else pltpu.VMEM) for i in range(count)
    ] + [pl.BlockSpec(memory_space=pl.ANY)] * after

    def kernel(*refs):
        body(*refs[:count], *refs[count + after :])

    return pl.pallas_call(
        kernel,
        out_shape=out_shape,
        in_specs=specs,
        scratch_shapes=scratch,
        name=name,
        compiler_params=pltpu.CompilerParams(vmem_limit_bytes=VMEM_LIMIT),
    )


def in_hbm(array):
    return pltpu.with_memory_space_constraint(array, pltpu.HBM)


def shape(dims, dtype=F32):
    return jax.ShapeDtypeStruct(dims, dtype)


def swap_far(axis, block):
    size = lax.axis_size(axis)
    pairs = [(i, (((i + size - 1) % size ^ 1) + 1) % size) for i in range(size)]
    return lax.ppermute(block, axis, pairs)


def swap_near(axis, block):
    return lax.ppermute(block, axis, [(i, i ^ 1) for i in range(lax.axis_size(axis))])


def swap(axis, far, near):
    return swap_far(axis, far), swap_near(axis, near)


def to_swaps(axis, low, high):
    even = lax.axis_index(axis) % 2 == 0
    return jnp.where(even, low, high), jnp.where(even, high, low)


def from_swaps(axis, first, second):
    even = lax.axis_index(axis) % 2 == 0
    return jnp.where(even, first, second), jnp.where(even, second, first)


def lagrange(step):
    x = step * (2.0 / QGRID) - 1.0
    rows = []
    for a in range(4):
        factor = None
        for b in range(4):
            if b != a:
                term = (x - GLL_NODES[b]) * (1.0 / (GLL_NODES[a] - GLL_NODES[b]))
                factor = term if factor is None else factor * term
        rows.append(factor)
    return rows


def halves(block):
    high = block.astype(BF16)
    return high, (block - high.astype(F32)).astype(BF16)


def one_hot(index_rows, depth):
    rows = lax.broadcasted_iota(jnp.int32, (depth, 128), 0).astype(F32).astype(BF16)
    parts = [jnp.where(rows == r.astype(BF16), BF16(1), BF16(0)) for r in index_rows]
    return jnp.concatenate(parts, axis=1)


def lane_index(rows):
    return lax.broadcasted_iota(jnp.int32, (rows, 128), 1)


def eight(row):
    return jnp.broadcast_to(row, (8, row.shape[1]))


def pick_lanes(block, index):
    return jnp.take_along_axis(block, index, axis=1, mode="promise_in_bounds")


def faces(tile):
    rows = tile(0, 0).shape[0]
    lane = lane_index(rows)
    along_x = jnp.zeros((rows, 128), F32)
    for b in range(4):
        along_x = jnp.where(lane // 16 == b, pltpu.roll(tile(b, 0), b * 16, 1), along_x)
        shifted = pltpu.roll(tile(12 + b, 1), (b * 16 + 80) % 128, 1)
        along_x = jnp.where(lane // 16 == b + 4, shifted, along_x)
    along_y = jnp.zeros((rows, 128), F32)
    index = (lane % 8) * 16
    for a in range(4):
        for t in range(2):
            here = ((lane % 64) // 16 == a) & ((lane % 16) // 8 == t)
            first = pick_lanes(tile(4 * a, t), index)
            last = pick_lanes(tile(4 * a + 3, t), index + 15)
            along_y = jnp.where(here, jnp.where(lane < 64, first, last), along_y)
    return along_x, along_y


def summed_faces(own, low, high):
    lane = lane_index(own.shape[0])
    place = lane % 64
    behind = pltpu.roll(own, 128 - 48 + 1, 1)
    ahead = pltpu.roll(own, 48 - 1, 1)
    behind = jnp.where(lane == 0, low[:, 64:65], jnp.where(lane == 64, low[:, 127:128], behind))
    ahead = jnp.where(lane == 63, high[:, 0:1], jnp.where(lane == 127, high[:, 63:64], ahead))
    return own + jnp.where(place < 16, behind, jnp.where(place >= 48, ahead, 0.0))


def summed_nodes(nodes, low, high):
    rows = nodes[0].shape[0]
    lane = lane_index(rows)
    wide = lax.broadcasted_iota(jnp.int32, (rows, E), 1)
    nodes = list(nodes)
    for b in range(4):
        first, last = nodes[b], nodes[12 + b]
        behind = pltpu.roll(last, 16, 1)
        ahead = pltpu.roll(first, E - 16, 1)
        from_low = pltpu.roll(low, (128 - 64 - 16 * b) % 128, 1)
        from_high = pltpu.roll(high, 112 - 16 * b, 1)
        behind = jnp.concatenate(
            [jnp.where(lane < 16, from_low, behind[:, :128]), behind[:, 128:]], axis=1
        )
        ahead = jnp.concatenate(
            [ahead[:, :128], jnp.where(lane >= 112, from_high, ahead[:, 128:])], axis=1
        )
        nodes[b] = first + behind
        nodes[12 + b] = last + ahead
    for a in range(4):
        first, last = nodes[4 * a], nodes[4 * a + 3]
        behind = jnp.where(wide % 16 == 0, 0.0, pltpu.roll(last, 1, 1))
        ahead = jnp.where(wide % 16 == 15, 0.0, pltpu.roll(first, E - 1, 1))
        nodes[4 * a] = first + behind
        nodes[4 * a + 3] = last + ahead
    return nodes


def halo_of(low, high):
    lane = lane_index(low.shape[0])
    return pltpu.roll(jnp.where(lane >= 64, low, high), 64, 1)


def with_halo(n, node, halo):
    if n % 4 not in (0, 3):
        return node
    rows = node.shape[0]
    lane = lane_index(rows)
    wide = lax.broadcasted_iota(jnp.int32, (rows, E), 1)
    start = 16 * (n // 4) + (64 if n % 4 == 3 else 0)
    spread = [pick_lanes(halo, start + 8 * t + lane // 16) for t in range(2)]
    at = 15 if n % 4 == 3 else 0
    return node + jnp.where(wide % 16 == at, jnp.concatenate(spread, axis=1), 0.0)


def fetch(pairs, sems):
    copies = [pltpu.make_async_copy(*pair, sems.at[i]) for i, pair in enumerate(pairs)]
    for copy in copies:
        copy.start()
    for copy in copies:
        copy.wait()


def asks_body(
    offsets_in, source_in, coords_in, mass_in, first, second, mid, mass_faces,
    offsets, source, coords, mass, rows, message, sems,
):
    fetch(
        [(offsets_in, offsets), (source_in, source), (coords_in, coords), (mass_in, mass)], sems
    )
    for s in range(SUBSTEPS):
        rows[3 * s : 3 * s + 1, :] = source[s : s + 1, :].astype(F32)
        rows[3 * s + 1 : 3 * s + 3, :] = coords[s].astype(F32)
    rows[6:8, :] = jnp.zeros((2, POINTS), F32)
    early = lax.broadcasted_iota(jnp.int32, (8, 128), 0) < 3
    for k in REMOTE:
        parts = []
        for s in range(SUBSTEPS):
            start = offsets[s, 0, k]
            tile = jnp.minimum(start // 128, TILES - 1)
            after = jnp.minimum(tile + 1, TILES - 1)
            wide = jnp.concatenate(
                [rows[:, pl.ds(pl.multiple_of(t * 128, 128), 128)] for t in (tile, after)], axis=1
            )
            parts.append(pltpu.roll(wide, 256 - (start - tile * 128), 1)[:, 0:128])
        message[k * 8 : (k + 1) * 8, :] = jnp.where(early, parts[0], parts[1])
    along_x, along_y = faces(lambda n, t: eight(mass[n : n + 1, t * 128 : (t + 1) * 128]))
    for k in (1, 7):
        message[k * 8 + 6 : k * 8 + 7, :] = along_x[0:1]
    mass_faces[:, 0:128] = along_x
    mass_faces[:, 128:256] = along_y
    message[32:40, :] = jnp.zeros((8, 128), F32)
    first[...], second[...] = to_swaps("fx", message[0:24, :], message[48:72, :])
    mid[...] = message[24:48, :]


def order_body(
    offsets_in, order_in, source_in, coords_in, picks, factors, face_picks, later, later_starts,
    offsets, order, source, coords, sems,
):
    fetch(
        [(offsets_in, offsets), (order_in, order), (source_in, source), (coords_in, coords)], sems
    )
    ordered(
        order[0], source[0:1], coords[0, 0:1], coords[0, 1:2], offsets[0], picks, factors, face_picks
    )
    later[0:1, :] = order[1]
    later[1:2, :] = source[1:2, :]
    later[2:4, :] = coords[1]
    later_starts[0:1, 0:10] = offsets[1]


def later_body(lists, starts, picks, factors, face_picks):
    ordered(
        lists[0:1], lists[1:2], lists[2:3], lists[3:4], starts[0:1], picks, factors, face_picks
    )


def ordered(nodes, sources, xs, ys, starts, picks, factors, face_picks):
    chunk = 1024
    total = None
    for c in range(POINTS // chunk):
        lanes = slice(c * chunk, (c + 1) * chunk)
        node = nodes[:, lanes]
        tile_of = (node // 128).astype(F32).astype(BF16)
        lane_of = (node % 128).astype(F32).astype(BF16)
        position = lax.broadcasted_iota(jnp.int32, (1, chunk), 1) + c * chunk
        run = jnp.zeros((1, chunk), jnp.int32)
        begin = jnp.broadcast_to(starts[:, 0:1], (1, chunk))
        for k in range(1, 9):
            start = jnp.broadcast_to(starts[:, k : k + 1], (1, chunk))
            passed = position >= start
            run = run + passed.astype(jnp.int32)
            begin = jnp.where(passed, start, begin)
        own = run == 4
        kind = jnp.where(own, 8, jnp.where(run > 4, run - 1, run))
        pick = jnp.where(own, sources[:, lanes], position - begin)
        cx = xs[:, lanes]
        cy = ys[:, lanes]
        values = [pick, cx // 8, cx % 8, cy // 8, cy % 8, kind]
        tiles = lax.broadcasted_iota(jnp.int32, (TILES, chunk), 0).astype(F32).astype(BF16)
        here = tiles == tile_of
        left = jnp.concatenate(
            [jnp.where(here, v.astype(F32).astype(BF16), BF16(0)) for v in values], axis=0
        )
        spots = lax.broadcasted_iota(jnp.int32, (128, chunk), 0).astype(F32).astype(BF16)
        right = jnp.where(spots == lane_of, BF16(1), BF16(0))
        part = lax.dot_general(left, right, (((1,), (1,)), ((), ())), preferred_element_type=F32)
        total = part if total is None else total + part
    pick, xh, xl, yh, yl, kind = [total[q * TILES : (q + 1) * TILES] for q in range(6)]
    own = kind > 7.5
    picks[0] = jnp.where(own, pick, -1.0)
    picks[1] = jnp.where(own, -1.0, pick)
    mask = jnp.where(own, 1.0, 0.0)
    along_x = [row * mask for row in lagrange(xh * 8.0 + xl)]
    along_y = lagrange(yh * 8.0 + yl)
    for n in range(NODES):
        factors[n] = along_x[n // 4] * along_y[n % 4]
    for d in range(8):
        factors[NODES + d] = jnp.where(jnp.abs(kind - d) < 0.5, 1.0, 0.0)
    for q, rows in enumerate((picks[1], kind, picks[0], xh * 8.0 + xl, yh * 8.0 + yl)):
        along = faces(lambda n, t: eight(rows[2 * n + t : 2 * n + t + 1]))
        face_picks[q : q + 1, :] = jnp.concatenate(along, axis=1)[0:1]


def table_body(tracers_in, table, tracers, sems):
    fetch([(tracers_in, tracers)], sems)
    for q in range(0, F, 16):
        block = jnp.swapaxes(tracers[q : q + 16], 0, 1)
        for n in range(NODES):
            high, low = halves(block[n])
            table[n * F + q : n * F + q + 16, 0:E] = high
            table[n * F + q : n * F + q + 16, E : 2 * E] = low


def column_body(x_first, x_second, mid, mass_faces, first, second, kept):
    low, high = from_swaps("fx", x_first[...], x_second[...])
    masses = summed_faces(mass_faces[:, 128:256], low[8:16], high[8:16])[6:7]
    rows = lax.broadcasted_iota(jnp.int32, (8, 128), 0)
    columns = []
    for k in (0, 2):
        block = slice(k * 8, (k + 1) * 8)
        center = jnp.where(rows == 6, masses, mid[block, :])
        columns.append(jnp.concatenate([high[block], center, low[block]], axis=0))
    first[...], second[...] = to_swaps("fy", *columns)
    kept[...] = first[...]


def row_body(y_first, y_second, own, near, far):
    low, high = from_swaps("fy", y_first[...], y_second[...])
    mine = own[...]
    ahead = jnp.concatenate([low[0:F], mine[0:F], high[0:F]], axis=0)
    behind = jnp.concatenate([low[2 * F :], mine[F:], high[2 * F :]], axis=0)
    far[...], near[...] = to_swaps("fx", behind, ahead)


def combine(products, weights):
    total = None
    for n, weight in enumerate(weights):
        term = products[n * F : (n + 1) * F] * weight
        total = term if total is None else total + term
    return total


def asked_blocks(x_first, x_second, y_first, y_second):
    x_low, x_high = from_swaps("fx", x_first[...], x_second[...])
    y_low, y_high = from_swaps("fy", y_first[...], y_second[...])
    by_direction = {(1, 0): x_low[8:16], (-1, 0): x_high[8:16]}
    for k in range(3):
        by_direction[(k - 1, 1)] = y_low[k * 8 : (k + 1) * 8]
        by_direction[(k - 1, -1)] = y_high[k * 8 : (k + 1) * 8]
    return [by_direction[(k // 3 - 1, k % 3 - 1)] for k in REMOTE]


def asked_rows(s, asked):
    return [
        jnp.concatenate([r[s * 3 + q : s * 3 + q + 1, :] for r in asked], axis=0) for q in range(3)
    ]


def weights_of(cx, cy):
    along_x = lagrange(cx)
    along_y = lagrange(cy)
    return [along_x[n // 4] * along_y[n % 4] for n in range(NODES)]


def answer(table, pick, weights, directions):
    values = {}
    for both in directions:
        hot = one_hot([pick[d : d + 1] for d in both], E)
        products = jnp.dot(
            table[...], jnp.concatenate([hot, hot], axis=0), preferred_element_type=F32
        )
        for h, d in enumerate(both):
            lanes = slice(h * 128, (h + 1) * 128)
            values[d] = combine(products[:, lanes], [w[d : d + 1] for w in weights])
    return values


BEHIND = (2, 4, 7)
AHEAD = (0, 3, 5)
SIDES = (1, 6)


def side(rows, far):
    even = lax.axis_index("fy") % 2 == 0
    pairs = [(rows[b : b + 1], rows[a : a + 1]) for b, a in zip(BEHIND, AHEAD)]
    if far:
        return [jnp.where(even, behind, ahead) for behind, ahead in pairs]
    return [jnp.where(even, ahead, behind) for behind, ahead in pairs]


def sides_first(rows):
    return jnp.concatenate(side(rows, True) + side(rows, False) + [rows[0:2]], axis=0)


def reply_y_body(table, x_first, x_second, y_first, y_second, far, near):
    rows = asked_rows(0, asked_blocks(x_first, x_second, y_first, y_second))
    pick, cx, cy = [sides_first(block) for block in rows]
    values = answer(table, pick, weights_of(cx, cy), ((0, 1), (2, 3), (4, 5)))
    for k in range(3):
        far[k * F : (k + 1) * F, :] = values[k]
        near[k * F : (k + 1) * F, :] = values[3 + k]


def reply_x_body(s, table, x_first, x_second, y_first, y_second, own):
    pick, cx, cy = asked_rows(s, asked_blocks(x_first, x_second, y_first, y_second))
    values = answer(table, pick, weights_of(cx, cy), (SIDES,))
    for k, d in enumerate(SIDES):
        own[k * F : (k + 1) * F, :] = values[d]


def partner_rows(s, asked):
    return [
        jnp.concatenate([asked[k * 8 + 3 * s + q : k * 8 + 3 * s + q + 1, :] for k in range(3)], axis=0)
        for q in range(3)
    ]


def between_body(
    weighted, x_first, x_second, inverse, asked_far, asked_near, summed, values, lanes, shares, table
):
    sum_body(weighted, x_first, x_second, inverse, summed, table)
    pick, cx, cy = [
        jnp.concatenate(pair, axis=0)
        for pair in zip(partner_rows(1, asked_far), partner_rows(1, asked_near))
    ]
    weights = weights_of(cx, cy)
    for d, value in answer(table, pick, weights, ((0, 1), (2, 3), (4, 5))).items():
        values[d] = value
    element = pick.astype(jnp.int32)
    lanes[0:6, :] = element // 16 + jnp.where(element % 16 == 15, 64, 0)
    for a in range(4):
        share = jnp.where(element % 16 == 15, weights[4 * a + 3], 0.0)
        shares[a, 0:6, :] = jnp.where(element % 16 == 0, weights[4 * a], share)


def shared(values, lanes, shares, halo, start, message):
    for k in range(3):
        d = start + k
        index = jnp.broadcast_to(lanes[d : d + 1, :], (F, 128))
        value = values[d]
        for a in range(4):
            value = value + pick_lanes(halo, index + 16 * a) * shares[a, d : d + 1, :]
        message[k * F : (k + 1) * F, :] = value


def late_far_body(values, lanes, shares, near, scale, message):
    even = lax.axis_index("fy") % 2 == 0
    block = pltpu.roll(near[...], 64, 1) * scale[0:1, :]
    lane = lane_index(F)
    halo = jnp.where(jnp.where(even, lane - 64, 63 - lane) >= 0, block, 0.0)
    shared(values, lanes, shares, halo, 0, message)


def late_near_body(values, lanes, shares, far, near, scale, message):
    halo = halo_of(*from_swaps("fy", far[...], near[...])) * scale[0:1, :]
    shared(values, lanes, shares, halo, 3, message)


def fix_body(far, asked, rims, scale, result):
    even = lax.axis_index("fy") % 2 == 0
    pick, cx, cy = partner_rows(1, asked)
    weights = weights_of(cx, cy)
    element = pick.astype(jnp.int32)
    on_face = element % 16 == jnp.where(even, 15, 0)
    lanes = element // 16 + jnp.where(even, 0, 64)
    own = rims[...] * scale[0:1, :]
    for k in range(3):
        index = jnp.broadcast_to(lanes[k : k + 1], (F, 128))
        value = far[k * F : (k + 1) * F, :]
        for a in range(4):
            weight = jnp.where(even, weights[4 * a + 3], weights[4 * a])
            weight = jnp.where(on_face, weight, 0.0)
            value = value + pick_lanes(own, index + 16 * a) * weight[k : k + 1]
        result[k * F : (k + 1) * F, :] = value


def own_body(begin, table, picks, factors, result):
    def block(i, carry):
        at = 2 * (begin + i)
        hot = one_hot([picks[0, pl.ds(at + h, 1), :] for h in range(2)], E)
        products = jnp.dot(
            table[...], jnp.concatenate([hot, hot], axis=0), preferred_element_type=F32
        )
        weights = [
            jnp.concatenate([factors[n, pl.ds(at + h, 1), :] for h in range(2)], axis=1)
            for n in range(NODES)
        ]
        result[:, pl.ds(pl.multiple_of(i * E, E), E)] = combine(products, weights)
        return carry

    count = result.shape[1] // E
    lax.fori_loop(0, count, block, 0, unroll=5 if count == 10 else 3 if count in (6, 9) else count)


def stacked(blocks):
    return jnp.concatenate([jnp.concatenate(halves(block), axis=1) for block in blocks], axis=0)


def three(ref):
    return [ref[k * F : (k + 1) * F, :] for k in range(3)]


def middles(y_first, y_second):
    return list(from_swaps("fy", y_first[F : 2 * F, :], y_second[F : 2 * F, :]))


def arrived(x_first, x_second, y_first, y_second):
    even = lax.axis_index("fx") % 2 == 0
    pairs = list(zip(three(x_first), three(x_second)))
    low = [jnp.where(even, far, near) for far, near in pairs]
    high = [jnp.where(even, near, far) for far, near in pairs]
    return stacked(low + middles(y_first, y_second) + high)


def placed(answers, slots, masks):
    hot = one_hot(slots, CAP)
    products = jnp.dot(answers, jnp.concatenate([hot, hot], axis=0), preferred_element_type=F32)
    return combine(products, masks)


def masks_of(kind, bases):
    return [jnp.where(jnp.abs(kind - base) < 0.5, 1.0, 0.0) for base in bases]


def kinds(even, near):
    start = jnp.where(even == near, 5.0, 0.0)
    return [start + k for k in range(3)]


def face_slots(face_picks):
    return [face_picks[0:1, h * 128 : (h + 1) * 128] for h in range(2)]


def own_faces_body(table, face_picks, result):
    hot = one_hot([face_picks[2:3, h * 128 : (h + 1) * 128] for h in range(2)], E)
    products = jnp.dot(table[...], jnp.concatenate([hot, hot], axis=0), preferred_element_type=F32)
    result[...] = combine(products, weights_of(face_picks[3:4, :], face_picks[4:5, :]))


def face_near_body(
    own, near, y_first, y_second, face_picks, mass_faces, partial, message
):
    even = lax.axis_index("fx") % 2 == 0
    masks = masks_of(face_picks[1:2, :], kinds(even, True) + [3.0, 4.0])
    answers = stacked(three(near) + middles(y_first, y_second))
    moved = own[...] + placed(answers, face_slots(face_picks), masks)
    moved = moved * mass_faces[0:1, :]
    partial[...] = moved
    message[0:F, :] = moved[:, 0:128]
    message[F : F + 8, :] = face_picks[:, 0:128]
    message[F + 2 : F + 3, :] = mass_faces[0:1, 0:128]


def face_far_body(partial, far, faces_in, sent, face_picks, mass_faces, along_x, along_y, other):
    even = lax.axis_index("fx") % 2 == 0
    masks = masks_of(face_picks[1:2, :], kinds(even, False))
    moved = placed(stacked(three(far)), face_slots(face_picks), masks) * mass_faces[0:1, :]
    result = partial[...] + moved
    along_x[...] = result[:, 0:128]
    along_y[...] = result[:, 128:256]
    slot, kind, weight = [faces_in[F + q : F + q + 1, :] for q in range(3)]
    moved = placed(stacked(three(sent)), [slot], masks_of(kind, kinds(even, True)))
    other[...] = faces_in[0:F, :] + moved * weight


def place_body(
    s, own_a, own_b, x_first, x_second, y_first, y_second, picks, factors, mass, result
):
    answers = arrived(x_first, x_second, y_first, y_second)
    for n in range(NODES):
        tiles = [slice(2 * n + h, 2 * n + h + 1) for h in range(2)]
        masks = [
            jnp.concatenate([factors[NODES + d, t, :] for t in tiles], axis=1) for d in range(8)
        ]
        moved = placed(answers, [picks[1, t, :] for t in tiles], masks)
        for ref, (begin, end) in zip((own_a, own_b), PIECES[s]):
            if begin <= n < end:
                own = ref[:, (n - begin) * E : (n - begin + 1) * E]
        result[:, n * E : (n + 1) * E] = (own + moved) * mass[n : n + 1, :]


def rim_body(along_y, x_first, x_second, *results):
    low, high = from_swaps("fx", x_first[...], x_second[...])
    result = summed_faces(along_y[...], low, high)
    for ref in results:
        ref[...] = result


def scale_body(mass, x_first, x_second, y_first, y_second, inverse, on_faces):
    x_low, x_high = from_swaps("fx", x_first[8:16, :], x_second[8:16, :])
    y_low, y_high = from_swaps("fy", y_first[8:16, :], y_second[8:16, :])
    low, high, halo = [
        eight(row[6:7]) for row in (x_low, x_high, halo_of(y_low, y_high))
    ]
    nodes = [eight(mass[n : n + 1, :]) for n in range(NODES)]
    nodes = summed_nodes(nodes, low, high)
    nodes = [1.0 / with_halo(n, node, halo) for n, node in enumerate(nodes)]
    for n in range(NODES):
        inverse[n : n + 1, :] = nodes[n][0:1]
    on_faces[...] = faces(lambda n, t: nodes[n][:, t * 128 : (t + 1) * 128])[1]


def sum_body(weighted, x_first, x_second, inverse, result, table=None):
    low, high = from_swaps("fx", x_first[...], x_second[...])
    nodes = summed_nodes([weighted[:, n * E : (n + 1) * E] for n in range(NODES)], low, high)
    for n in range(NODES):
        node = nodes[n] * inverse[n : n + 1, :]
        result[:, n * E : (n + 1) * E] = node
        if table is not None:
            high_part, low_part = halves(node)
            table[n * F : (n + 1) * F, 0:E] = high_part
            table[n * F : (n + 1) * F, E : 2 * E] = low_part


def finish_body(summed, y_first, y_second, scale, table):
    halo = halo_of(*from_swaps("fy", y_first[...], y_second[...])) * scale[0:1, :]
    for n in range(NODES):
        node = with_halo(n, summed[:, n * E : (n + 1) * E], halo)
        high, low = halves(node)
        table[n * F : (n + 1) * F, 0:E] = high
        table[n * F : (n + 1) * F, E : 2 * E] = low


FACE_NODES = tuple(n for n in range(NODES) if n % 4 in (0, 3))
INNER_NODES = tuple(n for n in range(NODES) if n % 4 in (1, 2))


def inner_body(weighted, x_first, x_second, inverse, part, result, block, sems):
    low, high = from_swaps("fx", x_first[...], x_second[...])
    nodes = summed_nodes([weighted[:, n * E : (n + 1) * E] for n in range(NODES)], low, high)
    copies = []
    for i, n in enumerate(INNER_NODES):
        block[i] = nodes[n] * inverse[n : n + 1, :]
        copy = pltpu.make_async_copy(block.at[i], result.at[:, n, :], sems.at[i])
        copy.start()
        copies.append(copy)
    for i, n in enumerate(FACE_NODES):
        part[:, i * E : (i + 1) * E] = nodes[n] * inverse[n : n + 1, :]
    for copy in copies:
        copy.wait()


def last_body(part, y_first, y_second, scale, begun, result, block, sems):
    halo = halo_of(*from_swaps("fy", y_first[...], y_second[...])) * scale[0:1, :]
    copies = []
    for i, n in enumerate(FACE_NODES):
        block[i] = with_halo(n, part[:, i * E : (i + 1) * E], halo)
        copy = pltpu.make_async_copy(block.at[i], result.at[:, n, :], sems.at[i])
        copy.start()
        copies.append(copy)
    for copy in copies:
        copy.wait()


def per_device(tracers, node_mass, point_order, offsets, source, coords):
    ask = shape((24, 128))
    answers = shape((3 * F, 128))
    face = shape((F, 128))
    table_shape = shape((NODES * F, 2 * E), BF16)
    lists = [
        pltpu.SMEM(offsets.shape, jnp.int32),
        pltpu.VMEM(source.shape, jnp.int32),
        pltpu.VMEM(coords.shape, jnp.int32),
    ]
    first, second, mid, mass_faces = call(
        asks_body,
        [ask, ask, ask, shape((8, 256))],
        "asks",
        hbm=(0, 1, 2, 3),
        count=4,
        scratch=lists
        + [
            pltpu.VMEM(node_mass.shape, F32),
            pltpu.VMEM((8, POINTS), F32),
            pltpu.VMEM((72, 128), F32),
            pltpu.SemaphoreType.DMA((4,)),
        ],
    )(*[in_hbm(a) for a in (offsets, source, coords, node_mass)])
    asked = swap("fx", first, second)
    requests = [shape((2, TILES, 128)), shape((NODES + 8, TILES, 128)), shape((8, 256))]
    *now, later, later_starts = call(
        order_body,
        requests + [shape((8, POINTS), jnp.int32), shape((8, 128), jnp.int32)],
        "order",
        hbm=(0, 1, 2, 3),
        count=4,
        scratch=[pltpu.VMEM(a.shape, jnp.int32) for a in (offsets, point_order, source, coords)]
        + [pltpu.SemaphoreType.DMA((4,))],
    )(*[in_hbm(a) for a in (offsets, point_order, source, coords)])
    ordered_lists = [now]

    def interpolate(s, piece, after=0):
        begin, end = PIECES[s][piece]
        return call(
            lambda *refs: own_body(begin, *refs),
            shape((F, (end - begin) * E)),
            "own",
            count=3,
            after=after,
        )

    column_far, column_near, column_kept = call(column_body, [ask] * 3, "column", count=4)(
        *asked, mid, mass_faces
    )
    asked += swap("fy", column_far, column_near)
    table = call(
        table_body,
        table_shape,
        "table",
        hbm=(0,),
        count=1,
        scratch=[pltpu.VMEM(tracers.shape, F32), pltpu.SemaphoreType.DMA((1,))],
    )(in_hbm(tracers))
    far, near = call(reply_y_body, [answers] * 2, "reply_y", count=5, after=1)(
        table, *asked, now[2]
    )
    answers_y = swap("fy", far, near)
    inverse, scale = call(scale_body, [shape((NODES, E)), shape((8, 128))], "scale", count=5)(
        node_mass, *asked
    )
    for s in range(SUBSTEPS):
        picks, factors, face_picks = ordered_lists[s]
        if s == 1:
            table = call(finish_body, table_shape, "finish", count=4)(summed, *edges_y, scale)
        own = call(
            lambda *refs, s=s: reply_x_body(s, *refs), shape((2 * F, 128)), "reply_x", count=5
        )(table, *asked)
        own_faces = call(own_faces_body, shape((F, 256)), "own_faces", count=2)(table, face_picks)
        own_a = interpolate(s, 0)(table, picks, factors)
        near_sent, far_sent = call(row_body, [answers] * 2, "row", count=3, after=3)(
            *answers_y, own, own_a, scale, own_faces
        )
        near = swap_near("fx", near_sent)
        far = swap_far("fx", far_sent)
        partial, message = call(
            face_near_body, [shape((F, 256)), shape((F + 8, 128))], "faces_near", count=6
        )(own_faces, near, *answers_y, face_picks, mass_faces)
        faces_in = swap_far("fx", message)
        own_b = interpolate(s, 1, after=1)(table, picks, factors, partial)
        if s == 0:
            ordered_lists.append(
                call(later_body, requests, "order", count=2, after=1)(
                    later, later_starts, partial
                )
            )
        along_x, along_y, other = call(
            face_far_body, [face] * 3, "faces_far", count=6, after=2
        )(partial, far, faces_in, far_sent, face_picks, mass_faces, own_b, ordered_lists[1][2])
        edges_x = (other, swap_near("fx", along_x))
        place = call(
            lambda *refs, s=s: place_body(s, *refs),
            shape((F, POINTS)),
            "place",
            count=9,
            after=1,
        )
        moved = (own_a, own_b, far, near, *answers_y, picks, factors, node_mass)
        if s == 0:
            weighted = place(*moved, other)
            rims_far, rims_near, rims_kept = call(rim_body, [face] * 3, "rim", count=3, after=1)(
                along_y, *edges_x, weighted
            )
        else:
            rims_far, rims_near = call(rim_body, [face] * 2, "rim", count=3)(along_y, *edges_x)
            weighted = place(*moved, rims_near)
        edges_y = swap("fy", rims_far, rims_near)
        if s == 0:
            summed, *early = call(
                between_body,
                [
                    shape((F, POINTS)),
                    shape((6, F, 128)),
                    shape((8, 128), jnp.int32),
                    shape((4, 8, 128)),
                ],
                "between",
                count=6,
                scratch=[pltpu.VMEM((NODES * F, 2 * E), BF16)],
            )(weighted, *edges_x, inverse, asked[2], asked[3])
            far = call(late_far_body, answers, "late_far", count=5)(*early, edges_y[1], scale)
            far = swap_far("fy", far)
            near = call(late_near_body, answers, "late_near", count=6)(*early, *edges_y, scale)
            near = swap_near("fy", near)
            far = call(fix_body, answers, "fix", count=4)(far, column_kept, rims_kept, scale)
            answers_y = (far, near)
        else:
            scratch = [pltpu.VMEM((8, F, E), F32), pltpu.SemaphoreType.DMA((8,))]
            vmem = pl.BlockSpec(memory_space=pltpu.VMEM)
            hbm = pl.BlockSpec(memory_space=pltpu.HBM)
            params = pltpu.CompilerParams(vmem_limit_bytes=VMEM_LIMIT)
            part, begun = pl.pallas_call(
                inner_body,
                out_shape=[shape((F, 8 * E)), shape((F, NODES, E))],
                in_specs=[vmem] * 4,
                out_specs=[vmem, hbm],
                scratch_shapes=scratch,
                name="inner",
                compiler_params=params,
            )(weighted, *edges_x, inverse)
            result = pl.pallas_call(
                last_body,
                out_shape=shape((F, NODES, E)),
                in_specs=[vmem] * 4 + [hbm],
                out_specs=hbm,
                scratch_shapes=scratch,
                input_output_aliases={4: 0},
                name="last",
                compiler_params=params,
            )(part, *edges_y, scale, begun)
    return result


def solution(mesh):
    return jax.shard_map(
        per_device,
        mesh=mesh,
        in_specs=(
            P(None, None, ("fx", "fy")),
            P(None, ("fx", "fy")),
            P(None, ("fx", "fy"), None),
            P(None, ("fx", "fy"), None),
            P(None, ("fx", "fy")),
            P(None, None, ("fx", "fy")),
        ),
        out_specs=P(None, None, ("fx", "fy")),
        check_vma=False,
    )
```

```python
import jax
import jax.numpy as jnp
from jax import lax
from jax.experimental import pallas as pl
from jax.experimental.pallas import tpu as pltpu
from jax.sharding import PartitionSpec as P

TX = 16
CAP = 128
QGRID = 1024
SUBSTEPS = 2
F = 64
E = 256
NODES = 16
POINTS = 4096
TILES = POINTS // 128
PIECES = (((0, 10), (10, 16)), ((0, 7), (7, 16)))
GLL_NODES = (-1.0, -0.4472135954999579, 0.4472135954999579, 1.0)
REMOTE = (0, 1, 2, 3, 5, 6, 7, 8)
BF16 = jnp.bfloat16
F32 = jnp.float32
VMEM_LIMIT = 40 * 2**20


def call(body, out_shape, name, hbm=(), count=0, after=0, scratch=()):
    specs = [
        pl.BlockSpec(memory_space=pltpu.HBM if i in hbm else pltpu.VMEM) for i in range(count)
    ] + [pl.BlockSpec(memory_space=pl.ANY)] * after

    def kernel(*refs):
        body(*refs[:count], *refs[count + after :])

    return pl.pallas_call(
        kernel,
        out_shape=out_shape,
        in_specs=specs,
        scratch_shapes=scratch,
        name=name,
        compiler_params=pltpu.CompilerParams(vmem_limit_bytes=VMEM_LIMIT),
    )


def in_hbm(array):
    return pltpu.with_memory_space_constraint(array, pltpu.HBM)


def shape(dims, dtype=F32):
    return jax.ShapeDtypeStruct(dims, dtype)


def swap_far(axis, block):
    size = lax.axis_size(axis)
    pairs = [(i, (((i + size - 1) % size ^ 1) + 1) % size) for i in range(size)]
    return lax.ppermute(block, axis, pairs)


def swap_near(axis, block):
    return lax.ppermute(block, axis, [(i, i ^ 1) for i in range(lax.axis_size(axis))])


def swap(axis, far, near):
    return swap_far(axis, far), swap_near(axis, near)


def to_swaps(axis, low, high):
    even = lax.axis_index(axis) % 2 == 0
    return jnp.where(even, low, high), jnp.where(even, high, low)


def from_swaps(axis, first, second):
    even = lax.axis_index(axis) % 2 == 0
    return jnp.where(even, first, second), jnp.where(even, second, first)


def lagrange(step):
    x = step * (2.0 / QGRID) - 1.0
    rows = []
    for a in range(4):
        factor = None
        for b in range(4):
            if b != a:
                term = (x - GLL_NODES[b]) * (1.0 / (GLL_NODES[a] - GLL_NODES[b]))
                factor = term if factor is None else factor * term
        rows.append(factor)
    return rows


def halves(block):
    high = block.astype(BF16)
    return high, (block - high.astype(F32)).astype(BF16)


def one_hot(index_rows, depth):
    rows = lax.broadcasted_iota(jnp.int32, (depth, 128), 0).astype(F32).astype(BF16)
    parts = [jnp.where(rows == r.astype(BF16), BF16(1), BF16(0)) for r in index_rows]
    return jnp.concatenate(parts, axis=1)


def lane_index(rows):
    return lax.broadcasted_iota(jnp.int32, (rows, 128), 1)


def eight(row):
    return jnp.broadcast_to(row, (8, row.shape[1]))


def pick_lanes(block, index):
    return jnp.take_along_axis(block, index, axis=1, mode="promise_in_bounds")


def faces(tile):
    rows = tile(0, 0).shape[0]
    lane = lane_index(rows)
    along_x = jnp.zeros((rows, 128), F32)
    for b in range(4):
        along_x = jnp.where(lane // 16 == b, pltpu.roll(tile(b, 0), b * 16, 1), along_x)
        shifted = pltpu.roll(tile(12 + b, 1), (b * 16 + 80) % 128, 1)
        along_x = jnp.where(lane // 16 == b + 4, shifted, along_x)
    along_y = jnp.zeros((rows, 128), F32)
    index = (lane % 8) * 16
    for a in range(4):
        for t in range(2):
            here = ((lane % 64) // 16 == a) & ((lane % 16) // 8 == t)
            first = pick_lanes(tile(4 * a, t), index)
            last = pick_lanes(tile(4 * a + 3, t), index + 15)
            along_y = jnp.where(here, jnp.where(lane < 64, first, last), along_y)
    return along_x, along_y


def summed_faces(own, low, high):
    lane = lane_index(own.shape[0])
    place = lane % 64
    behind = pltpu.roll(own, 128 - 48 + 1, 1)
    ahead = pltpu.roll(own, 48 - 1, 1)
    behind = jnp.where(lane == 0, low[:, 64:65], jnp.where(lane == 64, low[:, 127:128], behind))
    ahead = jnp.where(lane == 63, high[:, 0:1], jnp.where(lane == 127, high[:, 63:64], ahead))
    return own + jnp.where(place < 16, behind, jnp.where(place >= 48, ahead, 0.0))


def summed_nodes(nodes, low, high):
    rows = nodes[0].shape[0]
    lane = lane_index(rows)
    wide = lax.broadcasted_iota(jnp.int32, (rows, E), 1)
    nodes = list(nodes)
    for b in range(4):
        first, last = nodes[b], nodes[12 + b]
        behind = pltpu.roll(last, 16, 1)
        ahead = pltpu.roll(first, E - 16, 1)
        from_low = pltpu.roll(low, (128 - 64 - 16 * b) % 128, 1)
        from_high = pltpu.roll(high, 112 - 16 * b, 1)
        behind = jnp.concatenate(
            [jnp.where(lane < 16, from_low, behind[:, :128]), behind[:, 128:]], axis=1
        )
        ahead = jnp.concatenate(
            [ahead[:, :128], jnp.where(lane >= 112, from_high, ahead[:, 128:])], axis=1
        )
        nodes[b] = first + behind
        nodes[12 + b] = last + ahead
    for a in range(4):
        first, last = nodes[4 * a], nodes[4 * a + 3]
        behind = jnp.where(wide % 16 == 0, 0.0, pltpu.roll(last, 1, 1))
        ahead = jnp.where(wide % 16 == 15, 0.0, pltpu.roll(first, E - 1, 1))
        nodes[4 * a] = first + behind
        nodes[4 * a + 3] = last + ahead
    return nodes


def halo_of(low, high):
    lane = lane_index(low.shape[0])
    return pltpu.roll(jnp.where(lane >= 64, low, high), 64, 1)


def with_halo(n, node, halo):
    if n % 4 not in (0, 3):
        return node
    rows = node.shape[0]
    lane = lane_index(rows)
    wide = lax.broadcasted_iota(jnp.int32, (rows, E), 1)
    start = 16 * (n // 4) + (64 if n % 4 == 3 else 0)
    spread = [pick_lanes(halo, start + 8 * t + lane // 16) for t in range(2)]
    at = 15 if n % 4 == 3 else 0
    return node + jnp.where(wide % 16 == at, jnp.concatenate(spread, axis=1), 0.0)


def fetch(pairs, sems):
    copies = [pltpu.make_async_copy(*pair, sems.at[i]) for i, pair in enumerate(pairs)]
    for copy in copies:
        copy.start()
    for copy in copies:
        copy.wait()


def asks_body(
    offsets_in, source_in, coords_in, mass_in, first, second, mid, mass_faces,
    offsets, source, coords, mass, rows, message, sems,
):
    fetch(
        [(offsets_in, offsets), (source_in, source), (coords_in, coords), (mass_in, mass)], sems
    )
    for s in range(SUBSTEPS):
        rows[3 * s : 3 * s + 1, :] = source[s : s + 1, :].astype(F32)
        rows[3 * s + 1 : 3 * s + 3, :] = coords[s].astype(F32)
    rows[6:8, :] = jnp.zeros((2, POINTS), F32)
    early = lax.broadcasted_iota(jnp.int32, (8, 128), 0) < 3
    for k in REMOTE:
        parts = []
        for s in range(SUBSTEPS):
            start = offsets[s, 0, k]
            tile = jnp.minimum(start // 128, TILES - 1)
            after = jnp.minimum(tile + 1, TILES - 1)
            wide = jnp.concatenate(
                [rows[:, pl.ds(pl.multiple_of(t * 128, 128), 128)] for t in (tile, after)], axis=1
            )
            parts.append(pltpu.roll(wide, 256 - (start - tile * 128), 1)[:, 0:128])
        message[k * 8 : (k + 1) * 8, :] = jnp.where(early, parts[0], parts[1])
    along_x, along_y = faces(lambda n, t: eight(mass[n : n + 1, t * 128 : (t + 1) * 128]))
    for k in (1, 7):
        message[k * 8 + 6 : k * 8 + 7, :] = along_x[0:1]
    mass_faces[:, 0:128] = along_x
    mass_faces[:, 128:256] = along_y
    message[32:40, :] = jnp.zeros((8, 128), F32)
    first[...], second[...] = to_swaps("fx", message[0:24, :], message[48:72, :])
    mid[...] = message[24:48, :]


def order_body(
    offsets_in, order_in, source_in, coords_in, picks, factors, face_picks, later, later_starts,
    offsets, order, source, coords, sems,
):
    fetch(
        [(offsets_in, offsets), (order_in, order), (source_in, source), (coords_in, coords)], sems
    )
    ordered(
        order[0], source[0:1], coords[0, 0:1], coords[0, 1:2], offsets[0], picks, factors, face_picks
    )
    later[0:1, :] = order[1]
    later[1:2, :] = source[1:2, :]
    later[2:4, :] = coords[1]
    later_starts[0:1, 0:10] = offsets[1]


def later_body(lists, starts, picks, factors, face_picks):
    ordered(
        lists[0:1], lists[1:2], lists[2:3], lists[3:4], starts[0:1], picks, factors, face_picks
    )


def ordered(nodes, sources, xs, ys, starts, picks, factors, face_picks):
    chunk = 1024
    total = None
    for c in range(POINTS // chunk):
        lanes = slice(c * chunk, (c + 1) * chunk)
        node = nodes[:, lanes]
        tile_of = (node // 128).astype(F32).astype(BF16)
        lane_of = (node % 128).astype(F32).astype(BF16)
        position = lax.broadcasted_iota(jnp.int32, (1, chunk), 1) + c * chunk
        run = jnp.zeros((1, chunk), jnp.int32)
        begin = jnp.broadcast_to(starts[:, 0:1], (1, chunk))
        for k in range(1, 9):
            start = jnp.broadcast_to(starts[:, k : k + 1], (1, chunk))
            passed = position >= start
            run = run + passed.astype(jnp.int32)
            begin = jnp.where(passed, start, begin)
        own = run == 4
        kind = jnp.where(own, 8, jnp.where(run > 4, run - 1, run))
        pick = jnp.where(own, sources[:, lanes], position - begin)
        cx = xs[:, lanes]
        cy = ys[:, lanes]
        values = [pick, cx // 8, cx % 8, cy // 8, cy % 8, kind]
        tiles = lax.broadcasted_iota(jnp.int32, (TILES, chunk), 0).astype(F32).astype(BF16)
        here = tiles == tile_of
        left = jnp.concatenate(
            [jnp.where(here, v.astype(F32).astype(BF16), BF16(0)) for v in values], axis=0
        )
        spots = lax.broadcasted_iota(jnp.int32, (128, chunk), 0).astype(F32).astype(BF16)
        right = jnp.where(spots == lane_of, BF16(1), BF16(0))
        part = lax.dot_general(left, right, (((1,), (1,)), ((), ())), preferred_element_type=F32)
        total = part if total is None else total + part
    pick, xh, xl, yh, yl, kind = [total[q * TILES : (q + 1) * TILES] for q in range(6)]
    own = kind > 7.5
    picks[0] = jnp.where(own, pick, -1.0)
    picks[1] = jnp.where(own, -1.0, pick)
    mask = jnp.where(own, 1.0, 0.0)
    along_x = [row * mask for row in lagrange(xh * 8.0 + xl)]
    along_y = lagrange(yh * 8.0 + yl)
    for n in range(NODES):
        factors[n] = along_x[n // 4] * along_y[n % 4]
    for d in range(8):
        factors[NODES + d] = jnp.where(jnp.abs(kind - d) < 0.5, 1.0, 0.0)
    for q, rows in enumerate((picks[1], kind, picks[0], xh * 8.0 + xl, yh * 8.0 + yl)):
        along = faces(lambda n, t: eight(rows[2 * n + t : 2 * n + t + 1]))
        face_picks[q : q + 1, :] = jnp.concatenate(along, axis=1)[0:1]


def table_body(tracers_in, table, tracers, sems):
    fetch([(tracers_in, tracers)], sems)
    for q in range(0, F, 16):
        block = jnp.swapaxes(tracers[q : q + 16], 0, 1)
        for n in range(NODES):
            high, low = halves(block[n])
            table[n * F + q : n * F + q + 16, 0:E] = high
            table[n * F + q : n * F + q + 16, E : 2 * E] = low


def column_body(x_first, x_second, mid, mass_faces, first, second, kept):
    low, high = from_swaps("fx", x_first[...], x_second[...])
    masses = summed_faces(mass_faces[:, 128:256], low[8:16], high[8:16])[6:7]
    rows = lax.broadcasted_iota(jnp.int32, (8, 128), 0)
    columns = []
    for k in (0, 2):
        block = slice(k * 8, (k + 1) * 8)
        center = jnp.where(rows == 6, masses, mid[block, :])
        columns.append(jnp.concatenate([high[block], center, low[block]], axis=0))
    first[...], second[...] = to_swaps("fy", *columns)
    kept[...] = first[...]


def row_body(y_first, y_second, own, near, far):
    low, high = from_swaps("fy", y_first[...], y_second[...])
    mine = own[...]
    ahead = jnp.concatenate([low[0:F], mine[0:F], high[0:F]], axis=0)
    behind = jnp.concatenate([low[2 * F :], mine[F:], high[2 * F :]], axis=0)
    far[...], near[...] = to_swaps("fx", behind, ahead)


def combine(products, weights):
    total = None
    for n, weight in enumerate(weights):
        term = products[n * F : (n + 1) * F] * weight
        total = term if total is None else total + term
    return total


def asked_blocks(x_first, x_second, y_first, y_second):
    x_low, x_high = from_swaps("fx", x_first[...], x_second[...])
    y_low, y_high = from_swaps("fy", y_first[...], y_second[...])
    by_direction = {(1, 0): x_low[8:16], (-1, 0): x_high[8:16]}
    for k in range(3):
        by_direction[(k - 1, 1)] = y_low[k * 8 : (k + 1) * 8]
        by_direction[(k - 1, -1)] = y_high[k * 8 : (k + 1) * 8]
    return [by_direction[(k // 3 - 1, k % 3 - 1)] for k in REMOTE]


def asked_rows(s, asked):
    return [
        jnp.concatenate([r[s * 3 + q : s * 3 + q + 1, :] for r in asked], axis=0) for q in range(3)
    ]


def weights_of(cx, cy):
    along_x = lagrange(cx)
    along_y = lagrange(cy)
    return [along_x[n // 4] * along_y[n % 4] for n in range(NODES)]


def answer(table, pick, weights, directions):
    values = {}
    for both in directions:
        hot = one_hot([pick[d : d + 1] for d in both], E)
        products = jnp.dot(
            table[...], jnp.concatenate([hot, hot], axis=0), preferred_element_type=F32
        )
        for h, d in enumerate(both):
            lanes = slice(h * 128, (h + 1) * 128)
            values[d] = combine(products[:, lanes], [w[d : d + 1] for w in weights])
    return values


BEHIND = (2, 4, 7)
AHEAD = (0, 3, 5)
SIDES = (1, 6)


def partner_rows(s, asked):
    return [
        jnp.concatenate([asked[k * 8 + 3 * s + q : k * 8 + 3 * s + q + 1, :] for k in range(3)], axis=0)
        for q in range(3)
    ]


def partners_rows(s, far, near):
    pairs = zip(partner_rows(s, far), partner_rows(s, near))
    return [jnp.concatenate(pair, axis=0) for pair in pairs]


def reply_y_body(table, asked_far, asked_near, far, near):
    pick, cx, cy = partners_rows(0, asked_far, asked_near)
    values = answer(table, pick, weights_of(cx, cy), ((0, 1), (2, 3), (4, 5)))
    for k in range(3):
        far[k * F : (k + 1) * F, :] = values[k]
        near[k * F : (k + 1) * F, :] = values[3 + k]


def reply_x_body(s, table, x_first, x_second, y_first, y_second, own):
    pick, cx, cy = asked_rows(s, asked_blocks(x_first, x_second, y_first, y_second))
    values = answer(table, pick, weights_of(cx, cy), (SIDES,))
    for k, d in enumerate(SIDES):
        own[k * F : (k + 1) * F, :] = values[d]


def between_body(
    weighted, x_first, x_second, inverse, asked_far, asked_near, summed, values, lanes, shares, table
):
    sum_body(weighted, x_first, x_second, inverse, summed, table)
    pick, cx, cy = partners_rows(1, asked_far, asked_near)
    weights = weights_of(cx, cy)
    for d, value in answer(table, pick, weights, ((0, 1), (2, 3), (4, 5))).items():
        values[d] = value
    element = pick.astype(jnp.int32)
    lanes[0:6, :] = element // 16 + jnp.where(element % 16 == 15, 64, 0)
    for a in range(4):
        share = jnp.where(element % 16 == 15, weights[4 * a + 3], 0.0)
        shares[a, 0:6, :] = jnp.where(element % 16 == 0, weights[4 * a], share)


def shared(values, lanes, shares, halo, start, message):
    for k in range(3):
        d = start + k
        index = jnp.broadcast_to(lanes[d : d + 1, :], (F, 128))
        value = values[d]
        for a in range(4):
            value = value + pick_lanes(halo, index + 16 * a) * shares[a, d : d + 1, :]
        message[k * F : (k + 1) * F, :] = value


def late_far_body(values, lanes, shares, near, scale, message):
    even = lax.axis_index("fy") % 2 == 0
    block = pltpu.roll(near[...], 64, 1) * scale[0:1, :]
    lane = lane_index(F)
    halo = jnp.where(jnp.where(even, lane - 64, 63 - lane) >= 0, block, 0.0)
    shared(values, lanes, shares, halo, 0, message)


def late_near_body(values, lanes, shares, far, near, scale, message):
    halo = halo_of(*from_swaps("fy", far[...], near[...])) * scale[0:1, :]
    shared(values, lanes, shares, halo, 3, message)


def fix_body(far, asked, rims, scale, result):
    even = lax.axis_index("fy") % 2 == 0
    pick, cx, cy = partner_rows(1, asked)
    weights = weights_of(cx, cy)
    element = pick.astype(jnp.int32)
    on_face = element % 16 == jnp.where(even, 15, 0)
    lanes = element // 16 + jnp.where(even, 0, 64)
    own = rims[...] * scale[0:1, :]
    for k in range(3):
        index = jnp.broadcast_to(lanes[k : k + 1], (F, 128))
        value = far[k * F : (k + 1) * F, :]
        for a in range(4):
            weight = jnp.where(even, weights[4 * a + 3], weights[4 * a])
            weight = jnp.where(on_face, weight, 0.0)
            value = value + pick_lanes(own, index + 16 * a) * weight[k : k + 1]
        result[k * F : (k + 1) * F, :] = value


def own_body(begin, table, picks, factors, result):
    def block(i, carry):
        at = 2 * (begin + i)
        hot = one_hot([picks[0, pl.ds(at + h, 1), :] for h in range(2)], E)
        products = jnp.dot(
            table[...], jnp.concatenate([hot, hot], axis=0), preferred_element_type=F32
        )
        weights = [
            jnp.concatenate([factors[n, pl.ds(at + h, 1), :] for h in range(2)], axis=1)
            for n in range(NODES)
        ]
        result[:, pl.ds(pl.multiple_of(i * E, E), E)] = combine(products, weights)
        return carry

    count = result.shape[1] // E
    lax.fori_loop(0, count, block, 0, unroll=5 if count == 10 else 3 if count in (6, 9) else count)


def stacked(blocks):
    return jnp.concatenate([jnp.concatenate(halves(block), axis=1) for block in blocks], axis=0)


def three(ref):
    return [ref[k * F : (k + 1) * F, :] for k in range(3)]


def middles(y_first, y_second):
    return list(from_swaps("fy", y_first[F : 2 * F, :], y_second[F : 2 * F, :]))


def arrived(x_first, x_second, y_first, y_second):
    even = lax.axis_index("fx") % 2 == 0
    pairs = list(zip(three(x_first), three(x_second)))
    low = [jnp.where(even, far, near) for far, near in pairs]
    high = [jnp.where(even, near, far) for far, near in pairs]
    return stacked(low + middles(y_first, y_second) + high)


def placed(answers, slots, masks):
    hot = one_hot(slots, CAP)
    products = jnp.dot(answers, jnp.concatenate([hot, hot], axis=0), preferred_element_type=F32)
    return combine(products, masks)


def masks_of(kind, bases):
    return [jnp.where(jnp.abs(kind - base) < 0.5, 1.0, 0.0) for base in bases]


def kinds(even, near):
    start = jnp.where(even == near, 5.0, 0.0)
    return [start + k for k in range(3)]


def face_slots(face_picks):
    return [face_picks[0:1, h * 128 : (h + 1) * 128] for h in range(2)]


def own_faces_body(table, face_picks, result):
    hot = one_hot([face_picks[2:3, h * 128 : (h + 1) * 128] for h in range(2)], E)
    products = jnp.dot(table[...], jnp.concatenate([hot, hot], axis=0), preferred_element_type=F32)
    result[...] = combine(products, weights_of(face_picks[3:4, :], face_picks[4:5, :]))


def face_near_body(
    own, near, y_first, y_second, face_picks, mass_faces, partial, message
):
    even = lax.axis_index("fx") % 2 == 0
    masks = masks_of(face_picks[1:2, :], kinds(even, True) + [3.0, 4.0])
    answers = stacked(three(near) + middles(y_first, y_second))
    moved = own[...] + placed(answers, face_slots(face_picks), masks)
    moved = moved * mass_faces[0:1, :]
    partial[...] = moved
    message[0:F, :] = moved[:, 0:128]
    message[F : F + 8, :] = face_picks[:, 0:128]
    message[F + 2 : F + 3, :] = mass_faces[0:1, 0:128]


def face_far_body(partial, far, faces_in, sent, face_picks, mass_faces, along_x, along_y, other):
    even = lax.axis_index("fx") % 2 == 0
    masks = masks_of(face_picks[1:2, :], kinds(even, False))
    moved = placed(stacked(three(far)), face_slots(face_picks), masks) * mass_faces[0:1, :]
    result = partial[...] + moved
    along_x[...] = result[:, 0:128]
    along_y[...] = result[:, 128:256]
    slot, kind, weight = [faces_in[F + q : F + q + 1, :] for q in range(3)]
    moved = placed(stacked(three(sent)), [slot], masks_of(kind, kinds(even, True)))
    other[...] = faces_in[0:F, :] + moved * weight


def place_body(
    s, own_a, own_b, x_first, x_second, y_first, y_second, picks, factors, mass, result
):
    answers = arrived(x_first, x_second, y_first, y_second)
    for n in range(NODES):
        tiles = [slice(2 * n + h, 2 * n + h + 1) for h in range(2)]
        masks = [
            jnp.concatenate([factors[NODES + d, t, :] for t in tiles], axis=1) for d in range(8)
        ]
        moved = placed(answers, [picks[1, t, :] for t in tiles], masks)
        for ref, (begin, end) in zip((own_a, own_b), PIECES[s]):
            if begin <= n < end:
                own = ref[:, (n - begin) * E : (n - begin + 1) * E]
        result[:, n * E : (n + 1) * E] = (own + moved) * mass[n : n + 1, :]


def rim_body(along_y, x_first, x_second, *results):
    low, high = from_swaps("fx", x_first[...], x_second[...])
    result = summed_faces(along_y[...], low, high)
    for ref in results:
        ref[...] = result


def scale_body(mass, x_first, x_second, y_first, y_second, inverse, on_faces):
    x_low, x_high = from_swaps("fx", x_first[8:16, :], x_second[8:16, :])
    y_low, y_high = from_swaps("fy", y_first[8:16, :], y_second[8:16, :])
    low, high, halo = [
        eight(row[6:7]) for row in (x_low, x_high, halo_of(y_low, y_high))
    ]
    nodes = [eight(mass[n : n + 1, :]) for n in range(NODES)]
    nodes = summed_nodes(nodes, low, high)
    nodes = [1.0 / with_halo(n, node, halo) for n, node in enumerate(nodes)]
    for n in range(NODES):
        inverse[n : n + 1, :] = nodes[n][0:1]
    on_faces[...] = faces(lambda n, t: nodes[n][:, t * 128 : (t + 1) * 128])[1]


def sum_body(weighted, x_first, x_second, inverse, result, table=None):
    low, high = from_swaps("fx", x_first[...], x_second[...])
    nodes = summed_nodes([weighted[:, n * E : (n + 1) * E] for n in range(NODES)], low, high)
    for n in range(NODES):
        node = nodes[n] * inverse[n : n + 1, :]
        result[:, n * E : (n + 1) * E] = node
        if table is not None:
            high_part, low_part = halves(node)
            table[n * F : (n + 1) * F, 0:E] = high_part
            table[n * F : (n + 1) * F, E : 2 * E] = low_part


def finish_body(summed, y_first, y_second, scale, table):
    halo = halo_of(*from_swaps("fy", y_first[...], y_second[...])) * scale[0:1, :]
    for n in range(NODES):
        node = with_halo(n, summed[:, n * E : (n + 1) * E], halo)
        high, low = halves(node)
        table[n * F : (n + 1) * F, 0:E] = high
        table[n * F : (n + 1) * F, E : 2 * E] = low


FACE_NODES = tuple(n for n in range(NODES) if n % 4 in (0, 3))
INNER_NODES = tuple(n for n in range(NODES) if n % 4 in (1, 2))


def inner_body(weighted, x_first, x_second, inverse, part, result, block, sems):
    low, high = from_swaps("fx", x_first[...], x_second[...])
    nodes = summed_nodes([weighted[:, n * E : (n + 1) * E] for n in range(NODES)], low, high)
    copies = []
    for i, n in enumerate(INNER_NODES):
        block[i] = nodes[n] * inverse[n : n + 1, :]
        copy = pltpu.make_async_copy(block.at[i], result.at[:, n, :], sems.at[i])
        copy.start()
        copies.append(copy)
    for i, n in enumerate(FACE_NODES):
        part[:, i * E : (i + 1) * E] = nodes[n] * inverse[n : n + 1, :]
    for copy in copies:
        copy.wait()


def last_body(part, y_first, y_second, scale, begun, result, block, sems):
    halo = halo_of(*from_swaps("fy", y_first[...], y_second[...])) * scale[0:1, :]
    copies = []
    for i, n in enumerate(FACE_NODES):
        block[i] = with_halo(n, part[:, i * E : (i + 1) * E], halo)
        copy = pltpu.make_async_copy(block.at[i], result.at[:, n, :], sems.at[i])
        copy.start()
        copies.append(copy)
    for copy in copies:
        copy.wait()


def per_device(tracers, node_mass, point_order, offsets, source, coords):
    ask = shape((24, 128))
    answers = shape((3 * F, 128))
    face = shape((F, 128))
    table_shape = shape((NODES * F, 2 * E), BF16)
    lists = [
        pltpu.SMEM(offsets.shape, jnp.int32),
        pltpu.VMEM(source.shape, jnp.int32),
        pltpu.VMEM(coords.shape, jnp.int32),
    ]
    first, second, mid, mass_faces = call(
        asks_body,
        [ask, ask, ask, shape((8, 256))],
        "asks",
        hbm=(0, 1, 2, 3),
        count=4,
        scratch=lists
        + [
            pltpu.VMEM(node_mass.shape, F32),
            pltpu.VMEM((8, POINTS), F32),
            pltpu.VMEM((72, 128), F32),
            pltpu.SemaphoreType.DMA((4,)),
        ],
    )(*[in_hbm(a) for a in (offsets, source, coords, node_mass)])
    asked = swap("fx", first, second)
    requests = [shape((2, TILES, 128)), shape((NODES + 8, TILES, 128)), shape((8, 256))]
    *now, later, later_starts = call(
        order_body,
        requests + [shape((8, POINTS), jnp.int32), shape((8, 128), jnp.int32)],
        "order",
        hbm=(0, 1, 2, 3),
        count=4,
        scratch=[pltpu.VMEM(a.shape, jnp.int32) for a in (offsets, point_order, source, coords)]
        + [pltpu.SemaphoreType.DMA((4,))],
    )(*[in_hbm(a) for a in (offsets, point_order, source, coords)])
    ordered_lists = [now]

    def interpolate(s, piece, after=0):
        begin, end = PIECES[s][piece]
        return call(
            lambda *refs: own_body(begin, *refs),
            shape((F, (end - begin) * E)),
            "own",
            count=3,
            after=after,
        )

    column_far, column_near, column_kept = call(column_body, [ask] * 3, "column", count=4)(
        *asked, mid, mass_faces
    )
    asked += swap("fy", column_far, column_near)
    table = call(
        table_body,
        table_shape,
        "table",
        hbm=(0,),
        count=1,
        scratch=[pltpu.VMEM(tracers.shape, F32), pltpu.SemaphoreType.DMA((1,))],
    )(in_hbm(tracers))
    far, near = call(reply_y_body, [answers] * 2, "reply_y", count=3, after=1)(
        table, asked[2], asked[3], now[2]
    )
    answers_y = swap("fy", far, near)
    inverse, scale = call(scale_body, [shape((NODES, E)), shape((8, 128))], "scale", count=5)(
        node_mass, *asked
    )
    for s in range(SUBSTEPS):
        picks, factors, face_picks = ordered_lists[s]
        if s == 1:
            table = call(finish_body, table_shape, "finish", count=4)(summed, *edges_y, scale)
        own = call(
            lambda *refs, s=s: reply_x_body(s, *refs), shape((2 * F, 128)), "reply_x", count=5
        )(table, *asked)
        own_faces = call(own_faces_body, shape((F, 256)), "own_faces", count=2)(table, face_picks)
        own_a = interpolate(s, 0)(table, picks, factors)
        near_sent, far_sent = call(row_body, [answers] * 2, "row", count=3, after=3)(
            *answers_y, own, own_a, scale, own_faces
        )
        near = swap_near("fx", near_sent)
        far = swap_far("fx", far_sent)
        partial, message = call(
            face_near_body, [shape((F, 256)), shape((F + 8, 128))], "faces_near", count=6
        )(own_faces, near, *answers_y, face_picks, mass_faces)
        faces_in = swap_far("fx", message)
        own_b = interpolate(s, 1, after=1)(table, picks, factors, partial)
        if s == 0:
            ordered_lists.append(
                call(later_body, requests, "order", count=2, after=1)(
                    later, later_starts, partial
                )
            )
        along_x, along_y, other = call(
            face_far_body, [face] * 3, "faces_far", count=6, after=2
        )(partial, far, faces_in, far_sent, face_picks, mass_faces, own_b, ordered_lists[1][2])
        edges_x = (other, swap_near("fx", along_x))
        place = call(
            lambda *refs, s=s: place_body(s, *refs),
            shape((F, POINTS)),
            "place",
            count=9,
            after=1,
        )
        moved = (own_a, own_b, far, near, *answers_y, picks, factors, node_mass)
        if s == 0:
            weighted = place(*moved, other)
            rims_far, rims_near, rims_kept = call(rim_body, [face] * 3, "rim", count=3, after=1)(
                along_y, *edges_x, weighted
            )
        else:
            rims_far, rims_near = call(rim_body, [face] * 2, "rim", count=3)(along_y, *edges_x)
            weighted = place(*moved, rims_near)
        edges_y = swap("fy", rims_far, rims_near)
        if s == 0:
            summed, *early = call(
                between_body,
                [
                    shape((F, POINTS)),
                    shape((6, F, 128)),
                    shape((8, 128), jnp.int32),
                    shape((4, 8, 128)),
                ],
                "between",
                count=6,
                scratch=[pltpu.VMEM((NODES * F, 2 * E), BF16)],
            )(weighted, *edges_x, inverse, asked[2], asked[3])
            far = call(late_far_body, answers, "late_far", count=5)(*early, edges_y[1], scale)
            far = swap_far("fy", far)
            near = call(late_near_body, answers, "late_near", count=6)(*early, *edges_y, scale)
            near = swap_near("fy", near)
            far = call(fix_body, answers, "fix", count=4)(far, column_kept, rims_kept, scale)
            answers_y = (far, near)
        else:
            scratch = [pltpu.VMEM((8, F, E), F32), pltpu.SemaphoreType.DMA((8,))]
            vmem = pl.BlockSpec(memory_space=pltpu.VMEM)
            hbm = pl.BlockSpec(memory_space=pltpu.HBM)
            params = pltpu.CompilerParams(vmem_limit_bytes=VMEM_LIMIT)
            part, begun = pl.pallas_call(
                inner_body,
                out_shape=[shape((F, 8 * E)), shape((F, NODES, E))],
                in_specs=[vmem] * 4,
                out_specs=[vmem, hbm],
                scratch_shapes=scratch,
                name="inner",
                compiler_params=params,
            )(weighted, *edges_x, inverse)
            result = pl.pallas_call(
                last_body,
                out_shape=shape((F, NODES, E)),
                in_specs=[vmem] * 4 + [hbm],
                out_specs=hbm,
                scratch_shapes=scratch,
                input_output_aliases={4: 0},
                name="last",
                compiler_params=params,
            )(part, *edges_y, scale, begun)
    return result


def solution(mesh):
    return jax.shard_map(
        per_device,
        mesh=mesh,
        in_specs=(
            P(None, None, ("fx", "fy")),
            P(None, ("fx", "fy")),
            P(None, ("fx", "fy"), None),
            P(None, ("fx", "fy"), None),
            P(None, ("fx", "fy")),
            P(None, None, ("fx", "fy")),
        ),
        out_specs=P(None, None, ("fx", "fy")),
        check_vma=False,
    )
```

```python
import jax
import jax.numpy as jnp
from jax import lax
from jax.experimental import pallas as pl
from jax.experimental.pallas import tpu as pltpu
from jax.sharding import PartitionSpec as P

TX = 16
CAP = 128
QGRID = 1024
SUBSTEPS = 2
F = 64
E = 256
NODES = 16
POINTS = 4096
TILES = POINTS // 128
PIECES = (((0, 9), (9, 16)), ((0, 8), (8, 16)))
GLL_NODES = (-1.0, -0.4472135954999579, 0.4472135954999579, 1.0)
REMOTE = (0, 1, 2, 3, 5, 6, 7, 8)
BF16 = jnp.bfloat16
F32 = jnp.float32
VMEM_LIMIT = 40 * 2**20


def call(body, out_shape, name, hbm=(), count=0, after=0, scratch=()):
    specs = [
        pl.BlockSpec(memory_space=pltpu.HBM if i in hbm else pltpu.VMEM) for i in range(count)
    ] + [pl.BlockSpec(memory_space=pl.ANY)] * after

    def kernel(*refs):
        body(*refs[:count], *refs[count + after :])

    return pl.pallas_call(
        kernel,
        out_shape=out_shape,
        in_specs=specs,
        scratch_shapes=scratch,
        name=name,
        compiler_params=pltpu.CompilerParams(vmem_limit_bytes=VMEM_LIMIT),
    )


def in_hbm(array):
    return pltpu.with_memory_space_constraint(array, pltpu.HBM)


def shape(dims, dtype=F32):
    return jax.ShapeDtypeStruct(dims, dtype)


def swap_far(axis, block):
    size = lax.axis_size(axis)
    pairs = [(i, (((i + size - 1) % size ^ 1) + 1) % size) for i in range(size)]
    return lax.ppermute(block, axis, pairs)


def swap_near(axis, block):
    return lax.ppermute(block, axis, [(i, i ^ 1) for i in range(lax.axis_size(axis))])


def swap(axis, far, near):
    return swap_far(axis, far), swap_near(axis, near)


def to_swaps(axis, low, high):
    even = lax.axis_index(axis) % 2 == 0
    return jnp.where(even, low, high), jnp.where(even, high, low)


def from_swaps(axis, first, second):
    even = lax.axis_index(axis) % 2 == 0
    return jnp.where(even, first, second), jnp.where(even, second, first)


def lagrange(step):
    x = step * (2.0 / QGRID) - 1.0
    rows = []
    for a in range(4):
        factor = None
        for b in range(4):
            if b != a:
                term = (x - GLL_NODES[b]) * (1.0 / (GLL_NODES[a] - GLL_NODES[b]))
                factor = term if factor is None else factor * term
        rows.append(factor)
    return rows


def halves(block):
    high = block.astype(BF16)
    return high, (block - high.astype(F32)).astype(BF16)


def one_hot(index_rows, depth):
    rows = lax.broadcasted_iota(jnp.int32, (depth, 128), 0).astype(F32).astype(BF16)
    parts = [jnp.where(rows == r.astype(BF16), BF16(1), BF16(0)) for r in index_rows]
    return jnp.concatenate(parts, axis=1)


def lane_index(rows):
    return lax.broadcasted_iota(jnp.int32, (rows, 128), 1)


def eight(row):
    return jnp.broadcast_to(row, (8, row.shape[1]))


def pick_lanes(block, index):
    return jnp.take_along_axis(block, index, axis=1, mode="promise_in_bounds")


def faces(tile):
    rows = tile(0, 0).shape[0]
    lane = lane_index(rows)
    along_x = jnp.zeros((rows, 128), F32)
    for b in range(4):
        along_x = jnp.where(lane // 16 == b, pltpu.roll(tile(b, 0), b * 16, 1), along_x)
        shifted = pltpu.roll(tile(12 + b, 1), (b * 16 + 80) % 128, 1)
        along_x = jnp.where(lane // 16 == b + 4, shifted, along_x)
    along_y = jnp.zeros((rows, 128), F32)
    index = (lane % 8) * 16
    for a in range(4):
        for t in range(2):
            here = ((lane % 64) // 16 == a) & ((lane % 16) // 8 == t)
            first = pick_lanes(tile(4 * a, t), index)
            last = pick_lanes(tile(4 * a + 3, t), index + 15)
            along_y = jnp.where(here, jnp.where(lane < 64, first, last), along_y)
    return along_x, along_y


def summed_faces(own, low, high):
    lane = lane_index(own.shape[0])
    place = lane % 64
    behind = pltpu.roll(own, 128 - 48 + 1, 1)
    ahead = pltpu.roll(own, 48 - 1, 1)
    behind = jnp.where(lane == 0, low[:, 64:65], jnp.where(lane == 64, low[:, 127:128], behind))
    ahead = jnp.where(lane == 63, high[:, 0:1], jnp.where(lane == 127, high[:, 63:64], ahead))
    return own + jnp.where(place < 16, behind, jnp.where(place >= 48, ahead, 0.0))


def summed_nodes(nodes, low, high):
    rows = nodes[0].shape[0]
    lane = lane_index(rows)
    wide = lax.broadcasted_iota(jnp.int32, (rows, E), 1)
    nodes = list(nodes)
    for b in range(4):
        first, last = nodes[b], nodes[12 + b]
        behind = pltpu.roll(last, 16, 1)
        ahead = pltpu.roll(first, E - 16, 1)
        from_low = pltpu.roll(low, (128 - 64 - 16 * b) % 128, 1)
        from_high = pltpu.roll(high, 112 - 16 * b, 1)
        behind = jnp.concatenate(
            [jnp.where(lane < 16, from_low, behind[:, :128]), behind[:, 128:]], axis=1
        )
        ahead = jnp.concatenate(
            [ahead[:, :128], jnp.where(lane >= 112, from_high, ahead[:, 128:])], axis=1
        )
        nodes[b] = first + behind
        nodes[12 + b] = last + ahead
    for a in range(4):
        first, last = nodes[4 * a], nodes[4 * a + 3]
        behind = jnp.where(wide % 16 == 0, 0.0, pltpu.roll(last, 1, 1))
        ahead = jnp.where(wide % 16 == 15, 0.0, pltpu.roll(first, E - 1, 1))
        nodes[4 * a] = first + behind
        nodes[4 * a + 3] = last + ahead
    return nodes


def halo_of(low, high):
    lane = lane_index(low.shape[0])
    return pltpu.roll(jnp.where(lane >= 64, low, high), 64, 1)


def with_halo(n, node, halo):
    if n % 4 not in (0, 3):
        return node
    rows = node.shape[0]
    lane = lane_index(rows)
    wide = lax.broadcasted_iota(jnp.int32, (rows, E), 1)
    start = 16 * (n // 4) + (64 if n % 4 == 3 else 0)
    spread = [pick_lanes(halo, start + 8 * t + lane // 16) for t in range(2)]
    at = 15 if n % 4 == 3 else 0
    return node + jnp.where(wide % 16 == at, jnp.concatenate(spread, axis=1), 0.0)


def fetch(pairs, sems):
    copies = [pltpu.make_async_copy(*pair, sems.at[i]) for i, pair in enumerate(pairs)]
    for copy in copies:
        copy.start()
    for copy in copies:
        copy.wait()


def asks_body(
    offsets_in, source_in, coords_in, mass_in, first, second, mid, mass_faces,
    offsets, source, coords, mass, rows, message, sems,
):
    fetch(
        [(offsets_in, offsets), (source_in, source), (coords_in, coords), (mass_in, mass)], sems
    )
    for s in range(SUBSTEPS):
        rows[3 * s : 3 * s + 1, :] = source[s : s + 1, :].astype(F32)
        rows[3 * s + 1 : 3 * s + 3, :] = coords[s].astype(F32)
    rows[6:8, :] = jnp.zeros((2, POINTS), F32)
    early = lax.broadcasted_iota(jnp.int32, (8, 128), 0) < 3
    for k in REMOTE:
        parts = []
        for s in range(SUBSTEPS):
            start = offsets[s, 0, k]
            tile = jnp.minimum(start // 128, TILES - 1)
            after = jnp.minimum(tile + 1, TILES - 1)
            wide = jnp.concatenate(
                [rows[:, pl.ds(pl.multiple_of(t * 128, 128), 128)] for t in (tile, after)], axis=1
            )
            parts.append(pltpu.roll(wide, 256 - (start - tile * 128), 1)[:, 0:128])
        message[k * 8 : (k + 1) * 8, :] = jnp.where(early, parts[0], parts[1])
    along_x, along_y = faces(lambda n, t: eight(mass[n : n + 1, t * 128 : (t + 1) * 128]))
    for k in (1, 7):
        message[k * 8 + 6 : k * 8 + 7, :] = along_x[0:1]
    mass_faces[:, 0:128] = along_x
    mass_faces[:, 128:256] = along_y
    message[32:40, :] = jnp.zeros((8, 128), F32)
    first[...], second[...] = to_swaps("fx", message[0:24, :], message[48:72, :])
    mid[...] = message[24:48, :]


def order_body(
    offsets_in, order_in, source_in, coords_in, picks, factors, face_picks, later, later_starts,
    offsets, order, source, coords, sems,
):
    fetch(
        [(offsets_in, offsets), (order_in, order), (source_in, source), (coords_in, coords)], sems
    )
    ordered(
        order[0], source[0:1], coords[0, 0:1], coords[0, 1:2], offsets[0], picks, factors, face_picks
    )
    later[0:1, :] = order[1]
    later[1:2, :] = source[1:2, :]
    later[2:4, :] = coords[1]
    later_starts[0:1, 0:10] = offsets[1]


def later_body(lists, starts, picks, factors, face_picks):
    ordered(
        lists[0:1], lists[1:2], lists[2:3], lists[3:4], starts[0:1], picks, factors, face_picks
    )


def ordered(nodes, sources, xs, ys, starts, picks, factors, face_picks):
    chunk = 1024
    total = None
    for c in range(POINTS // chunk):
        lanes = slice(c * chunk, (c + 1) * chunk)
        node = nodes[:, lanes]
        tile_of = (node // 128).astype(F32).astype(BF16)
        lane_of = (node % 128).astype(F32).astype(BF16)
        position = lax.broadcasted_iota(jnp.int32, (1, chunk), 1) + c * chunk
        run = jnp.zeros((1, chunk), jnp.int32)
        begin = jnp.broadcast_to(starts[:, 0:1], (1, chunk))
        for k in range(1, 9):
            start = jnp.broadcast_to(starts[:, k : k + 1], (1, chunk))
            passed = position >= start
            run = run + passed.astype(jnp.int32)
            begin = jnp.where(passed, start, begin)
        own = run == 4
        kind = jnp.where(own, 8, jnp.where(run > 4, run - 1, run))
        pick = jnp.where(own, sources[:, lanes], position - begin)
        cx = xs[:, lanes]
        cy = ys[:, lanes]
        values = [pick, cx // 8, cx % 8, cy // 8, cy % 8, kind]
        tiles = lax.broadcasted_iota(jnp.int32, (TILES, chunk), 0).astype(F32).astype(BF16)
        here = tiles == tile_of
        left = jnp.concatenate(
            [jnp.where(here, v.astype(F32).astype(BF16), BF16(0)) for v in values], axis=0
        )
        spots = lax.broadcasted_iota(jnp.int32, (128, chunk), 0).astype(F32).astype(BF16)
        right = jnp.where(spots == lane_of, BF16(1), BF16(0))
        part = lax.dot_general(left, right, (((1,), (1,)), ((), ())), preferred_element_type=F32)
        total = part if total is None else total + part
    pick, xh, xl, yh, yl, kind = [total[q * TILES : (q + 1) * TILES] for q in range(6)]
    own = kind > 7.5
    picks[0] = jnp.where(own, pick, -1.0)
    picks[1] = jnp.where(own, -1.0, pick)
    mask = jnp.where(own, 1.0, 0.0)
    along_x = [row * mask for row in lagrange(xh * 8.0 + xl)]
    along_y = lagrange(yh * 8.0 + yl)
    for n in range(NODES):
        factors[n] = along_x[n // 4] * along_y[n % 4]
    for d in range(8):
        factors[NODES + d] = jnp.where(jnp.abs(kind - d) < 0.5, 1.0, 0.0)
    for q, rows in enumerate((picks[1], kind, picks[0], xh * 8.0 + xl, yh * 8.0 + yl)):
        along = faces(lambda n, t: eight(rows[2 * n + t : 2 * n + t + 1]))
        face_picks[q : q + 1, :] = jnp.concatenate(along, axis=1)[0:1]


def table_body(tracers_in, table, tracers, sems):
    fetch([(tracers_in, tracers)], sems)
    for q in range(0, F, 16):
        block = jnp.swapaxes(tracers[q : q + 16], 0, 1)
        for n in range(NODES):
            high, low = halves(block[n])
            table[n * F + q : n * F + q + 16, 0:E] = high
            table[n * F + q : n * F + q + 16, E : 2 * E] = low


def column_body(x_first, x_second, mid, mass_faces, first, second, kept):
    low, high = from_swaps("fx", x_first[...], x_second[...])
    masses = summed_faces(mass_faces[:, 128:256], low[8:16], high[8:16])[6:7]
    rows = lax.broadcasted_iota(jnp.int32, (8, 128), 0)
    columns = []
    for k in (0, 2):
        block = slice(k * 8, (k + 1) * 8)
        center = jnp.where(rows == 6, masses, mid[block, :])
        columns.append(jnp.concatenate([high[block], center, low[block]], axis=0))
    first[...], second[...] = to_swaps("fy", *columns)
    kept[...] = first[...]


def row_body(y_first, y_second, own, near, far):
    low, high = from_swaps("fy", y_first[...], y_second[...])
    mine = own[...]
    ahead = jnp.concatenate([low[0:F], mine[0:F], high[0:F]], axis=0)
    behind = jnp.concatenate([low[2 * F :], mine[F:], high[2 * F :]], axis=0)
    far[...], near[...] = to_swaps("fx", behind, ahead)


def combine(products, weights):
    total = None
    for n, weight in enumerate(weights):
        term = products[n * F : (n + 1) * F] * weight
        total = term if total is None else total + term
    return total


def asked_blocks(x_first, x_second, y_first, y_second):
    x_low, x_high = from_swaps("fx", x_first[...], x_second[...])
    y_low, y_high = from_swaps("fy", y_first[...], y_second[...])
    by_direction = {(1, 0): x_low[8:16], (-1, 0): x_high[8:16]}
    for k in range(3):
        by_direction[(k - 1, 1)] = y_low[k * 8 : (k + 1) * 8]
        by_direction[(k - 1, -1)] = y_high[k * 8 : (k + 1) * 8]
    return [by_direction[(k // 3 - 1, k % 3 - 1)] for k in REMOTE]


def asked_rows(s, asked):
    return [
        jnp.concatenate([r[s * 3 + q : s * 3 + q + 1, :] for r in asked], axis=0) for q in range(3)
    ]


def weights_of(cx, cy):
    along_x = lagrange(cx)
    along_y = lagrange(cy)
    return [along_x[n // 4] * along_y[n % 4] for n in range(NODES)]


def answer(table, pick, weights, directions):
    values = {}
    for both in directions:
        hot = one_hot([pick[d : d + 1] for d in both], E)
        products = jnp.dot(
            table[...], jnp.concatenate([hot, hot], axis=0), preferred_element_type=F32
        )
        for h, d in enumerate(both):
            lanes = slice(h * 128, (h + 1) * 128)
            values[d] = combine(products[:, lanes], [w[d : d + 1] for w in weights])
    return values


BEHIND = (2, 4, 7)
AHEAD = (0, 3, 5)
SIDES = (1, 6)


def partner_rows(s, asked):
    return [
        jnp.concatenate([asked[k * 8 + 3 * s + q : k * 8 + 3 * s + q + 1, :] for k in range(3)], axis=0)
        for q in range(3)
    ]


def partners_rows(s, far, near):
    pairs = zip(partner_rows(s, far), partner_rows(s, near))
    return [jnp.concatenate(pair, axis=0) for pair in pairs]


def reply_y_body(table, asked_far, asked_near, far, near):
    pick, cx, cy = partners_rows(0, asked_far, asked_near)
    values = answer(table, pick, weights_of(cx, cy), ((0, 1), (2, 3), (4, 5)))
    for k in range(3):
        far[k * F : (k + 1) * F, :] = values[k]
        near[k * F : (k + 1) * F, :] = values[3 + k]


def reply_x_body(s, table, x_first, x_second, y_first, y_second, own):
    pick, cx, cy = asked_rows(s, asked_blocks(x_first, x_second, y_first, y_second))
    values = answer(table, pick, weights_of(cx, cy), (SIDES,))
    for k, d in enumerate(SIDES):
        own[k * F : (k + 1) * F, :] = values[d]


def between_body(
    weighted, x_first, x_second, inverse, asked_far, asked_near, summed, values, lanes, shares, table
):
    sum_body(weighted, x_first, x_second, inverse, summed, table)
    pick, cx, cy = partners_rows(1, asked_far, asked_near)
    weights = weights_of(cx, cy)
    for d, value in answer(table, pick, weights, ((0, 1), (2, 3), (4, 5))).items():
        values[d] = value
    element = pick.astype(jnp.int32)
    lanes[0:6, :] = element // 16 + jnp.where(element % 16 == 15, 64, 0)
    for a in range(4):
        share = jnp.where(element % 16 == 15, weights[4 * a + 3], 0.0)
        shares[a, 0:6, :] = jnp.where(element % 16 == 0, weights[4 * a], share)


def shared(values, lanes, shares, halo, start, message):
    for k in range(3):
        d = start + k
        index = jnp.broadcast_to(lanes[d : d + 1, :], (F, 128))
        value = values[d]
        for a in range(4):
            value = value + pick_lanes(halo, index + 16 * a) * shares[a, d : d + 1, :]
        message[k * F : (k + 1) * F, :] = value


def late_far_body(values, lanes, shares, near, scale, message):
    even = lax.axis_index("fy") % 2 == 0
    block = pltpu.roll(near[...], 64, 1) * scale[0:1, :]
    lane = lane_index(F)
    halo = jnp.where(jnp.where(even, lane - 64, 63 - lane) >= 0, block, 0.0)
    shared(values, lanes, shares, halo, 0, message)


def late_near_body(values, lanes, shares, far, near, scale, message):
    halo = halo_of(*from_swaps("fy", far[...], near[...])) * scale[0:1, :]
    shared(values, lanes, shares, halo, 3, message)


def fix_body(far, asked, rims, scale, result):
    even = lax.axis_index("fy") % 2 == 0
    pick, cx, cy = partner_rows(1, asked)
    weights = weights_of(cx, cy)
    element = pick.astype(jnp.int32)
    on_face = element % 16 == jnp.where(even, 15, 0)
    lanes = element // 16 + jnp.where(even, 0, 64)
    own = rims[...] * scale[0:1, :]
    for k in range(3):
        index = jnp.broadcast_to(lanes[k : k + 1], (F, 128))
        value = far[k * F : (k + 1) * F, :]
        for a in range(4):
            weight = jnp.where(even, weights[4 * a + 3], weights[4 * a])
            weight = jnp.where(on_face, weight, 0.0)
            value = value + pick_lanes(own, index + 16 * a) * weight[k : k + 1]
        result[k * F : (k + 1) * F, :] = value


def own_body(begin, table, picks, factors, result):
    def block(i, carry):
        at = 2 * (begin + i)
        hot = one_hot([picks[0, pl.ds(at + h, 1), :] for h in range(2)], E)
        products = jnp.dot(
            table[...], jnp.concatenate([hot, hot], axis=0), preferred_element_type=F32
        )
        weights = [
            jnp.concatenate([factors[n, pl.ds(at + h, 1), :] for h in range(2)], axis=1)
            for n in range(NODES)
        ]
        result[:, pl.ds(pl.multiple_of(i * E, E), E)] = combine(products, weights)
        return carry

    count = result.shape[1] // E
    lax.fori_loop(0, count, block, 0, unroll=3 if count == 9 else 4 if count == 8 else count)


def stacked(blocks):
    return jnp.concatenate([jnp.concatenate(halves(block), axis=1) for block in blocks], axis=0)


def three(ref):
    return [ref[k * F : (k + 1) * F, :] for k in range(3)]


def middles(y_first, y_second):
    return list(from_swaps("fy", y_first[F : 2 * F, :], y_second[F : 2 * F, :]))


def arrived(x_first, x_second, y_first, y_second):
    even = lax.axis_index("fx") % 2 == 0
    pairs = list(zip(three(x_first), three(x_second)))
    low = [jnp.where(even, far, near) for far, near in pairs]
    high = [jnp.where(even, near, far) for far, near in pairs]
    return stacked(low + middles(y_first, y_second) + high)


def placed(answers, slots, masks):
    hot = one_hot(slots, CAP)
    products = jnp.dot(answers, jnp.concatenate([hot, hot], axis=0), preferred_element_type=F32)
    return combine(products, masks)


def masks_of(kind, bases):
    return [jnp.where(jnp.abs(kind - base) < 0.5, 1.0, 0.0) for base in bases]


def kinds(even, near):
    start = jnp.where(even == near, 5.0, 0.0)
    return [start + k for k in range(3)]


def face_slots(face_picks):
    return [face_picks[0:1, h * 128 : (h + 1) * 128] for h in range(2)]


def own_faces_body(table, face_picks, result):
    hot = one_hot([face_picks[2:3, h * 128 : (h + 1) * 128] for h in range(2)], E)
    products = jnp.dot(table[...], jnp.concatenate([hot, hot], axis=0), preferred_element_type=F32)
    result[...] = combine(products, weights_of(face_picks[3:4, :], face_picks[4:5, :]))


def face_near_body(
    own, near, y_first, y_second, face_picks, mass_faces, partial, message
):
    even = lax.axis_index("fx") % 2 == 0
    masks = masks_of(face_picks[1:2, :], kinds(even, True) + [3.0, 4.0])
    answers = stacked(three(near) + middles(y_first, y_second))
    moved = own[...] + placed(answers, face_slots(face_picks), masks)
    moved = moved * mass_faces[0:1, :]
    partial[...] = moved
    message[0:F, :] = moved[:, 0:128]
    message[F : F + 8, :] = face_picks[:, 0:128]
    message[F + 2 : F + 3, :] = mass_faces[0:1, 0:128]


def face_far_body(partial, far, faces_in, sent, face_picks, mass_faces, along_x, along_y, other):
    even = lax.axis_index("fx") % 2 == 0
    masks = masks_of(face_picks[1:2, :], kinds(even, False))
    moved = placed(stacked(three(far)), face_slots(face_picks), masks) * mass_faces[0:1, :]
    result = partial[...] + moved
    along_x[...] = result[:, 0:128]
    along_y[...] = result[:, 128:256]
    slot, kind, weight = [faces_in[F + q : F + q + 1, :] for q in range(3)]
    moved = placed(stacked(three(sent)), [slot], masks_of(kind, kinds(even, True)))
    other[...] = faces_in[0:F, :] + moved * weight


def place_body(
    s, own_a, own_b, x_first, x_second, y_first, y_second, picks, factors, mass, result
):
    answers = arrived(x_first, x_second, y_first, y_second)
    for n in range(NODES):
        tiles = [slice(2 * n + h, 2 * n + h + 1) for h in range(2)]
        masks = [
            jnp.concatenate([factors[NODES + d, t, :] for t in tiles], axis=1) for d in range(8)
        ]
        moved = placed(answers, [picks[1, t, :] for t in tiles], masks)
        for ref, (begin, end) in zip((own_a, own_b), PIECES[s]):
            if begin <= n < end:
                own = ref[:, (n - begin) * E : (n - begin + 1) * E]
        result[:, n * E : (n + 1) * E] = (own + moved) * mass[n : n + 1, :]


def rim_body(along_y, x_first, x_second, *results):
    low, high = from_swaps("fx", x_first[...], x_second[...])
    result = summed_faces(along_y[...], low, high)
    for ref in results:
        ref[...] = result


def scale_body(mass, x_first, x_second, y_first, y_second, inverse, on_faces):
    x_low, x_high = from_swaps("fx", x_first[8:16, :], x_second[8:16, :])
    y_low, y_high = from_swaps("fy", y_first[8:16, :], y_second[8:16, :])
    low, high, halo = [
        eight(row[6:7]) for row in (x_low, x_high, halo_of(y_low, y_high))
    ]
    nodes = [eight(mass[n : n + 1, :]) for n in range(NODES)]
    nodes = summed_nodes(nodes, low, high)
    nodes = [1.0 / with_halo(n, node, halo) for n, node in enumerate(nodes)]
    for n in range(NODES):
        inverse[n : n + 1, :] = nodes[n][0:1]
    on_faces[...] = faces(lambda n, t: nodes[n][:, t * 128 : (t + 1) * 128])[1]


def sum_body(weighted, x_first, x_second, inverse, result, table=None):
    low, high = from_swaps("fx", x_first[...], x_second[...])
    nodes = summed_nodes([weighted[:, n * E : (n + 1) * E] for n in range(NODES)], low, high)
    for n in range(NODES):
        node = nodes[n] * inverse[n : n + 1, :]
        result[:, n * E : (n + 1) * E] = node
        if table is not None:
            high_part, low_part = halves(node)
            table[n * F : (n + 1) * F, 0:E] = high_part
            table[n * F : (n + 1) * F, E : 2 * E] = low_part


def finish_body(summed, y_first, y_second, scale, table):
    halo = halo_of(*from_swaps("fy", y_first[...], y_second[...])) * scale[0:1, :]
    for n in range(NODES):
        node = with_halo(n, summed[:, n * E : (n + 1) * E], halo)
        high, low = halves(node)
        table[n * F : (n + 1) * F, 0:E] = high
        table[n * F : (n + 1) * F, E : 2 * E] = low


FACE_NODES = tuple(n for n in range(NODES) if n % 4 in (0, 3))
INNER_NODES = tuple(n for n in range(NODES) if n % 4 in (1, 2))


def inner_body(weighted, x_first, x_second, inverse, part, result, block, sems):
    low, high = from_swaps("fx", x_first[...], x_second[...])
    nodes = summed_nodes([weighted[:, n * E : (n + 1) * E] for n in range(NODES)], low, high)
    copies = []
    for i, n in enumerate(INNER_NODES):
        block[i] = nodes[n] * inverse[n : n + 1, :]
        copy = pltpu.make_async_copy(block.at[i], result.at[:, n, :], sems.at[i])
        copy.start()
        copies.append(copy)
    for i, n in enumerate(FACE_NODES):
        part[:, i * E : (i + 1) * E] = nodes[n] * inverse[n : n + 1, :]
    for copy in copies:
        copy.wait()


def last_body(part, y_first, y_second, scale, begun, result, block, sems):
    halo = halo_of(*from_swaps("fy", y_first[...], y_second[...])) * scale[0:1, :]
    copies = []
    for i, n in enumerate(FACE_NODES):
        block[i] = with_halo(n, part[:, i * E : (i + 1) * E], halo)
        copy = pltpu.make_async_copy(block.at[i], result.at[:, n, :], sems.at[i])
        copy.start()
        copies.append(copy)
    for copy in copies:
        copy.wait()


def per_device(tracers, node_mass, point_order, offsets, source, coords):
    ask = shape((24, 128))
    answers = shape((3 * F, 128))
    face = shape((F, 128))
    table_shape = shape((NODES * F, 2 * E), BF16)
    lists = [
        pltpu.SMEM(offsets.shape, jnp.int32),
        pltpu.VMEM(source.shape, jnp.int32),
        pltpu.VMEM(coords.shape, jnp.int32),
    ]
    first, second, mid, mass_faces = call(
        asks_body,
        [ask, ask, ask, shape((8, 256))],
        "asks",
        hbm=(0, 1, 2, 3),
        count=4,
        scratch=lists
        + [
            pltpu.VMEM(node_mass.shape, F32),
            pltpu.VMEM((8, POINTS), F32),
            pltpu.VMEM((72, 128), F32),
            pltpu.SemaphoreType.DMA((4,)),
        ],
    )(*[in_hbm(a) for a in (offsets, source, coords, node_mass)])
    asked = swap("fx", first, second)
    requests = [shape((2, TILES, 128)), shape((NODES + 8, TILES, 128)), shape((8, 256))]
    *now, later, later_starts = call(
        order_body,
        requests + [shape((8, POINTS), jnp.int32), shape((8, 128), jnp.int32)],
        "order",
        hbm=(0, 1, 2, 3),
        count=4,
        scratch=[pltpu.VMEM(a.shape, jnp.int32) for a in (offsets, point_order, source, coords)]
        + [pltpu.SemaphoreType.DMA((4,))],
    )(*[in_hbm(a) for a in (offsets, point_order, source, coords)])
    ordered_lists = [now]

    def interpolate(s, piece, after=0):
        begin, end = PIECES[s][piece]
        return call(
            lambda *refs: own_body(begin, *refs),
            shape((F, (end - begin) * E)),
            "own",
            count=3,
            after=after,
        )

    column_far, column_near, column_kept = call(column_body, [ask] * 3, "column", count=4)(
        *asked, mid, mass_faces
    )
    asked += swap("fy", column_far, column_near)
    table = call(
        table_body,
        table_shape,
        "table",
        hbm=(0,),
        count=1,
        scratch=[pltpu.VMEM(tracers.shape, F32), pltpu.SemaphoreType.DMA((1,))],
    )(in_hbm(tracers))
    far, near = call(reply_y_body, [answers] * 2, "reply_y", count=3, after=1)(
        table, asked[2], asked[3], now[2]
    )
    answers_y = swap("fy", far, near)
    inverse, scale = call(scale_body, [shape((NODES, E)), shape((8, 128))], "scale", count=5)(
        node_mass, *asked
    )
    for s in range(SUBSTEPS):
        picks, factors, face_picks = ordered_lists[s]
        if s == 1:
            table = call(finish_body, table_shape, "finish", count=4)(summed, *edges_y, scale)
        own = call(
            lambda *refs, s=s: reply_x_body(s, *refs), shape((2 * F, 128)), "reply_x", count=5
        )(table, *asked)
        own_faces = call(own_faces_body, shape((F, 256)), "own_faces", count=2)(table, face_picks)
        own_a = interpolate(s, 0)(table, picks, factors)
        near_sent, far_sent = call(row_body, [answers] * 2, "row", count=3, after=3)(
            *answers_y, own, own_a, scale, own_faces
        )
        near = swap_near("fx", near_sent)
        far = swap_far("fx", far_sent)
        partial, message = call(
            face_near_body, [shape((F, 256)), shape((F + 8, 128))], "faces_near", count=6
        )(own_faces, near, *answers_y, face_picks, mass_faces)
        faces_in = swap_far("fx", message)
        own_b = interpolate(s, 1, after=1)(table, picks, factors, partial)
        if s == 0:
            ordered_lists.append(
                call(later_body, requests, "order", count=2, after=1)(
                    later, later_starts, partial
                )
            )
        along_x, along_y, other = call(
            face_far_body, [face] * 3, "faces_far", count=6, after=2
        )(partial, far, faces_in, far_sent, face_picks, mass_faces, own_b, ordered_lists[1][2])
        edges_x = (other, swap_near("fx", along_x))
        place = call(
            lambda *refs, s=s: place_body(s, *refs),
            shape((F, POINTS)),
            "place",
            count=9,
            after=1,
        )
        moved = (own_a, own_b, far, near, *answers_y, picks, factors, node_mass)
        if s == 0:
            weighted = place(*moved, other)
            rims_far, rims_near, rims_kept = call(rim_body, [face] * 3, "rim", count=3, after=1)(
                along_y, *edges_x, weighted
            )
        else:
            rims_far, rims_near = call(rim_body, [face] * 2, "rim", count=3)(along_y, *edges_x)
            weighted = place(*moved, rims_near)
        edges_y = swap("fy", rims_far, rims_near)
        if s == 0:
            summed, *early = call(
                between_body,
                [
                    shape((F, POINTS)),
                    shape((6, F, 128)),
                    shape((8, 128), jnp.int32),
                    shape((4, 8, 128)),
                ],
                "between",
                count=6,
                scratch=[pltpu.VMEM((NODES * F, 2 * E), BF16)],
            )(weighted, *edges_x, inverse, asked[2], asked[3])
            far = call(late_far_body, answers, "late_far", count=5)(*early, edges_y[1], scale)
            far = swap_far("fy", far)
            near = call(late_near_body, answers, "late_near", count=6)(*early, *edges_y, scale)
            near = swap_near("fy", near)
            far = call(fix_body, answers, "fix", count=4)(far, column_kept, rims_kept, scale)
            answers_y = (far, near)
        else:
            scratch = [pltpu.VMEM((8, F, E), F32), pltpu.SemaphoreType.DMA((8,))]
            vmem = pl.BlockSpec(memory_space=pltpu.VMEM)
            hbm = pl.BlockSpec(memory_space=pltpu.HBM)
            params = pltpu.CompilerParams(vmem_limit_bytes=VMEM_LIMIT)
            part, begun = pl.pallas_call(
                inner_body,
                out_shape=[shape((F, 8 * E)), shape((F, NODES, E))],
                in_specs=[vmem] * 4,
                out_specs=[vmem, hbm],
                scratch_shapes=scratch,
                name="inner",
                compiler_params=params,
            )(weighted, *edges_x, inverse)
            result = pl.pallas_call(
                last_body,
                out_shape=shape((F, NODES, E)),
                in_specs=[vmem] * 4 + [hbm],
                out_specs=hbm,
                scratch_shapes=scratch,
                input_output_aliases={4: 0},
                name="last",
                compiler_params=params,
            )(part, *edges_y, scale, begun)
    return result


def solution(mesh):
    return jax.shard_map(
        per_device,
        mesh=mesh,
        in_specs=(
            P(None, None, ("fx", "fy")),
            P(None, ("fx", "fy")),
            P(None, ("fx", "fy"), None),
            P(None, ("fx", "fy"), None),
            P(None, ("fx", "fy")),
            P(None, None, ("fx", "fy")),
        ),
        out_specs=P(None, None, ("fx", "fy")),
        check_vma=False,
    )
```

```python
import jax
import jax.numpy as jnp
from jax import lax
from jax.experimental import pallas as pl
from jax.experimental.pallas import tpu as pltpu
from jax.sharding import PartitionSpec as P

TX = 16
CAP = 128
QGRID = 1024
SUBSTEPS = 2
F = 64
E = 256
NODES = 16
POINTS = 4096
TILES = POINTS // 128
PIECES = (((0, 10), (10, 16)), ((0, 9), (9, 16)))
GLL_NODES = (-1.0, -0.4472135954999579, 0.4472135954999579, 1.0)
REMOTE = (0, 1, 2, 3, 5, 6, 7, 8)
BF16 = jnp.bfloat16
F32 = jnp.float32
VMEM_LIMIT = 40 * 2**20


def call(body, out_shape, name, hbm=(), count=0, after=0, scratch=()):
    specs = [
        pl.BlockSpec(memory_space=pltpu.HBM if i in hbm else pltpu.VMEM) for i in range(count)
    ] + [pl.BlockSpec(memory_space=pl.ANY)] * after

    def kernel(*refs):
        body(*refs[:count], *refs[count + after :])

    return pl.pallas_call(
        kernel,
        out_shape=out_shape,
        in_specs=specs,
        scratch_shapes=scratch,
        name=name,
        compiler_params=pltpu.CompilerParams(vmem_limit_bytes=VMEM_LIMIT),
    )


def in_hbm(array):
    return pltpu.with_memory_space_constraint(array, pltpu.HBM)


def shape(dims, dtype=F32):
    return jax.ShapeDtypeStruct(dims, dtype)


def swap_far(axis, block):
    size = lax.axis_size(axis)
    pairs = [(i, (((i + size - 1) % size ^ 1) + 1) % size) for i in range(size)]
    return lax.ppermute(block, axis, pairs)


def swap_near(axis, block):
    return lax.ppermute(block, axis, [(i, i ^ 1) for i in range(lax.axis_size(axis))])


def swap(axis, far, near):
    return swap_far(axis, far), swap_near(axis, near)


def to_swaps(axis, low, high):
    even = lax.axis_index(axis) % 2 == 0
    return jnp.where(even, low, high), jnp.where(even, high, low)


def from_swaps(axis, first, second):
    even = lax.axis_index(axis) % 2 == 0
    return jnp.where(even, first, second), jnp.where(even, second, first)


def lagrange(step):
    x = step * (2.0 / QGRID) - 1.0
    rows = []
    for a in range(4):
        factor = None
        for b in range(4):
            if b != a:
                term = (x - GLL_NODES[b]) * (1.0 / (GLL_NODES[a] - GLL_NODES[b]))
                factor = term if factor is None else factor * term
        rows.append(factor)
    return rows


def halves(block):
    high = block.astype(BF16)
    return high, (block - high.astype(F32)).astype(BF16)


def one_hot(index_rows, depth):
    rows = lax.broadcasted_iota(jnp.int32, (depth, 128), 0).astype(F32).astype(BF16)
    parts = [jnp.where(rows == r.astype(BF16), BF16(1), BF16(0)) for r in index_rows]
    return jnp.concatenate(parts, axis=1)


def lane_index(rows):
    return lax.broadcasted_iota(jnp.int32, (rows, 128), 1)


def eight(row):
    return jnp.broadcast_to(row, (8, row.shape[1]))


def pick_lanes(block, index):
    return jnp.take_along_axis(block, index, axis=1, mode="promise_in_bounds")


def faces(tile):
    rows = tile(0, 0).shape[0]
    lane = lane_index(rows)
    along_x = jnp.zeros((rows, 128), F32)
    for b in range(4):
        along_x = jnp.where(lane // 16 == b, pltpu.roll(tile(b, 0), b * 16, 1), along_x)
        shifted = pltpu.roll(tile(12 + b, 1), (b * 16 + 80) % 128, 1)
        along_x = jnp.where(lane // 16 == b + 4, shifted, along_x)
    along_y = jnp.zeros((rows, 128), F32)
    index = (lane % 8) * 16
    for a in range(4):
        for t in range(2):
            here = ((lane % 64) // 16 == a) & ((lane % 16) // 8 == t)
            first = pick_lanes(tile(4 * a, t), index)
            last = pick_lanes(tile(4 * a + 3, t), index + 15)
            along_y = jnp.where(here, jnp.where(lane < 64, first, last), along_y)
    return along_x, along_y


def summed_faces(own, low, high):
    lane = lane_index(own.shape[0])
    place = lane % 64
    behind = pltpu.roll(own, 128 - 48 + 1, 1)
    ahead = pltpu.roll(own, 48 - 1, 1)
    behind = jnp.where(lane == 0, low[:, 64:65], jnp.where(lane == 64, low[:, 127:128], behind))
    ahead = jnp.where(lane == 63, high[:, 0:1], jnp.where(lane == 127, high[:, 63:64], ahead))
    return own + jnp.where(place < 16, behind, jnp.where(place >= 48, ahead, 0.0))


def summed_nodes(nodes, low, high):
    rows = nodes[0].shape[0]
    lane = lane_index(rows)
    wide = lax.broadcasted_iota(jnp.int32, (rows, E), 1)
    nodes = list(nodes)
    for b in range(4):
        first, last = nodes[b], nodes[12 + b]
        behind = pltpu.roll(last, 16, 1)
        ahead = pltpu.roll(first, E - 16, 1)
        from_low = pltpu.roll(low, (128 - 64 - 16 * b) % 128, 1)
        from_high = pltpu.roll(high, 112 - 16 * b, 1)
        behind = jnp.concatenate(
            [jnp.where(lane < 16, from_low, behind[:, :128]), behind[:, 128:]], axis=1
        )
        ahead = jnp.concatenate(
            [ahead[:, :128], jnp.where(lane >= 112, from_high, ahead[:, 128:])], axis=1
        )
        nodes[b] = first + behind
        nodes[12 + b] = last + ahead
    for a in range(4):
        first, last = nodes[4 * a], nodes[4 * a + 3]
        behind = jnp.where(wide % 16 == 0, 0.0, pltpu.roll(last, 1, 1))
        ahead = jnp.where(wide % 16 == 15, 0.0, pltpu.roll(first, E - 1, 1))
        nodes[4 * a] = first + behind
        nodes[4 * a + 3] = last + ahead
    return nodes


def halo_of(low, high):
    lane = lane_index(low.shape[0])
    return pltpu.roll(jnp.where(lane >= 64, low, high), 64, 1)


def with_halo(n, node, halo):
    if n % 4 not in (0, 3):
        return node
    rows = node.shape[0]
    lane = lane_index(rows)
    wide = lax.broadcasted_iota(jnp.int32, (rows, E), 1)
    start = 16 * (n // 4) + (64 if n % 4 == 3 else 0)
    spread = [pick_lanes(halo, start + 8 * t + lane // 16) for t in range(2)]
    at = 15 if n % 4 == 3 else 0
    return node + jnp.where(wide % 16 == at, jnp.concatenate(spread, axis=1), 0.0)


def fetch(pairs, sems):
    copies = [pltpu.make_async_copy(*pair, sems.at[i]) for i, pair in enumerate(pairs)]
    for copy in copies:
        copy.start()
    for copy in copies:
        copy.wait()


def asks_body(
    offsets_in, source_in, coords_in, mass_in, first, second, mid, mass_faces,
    offsets, source, coords, mass, rows, message, sems,
):
    fetch(
        [(offsets_in, offsets), (source_in, source), (coords_in, coords), (mass_in, mass)], sems
    )
    for s in range(SUBSTEPS):
        rows[3 * s : 3 * s + 1, :] = source[s : s + 1, :].astype(F32)
        rows[3 * s + 1 : 3 * s + 3, :] = coords[s].astype(F32)
    rows[6:8, :] = jnp.zeros((2, POINTS), F32)
    early = lax.broadcasted_iota(jnp.int32, (8, 128), 0) < 3
    for k in REMOTE:
        parts = []
        for s in range(SUBSTEPS):
            start = offsets[s, 0, k]
            tile = jnp.minimum(start // 128, TILES - 1)
            after = jnp.minimum(tile + 1, TILES - 1)
            wide = jnp.concatenate(
                [rows[:, pl.ds(pl.multiple_of(t * 128, 128), 128)] for t in (tile, after)], axis=1
            )
            parts.append(pltpu.roll(wide, 256 - (start - tile * 128), 1)[:, 0:128])
        message[k * 8 : (k + 1) * 8, :] = jnp.where(early, parts[0], parts[1])
    along_x, along_y = faces(lambda n, t: eight(mass[n : n + 1, t * 128 : (t + 1) * 128]))
    for k in (1, 7):
        message[k * 8 + 6 : k * 8 + 7, :] = along_x[0:1]
    mass_faces[:, 0:128] = along_x
    mass_faces[:, 128:256] = along_y
    message[32:40, :] = jnp.zeros((8, 128), F32)
    first[...], second[...] = to_swaps("fx", message[0:24, :], message[48:72, :])
    mid[...] = message[24:48, :]


def order_body(
    offsets_in, order_in, source_in, coords_in, picks, factors, face_picks, later, later_starts,
    offsets, order, source, coords, sems,
):
    fetch(
        [(offsets_in, offsets), (order_in, order), (source_in, source), (coords_in, coords)], sems
    )
    ordered(
        order[0], source[0:1], coords[0, 0:1], coords[0, 1:2], offsets[0], picks, factors, face_picks
    )
    later[0:1, :] = order[1]
    later[1:2, :] = source[1:2, :]
    later[2:4, :] = coords[1]
    later_starts[0:1, 0:10] = offsets[1]


def later_body(lists, starts, picks, factors, face_picks):
    ordered(
        lists[0:1], lists[1:2], lists[2:3], lists[3:4], starts[0:1], picks, factors, face_picks
    )


def ordered(nodes, sources, xs, ys, starts, picks, factors, face_picks):
    chunk = 1024
    total = None
    for c in range(POINTS // chunk):
        lanes = slice(c * chunk, (c + 1) * chunk)
        node = nodes[:, lanes]
        tile_of = (node // 128).astype(F32).astype(BF16)
        lane_of = (node % 128).astype(F32).astype(BF16)
        position = lax.broadcasted_iota(jnp.int32, (1, chunk), 1) + c * chunk
        run = jnp.zeros((1, chunk), jnp.int32)
        begin = jnp.broadcast_to(starts[:, 0:1], (1, chunk))
        for k in range(1, 9):
            start = jnp.broadcast_to(starts[:, k : k + 1], (1, chunk))
            passed = position >= start
            run = run + passed.astype(jnp.int32)
            begin = jnp.where(passed, start, begin)
        own = run == 4
        kind = jnp.where(own, 8, jnp.where(run > 4, run - 1, run))
        pick = jnp.where(own, sources[:, lanes], position - begin)
        cx = xs[:, lanes]
        cy = ys[:, lanes]
        values = [pick, cx // 8, cx % 8, cy // 8, cy % 8, kind]
        tiles = lax.broadcasted_iota(jnp.int32, (TILES, chunk), 0).astype(F32).astype(BF16)
        here = tiles == tile_of
        left = jnp.concatenate(
            [jnp.where(here, v.astype(F32).astype(BF16), BF16(0)) for v in values], axis=0
        )
        spots = lax.broadcasted_iota(jnp.int32, (128, chunk), 0).astype(F32).astype(BF16)
        right = jnp.where(spots == lane_of, BF16(1), BF16(0))
        part = lax.dot_general(left, right, (((1,), (1,)), ((), ())), preferred_element_type=F32)
        total = part if total is None else total + part
    pick, xh, xl, yh, yl, kind = [total[q * TILES : (q + 1) * TILES] for q in range(6)]
    own = kind > 7.5
    picks[0] = jnp.where(own, pick, -1.0)
    picks[1] = jnp.where(own, -1.0, pick)
    mask = jnp.where(own, 1.0, 0.0)
    along_x = [row * mask for row in lagrange(xh * 8.0 + xl)]
    along_y = lagrange(yh * 8.0 + yl)
    for n in range(NODES):
        factors[n] = along_x[n // 4] * along_y[n % 4]
    for d in range(8):
        factors[NODES + d] = jnp.where(jnp.abs(kind - d) < 0.5, 1.0, 0.0)
    for q, rows in enumerate((picks[1], kind, picks[0], xh * 8.0 + xl, yh * 8.0 + yl)):
        along = faces(lambda n, t: eight(rows[2 * n + t : 2 * n + t + 1]))
        face_picks[q : q + 1, :] = jnp.concatenate(along, axis=1)[0:1]


def table_body(tracers_in, table, tracers, sems):
    fetch([(tracers_in, tracers)], sems)
    for q in range(0, F, 16):
        block = jnp.swapaxes(tracers[q : q + 16], 0, 1)
        for n in range(NODES):
            high, low = halves(block[n])
            table[n * F + q : n * F + q + 16, 0:E] = high
            table[n * F + q : n * F + q + 16, E : 2 * E] = low


def column_body(x_first, x_second, mid, mass_faces, first, second, kept):
    low, high = from_swaps("fx", x_first[...], x_second[...])
    masses = summed_faces(mass_faces[:, 128:256], low[8:16], high[8:16])[6:7]
    rows = lax.broadcasted_iota(jnp.int32, (8, 128), 0)
    columns = []
    for k in (0, 2):
        block = slice(k * 8, (k + 1) * 8)
        center = jnp.where(rows == 6, masses, mid[block, :])
        columns.append(jnp.concatenate([high[block], center, low[block]], axis=0))
    first[...], second[...] = to_swaps("fy", *columns)
    kept[...] = first[...]


def row_body(y_first, y_second, own, near, far):
    low, high = from_swaps("fy", y_first[...], y_second[...])
    mine = own[...]
    ahead = jnp.concatenate([low[0:F], mine[0:F], high[0:F]], axis=0)
    behind = jnp.concatenate([low[2 * F :], mine[F:], high[2 * F :]], axis=0)
    far[...], near[...] = to_swaps("fx", behind, ahead)


def combine(products, weights):
    total = None
    for n, weight in enumerate(weights):
        term = products[n * F : (n + 1) * F] * weight
        total = term if total is None else total + term
    return total


def asked_blocks(x_first, x_second, y_first, y_second):
    x_low, x_high = from_swaps("fx", x_first[...], x_second[...])
    y_low, y_high = from_swaps("fy", y_first[...], y_second[...])
    by_direction = {(1, 0): x_low[8:16], (-1, 0): x_high[8:16]}
    for k in range(3):
        by_direction[(k - 1, 1)] = y_low[k * 8 : (k + 1) * 8]
        by_direction[(k - 1, -1)] = y_high[k * 8 : (k + 1) * 8]
    return [by_direction[(k // 3 - 1, k % 3 - 1)] for k in REMOTE]


def asked_rows(s, asked):
    return [
        jnp.concatenate([r[s * 3 + q : s * 3 + q + 1, :] for r in asked], axis=0) for q in range(3)
    ]


def weights_of(cx, cy):
    along_x = lagrange(cx)
    along_y = lagrange(cy)
    return [along_x[n // 4] * along_y[n % 4] for n in range(NODES)]


def answer(table, pick, weights, directions):
    values = {}
    for both in directions:
        hot = one_hot([pick[d : d + 1] for d in both], E)
        products = jnp.dot(
            table[...], jnp.concatenate([hot, hot], axis=0), preferred_element_type=F32
        )
        for h, d in enumerate(both):
            lanes = slice(h * 128, (h + 1) * 128)
            values[d] = combine(products[:, lanes], [w[d : d + 1] for w in weights])
    return values


BEHIND = (2, 4, 7)
AHEAD = (0, 3, 5)
SIDES = (1, 6)


def partner_rows(s, asked):
    return [
        jnp.concatenate([asked[k * 8 + 3 * s + q : k * 8 + 3 * s + q + 1, :] for k in range(3)], axis=0)
        for q in range(3)
    ]


def partners_rows(s, far, near):
    pairs = zip(partner_rows(s, far), partner_rows(s, near))
    return [jnp.concatenate(pair, axis=0) for pair in pairs]


def reply_y_body(table, asked_far, asked_near, far, near):
    pick, cx, cy = partners_rows(0, asked_far, asked_near)
    values = answer(table, pick, weights_of(cx, cy), ((0, 1), (2, 3), (4, 5)))
    for k in range(3):
        far[k * F : (k + 1) * F, :] = values[k]
        near[k * F : (k + 1) * F, :] = values[3 + k]


def reply_x_body(s, table, x_first, x_second, y_first, y_second, own):
    pick, cx, cy = asked_rows(s, asked_blocks(x_first, x_second, y_first, y_second))
    values = answer(table, pick, weights_of(cx, cy), (SIDES,))
    for k, d in enumerate(SIDES):
        own[k * F : (k + 1) * F, :] = values[d]


def between_body(
    weighted, x_first, x_second, inverse, asked_far, asked_near, summed, values, lanes, shares, table
):
    sum_body(weighted, x_first, x_second, inverse, summed, table)
    pick, cx, cy = partners_rows(1, asked_far, asked_near)
    weights = weights_of(cx, cy)
    for d, value in answer(table, pick, weights, ((0, 1), (2, 3), (4, 5))).items():
        values[d] = value
    element = pick.astype(jnp.int32)
    lanes[0:6, :] = element // 16 + jnp.where(element % 16 == 15, 64, 0)
    for a in range(4):
        share = jnp.where(element % 16 == 15, weights[4 * a + 3], 0.0)
        shares[a, 0:6, :] = jnp.where(element % 16 == 0, weights[4 * a], share)


def shared(values, lanes, shares, halo, start, message):
    for k in range(3):
        d = start + k
        index = jnp.broadcast_to(lanes[d : d + 1, :], (F, 128))
        value = values[d]
        for a in range(4):
            value = value + pick_lanes(halo, index + 16 * a) * shares[a, d : d + 1, :]
        message[k * F : (k + 1) * F, :] = value


def late_far_body(values, lanes, shares, near, scale, message):
    even = lax.axis_index("fy") % 2 == 0
    block = pltpu.roll(near[...], 64, 1) * scale[0:1, :]
    lane = lane_index(F)
    halo = jnp.where(jnp.where(even, lane - 64, 63 - lane) >= 0, block, 0.0)
    shared(values, lanes, shares, halo, 0, message)


def late_near_body(values, lanes, shares, far, near, scale, message):
    halo = halo_of(*from_swaps("fy", far[...], near[...])) * scale[0:1, :]
    shared(values, lanes, shares, halo, 3, message)


def fix_body(far, asked, rims, scale, result):
    even = lax.axis_index("fy") % 2 == 0
    pick, cx, cy = partner_rows(1, asked)
    weights = weights_of(cx, cy)
    element = pick.astype(jnp.int32)
    on_face = element % 16 == jnp.where(even, 15, 0)
    lanes = element // 16 + jnp.where(even, 0, 64)
    own = rims[...] * scale[0:1, :]
    for k in range(3):
        index = jnp.broadcast_to(lanes[k : k + 1], (F, 128))
        value = far[k * F : (k + 1) * F, :]
        for a in range(4):
            weight = jnp.where(even, weights[4 * a + 3], weights[4 * a])
            weight = jnp.where(on_face, weight, 0.0)
            value = value + pick_lanes(own, index + 16 * a) * weight[k : k + 1]
        result[k * F : (k + 1) * F, :] = value


def own_body(begin, table, picks, factors, result):
    def block(i, carry):
        at = 2 * (begin + i)
        hot = one_hot([picks[0, pl.ds(at + h, 1), :] for h in range(2)], E)
        products = jnp.dot(
            table[...], jnp.concatenate([hot, hot], axis=0), preferred_element_type=F32
        )
        weights = [
            jnp.concatenate([factors[n, pl.ds(at + h, 1), :] for h in range(2)], axis=1)
            for n in range(NODES)
        ]
        result[:, pl.ds(pl.multiple_of(i * E, E), E)] = combine(products, weights)
        return carry

    count = result.shape[1] // E
    lax.fori_loop(0, count, block, 0, unroll=5 if count == 10 else 3 if count in (6, 9) else count)


def stacked(blocks):
    return jnp.concatenate([jnp.concatenate(halves(block), axis=1) for block in blocks], axis=0)


def three(ref):
    return [ref[k * F : (k + 1) * F, :] for k in range(3)]


def middles(y_first, y_second):
    return list(from_swaps("fy", y_first[F : 2 * F, :], y_second[F : 2 * F, :]))


def arrived(x_first, x_second, y_first, y_second):
    even = lax.axis_index("fx") % 2 == 0
    pairs = list(zip(three(x_first), three(x_second)))
    low = [jnp.where(even, far, near) for far, near in pairs]
    high = [jnp.where(even, near, far) for far, near in pairs]
    return stacked(low + middles(y_first, y_second) + high)


def placed(answers, slots, masks):
    hot = one_hot(slots, CAP)
    products = jnp.dot(answers, jnp.concatenate([hot, hot], axis=0), preferred_element_type=F32)
    return combine(products, masks)


def masks_of(kind, bases):
    return [jnp.where(jnp.abs(kind - base) < 0.5, 1.0, 0.0) for base in bases]


def kinds(even, near):
    start = jnp.where(even == near, 5.0, 0.0)
    return [start + k for k in range(3)]


def face_slots(face_picks):
    return [face_picks[0:1, h * 128 : (h + 1) * 128] for h in range(2)]


def own_faces_body(table, face_picks, result):
    hot = one_hot([face_picks[2:3, h * 128 : (h + 1) * 128] for h in range(2)], E)
    products = jnp.dot(table[...], jnp.concatenate([hot, hot], axis=0), preferred_element_type=F32)
    result[...] = combine(products, weights_of(face_picks[3:4, :], face_picks[4:5, :]))


def face_near_body(
    own, near, y_first, y_second, face_picks, mass_faces, partial, message
):
    even = lax.axis_index("fx") % 2 == 0
    masks = masks_of(face_picks[1:2, :], kinds(even, True) + [3.0, 4.0])
    answers = stacked(three(near) + middles(y_first, y_second))
    moved = own[...] + placed(answers, face_slots(face_picks), masks)
    moved = moved * mass_faces[0:1, :]
    partial[...] = moved
    message[0:F, :] = moved[:, 0:128]
    message[F : F + 8, :] = face_picks[:, 0:128]
    message[F + 2 : F + 3, :] = mass_faces[0:1, 0:128]


def face_far_body(partial, far, faces_in, sent, face_picks, mass_faces, along_x, along_y, other):
    even = lax.axis_index("fx") % 2 == 0
    masks = masks_of(face_picks[1:2, :], kinds(even, False))
    moved = placed(stacked(three(far)), face_slots(face_picks), masks) * mass_faces[0:1, :]
    result = partial[...] + moved
    along_x[...] = result[:, 0:128]
    along_y[...] = result[:, 128:256]
    slot, kind, weight = [faces_in[F + q : F + q + 1, :] for q in range(3)]
    moved = placed(stacked(three(sent)), [slot], masks_of(kind, kinds(even, True)))
    other[...] = faces_in[0:F, :] + moved * weight


def place_body(
    s, own_a, own_b, x_first, x_second, y_first, y_second, picks, factors, mass, result
):
    answers = arrived(x_first, x_second, y_first, y_second)
    for n in range(NODES):
        tiles = [slice(2 * n + h, 2 * n + h + 1) for h in range(2)]
        masks = [
            jnp.concatenate([factors[NODES + d, t, :] for t in tiles], axis=1) for d in range(8)
        ]
        moved = placed(answers, [picks[1, t, :] for t in tiles], masks)
        for ref, (begin, end) in zip((own_a, own_b), PIECES[s]):
            if begin <= n < end:
                own = ref[:, (n - begin) * E : (n - begin + 1) * E]
        result[:, n * E : (n + 1) * E] = (own + moved) * mass[n : n + 1, :]


def rim_body(along_y, x_first, x_second, *results):
    low, high = from_swaps("fx", x_first[...], x_second[...])
    result = summed_faces(along_y[...], low, high)
    for ref in results:
        ref[...] = result


def scale_body(mass, x_first, x_second, y_first, y_second, inverse, on_faces):
    x_low, x_high = from_swaps("fx", x_first[8:16, :], x_second[8:16, :])
    y_low, y_high = from_swaps("fy", y_first[8:16, :], y_second[8:16, :])
    low, high, halo = [
        eight(row[6:7]) for row in (x_low, x_high, halo_of(y_low, y_high))
    ]
    nodes = [eight(mass[n : n + 1, :]) for n in range(NODES)]
    nodes = summed_nodes(nodes, low, high)
    nodes = [1.0 / with_halo(n, node, halo) for n, node in enumerate(nodes)]
    for n in range(NODES):
        inverse[n : n + 1, :] = nodes[n][0:1]
    on_faces[...] = faces(lambda n, t: nodes[n][:, t * 128 : (t + 1) * 128])[1]


def sum_body(weighted, x_first, x_second, inverse, result, table=None):
    low, high = from_swaps("fx", x_first[...], x_second[...])
    nodes = summed_nodes([weighted[:, n * E : (n + 1) * E] for n in range(NODES)], low, high)
    for n in range(NODES):
        node = nodes[n] * inverse[n : n + 1, :]
        result[:, n * E : (n + 1) * E] = node
        if table is not None:
            high_part, low_part = halves(node)
            table[n * F : (n + 1) * F, 0:E] = high_part
            table[n * F : (n + 1) * F, E : 2 * E] = low_part


def finish_body(summed, y_first, y_second, scale, table):
    halo = halo_of(*from_swaps("fy", y_first[...], y_second[...])) * scale[0:1, :]
    for n in range(NODES):
        node = with_halo(n, summed[:, n * E : (n + 1) * E], halo)
        high, low = halves(node)
        table[n * F : (n + 1) * F, 0:E] = high
        table[n * F : (n + 1) * F, E : 2 * E] = low


FACE_NODES = tuple(n for n in range(NODES) if n % 4 in (0, 3))
INNER_NODES = tuple(n for n in range(NODES) if n % 4 in (1, 2))


def inner_body(weighted, x_first, x_second, inverse, part, result, block, sems):
    low, high = from_swaps("fx", x_first[...], x_second[...])
    nodes = summed_nodes([weighted[:, n * E : (n + 1) * E] for n in range(NODES)], low, high)
    copies = []
    for i, n in enumerate(INNER_NODES):
        block[i] = nodes[n] * inverse[n : n + 1, :]
        copy = pltpu.make_async_copy(block.at[i], result.at[:, n, :], sems.at[i])
        copy.start()
        copies.append(copy)
    for i, n in enumerate(FACE_NODES):
        part[:, i * E : (i + 1) * E] = nodes[n] * inverse[n : n + 1, :]
    for copy in copies:
        copy.wait()


def last_body(part, y_first, y_second, scale, begun, result, block, sems):
    halo = halo_of(*from_swaps("fy", y_first[...], y_second[...])) * scale[0:1, :]
    copies = []
    for i, n in enumerate(FACE_NODES):
        block[i] = with_halo(n, part[:, i * E : (i + 1) * E], halo)
        copy = pltpu.make_async_copy(block.at[i], result.at[:, n, :], sems.at[i])
        copy.start()
        copies.append(copy)
    for copy in copies:
        copy.wait()


def per_device(tracers, node_mass, point_order, offsets, source, coords):
    ask = shape((24, 128))
    answers = shape((3 * F, 128))
    face = shape((F, 128))
    table_shape = shape((NODES * F, 2 * E), BF16)
    lists = [
        pltpu.SMEM(offsets.shape, jnp.int32),
        pltpu.VMEM(source.shape, jnp.int32),
        pltpu.VMEM(coords.shape, jnp.int32),
    ]
    first, second, mid, mass_faces = call(
        asks_body,
        [ask, ask, ask, shape((8, 256))],
        "asks",
        hbm=(0, 1, 2, 3),
        count=4,
        scratch=lists
        + [
            pltpu.VMEM(node_mass.shape, F32),
            pltpu.VMEM((8, POINTS), F32),
            pltpu.VMEM((72, 128), F32),
            pltpu.SemaphoreType.DMA((4,)),
        ],
    )(*[in_hbm(a) for a in (offsets, source, coords, node_mass)])
    asked = swap("fx", first, second)
    requests = [shape((2, TILES, 128)), shape((NODES + 8, TILES, 128)), shape((8, 256))]
    *now, later, later_starts = call(
        order_body,
        requests + [shape((8, POINTS), jnp.int32), shape((8, 128), jnp.int32)],
        "order",
        hbm=(0, 1, 2, 3),
        count=4,
        scratch=[pltpu.VMEM(a.shape, jnp.int32) for a in (offsets, point_order, source, coords)]
        + [pltpu.SemaphoreType.DMA((4,))],
    )(*[in_hbm(a) for a in (offsets, point_order, source, coords)])
    ordered_lists = [now]

    def interpolate(s, piece, after=0):
        begin, end = PIECES[s][piece]
        return call(
            lambda *refs: own_body(begin, *refs),
            shape((F, (end - begin) * E)),
            "own",
            count=3,
            after=after,
        )

    column_far, column_near, column_kept = call(column_body, [ask] * 3, "column", count=4)(
        *asked, mid, mass_faces
    )
    asked += swap("fy", column_far, column_near)
    table = call(
        table_body,
        table_shape,
        "table",
        hbm=(0,),
        count=1,
        scratch=[pltpu.VMEM(tracers.shape, F32), pltpu.SemaphoreType.DMA((1,))],
    )(in_hbm(tracers))
    far, near = call(reply_y_body, [answers] * 2, "reply_y", count=3, after=1)(
        table, asked[2], asked[3], now[2]
    )
    answers_y = swap("fy", far, near)
    inverse, scale = call(scale_body, [shape((NODES, E)), shape((8, 128))], "scale", count=5)(
        node_mass, *asked
    )
    for s in range(SUBSTEPS):
        picks, factors, face_picks = ordered_lists[s]
        if s == 1:
            table = call(finish_body, table_shape, "finish", count=4)(summed, *edges_y, scale)
        own = call(
            lambda *refs, s=s: reply_x_body(s, *refs), shape((2 * F, 128)), "reply_x", count=5
        )(table, *asked)
        own_faces = call(own_faces_body, shape((F, 256)), "own_faces", count=2)(table, face_picks)
        own_a = interpolate(s, 0)(table, picks, factors)
        near_sent, far_sent = call(row_body, [answers] * 2, "row", count=3, after=3)(
            *answers_y, own, own_a, scale, own_faces
        )
        near = swap_near("fx", near_sent)
        far = swap_far("fx", far_sent)
        partial, message = call(
            face_near_body, [shape((F, 256)), shape((F + 8, 128))], "faces_near", count=6
        )(own_faces, near, *answers_y, face_picks, mass_faces)
        faces_in = swap_far("fx", message)
        own_b = interpolate(s, 1, after=1)(table, picks, factors, partial)
        if s == 0:
            ordered_lists.append(
                call(later_body, requests, "order", count=2, after=1)(
                    later, later_starts, partial
                )
            )
        along_x, along_y, other = call(
            face_far_body, [face] * 3, "faces_far", count=6, after=2
        )(partial, far, faces_in, far_sent, face_picks, mass_faces, own_b, ordered_lists[1][2])
        edges_x = (other, swap_near("fx", along_x))
        place = call(
            lambda *refs, s=s: place_body(s, *refs),
            shape((F, POINTS)),
            "place",
            count=9,
            after=1,
        )
        moved = (own_a, own_b, far, near, *answers_y, picks, factors, node_mass)
        if s == 0:
            weighted = place(*moved, other)
            rims_far, rims_near, rims_kept = call(rim_body, [face] * 3, "rim", count=3, after=1)(
                along_y, *edges_x, weighted
            )
        else:
            rims_far, rims_near = call(rim_body, [face] * 2, "rim", count=3)(along_y, *edges_x)
            weighted = place(*moved, rims_near)
        edges_y = swap("fy", rims_far, rims_near)
        if s == 0:
            summed, *early = call(
                between_body,
                [
                    shape((F, POINTS)),
                    shape((6, F, 128)),
                    shape((8, 128), jnp.int32),
                    shape((4, 8, 128)),
                ],
                "between",
                count=6,
                scratch=[pltpu.VMEM((NODES * F, 2 * E), BF16)],
            )(weighted, *edges_x, inverse, asked[2], asked[3])
            far = call(late_far_body, answers, "late_far", count=5)(*early, edges_y[1], scale)
            far = swap_far("fy", far)
            near = call(late_near_body, answers, "late_near", count=6)(*early, *edges_y, scale)
            near = swap_near("fy", near)
            far = call(fix_body, answers, "fix", count=4)(far, column_kept, rims_kept, scale)
            answers_y = (far, near)
        else:
            scratch = [pltpu.VMEM((8, F, E), F32), pltpu.SemaphoreType.DMA((8,))]
            vmem = pl.BlockSpec(memory_space=pltpu.VMEM)
            hbm = pl.BlockSpec(memory_space=pltpu.HBM)
            params = pltpu.CompilerParams(vmem_limit_bytes=VMEM_LIMIT)
            part, begun = pl.pallas_call(
                inner_body,
                out_shape=[shape((F, 8 * E)), shape((F, NODES, E))],
                in_specs=[vmem] * 4,
                out_specs=[vmem, hbm],
                scratch_shapes=scratch,
                name="inner",
                compiler_params=params,
            )(weighted, *edges_x, inverse)
            result = pl.pallas_call(
                last_body,
                out_shape=shape((F, NODES, E)),
                in_specs=[vmem] * 4 + [hbm],
                out_specs=hbm,
                scratch_shapes=scratch,
                input_output_aliases={4: 0},
                name="last",
                compiler_params=params,
            )(part, *edges_y, scale, begun)
    return result


def solution(mesh):
    return jax.shard_map(
        per_device,
        mesh=mesh,
        in_specs=(
            P(None, None, ("fx", "fy")),
            P(None, ("fx", "fy")),
            P(None, ("fx", "fy"), None),
            P(None, ("fx", "fy"), None),
            P(None, ("fx", "fy")),
            P(None, None, ("fx", "fy")),
        ),
        out_specs=P(None, None, ("fx", "fy")),
        check_vma=False,
    )
```
